32 devices in a mesh: groups: 2 (over y), seq: 4 (over z), segment: 2 (over x), owner: 2 (over core).
Axes of the slice: x: 2, y: 2, z: 4, core: 2. Of those that a mesh axis runs over, the one named last changes fastest.
Arguments:
- layer_input_rows: bfloat16 [2, 512, 5376], P('segment', ('groups', 'seq')), parts along dimension 1, may hold values from -40 to 40
- encoded_query_rows: bfloat16 [2, 512, 2048], P('segment', ('groups', 'seq'), 'owner'), parts along dimension 1, may hold values from -213 to 213
- encoded_key_rows: bfloat16 [2, 512, 1024], P('segment', ('groups', 'seq'), 'owner'), parts along dimension 1, may hold values from -6 to 6
- layer_norm_gain: float32 [2, 5376], P('segment'), may hold values from 0.25 to 1.75
- base_value_matrix: bfloat16 [2, 5376, 1024], P('segment', ('seq', 'owner')), may hold values from -0.078125 to 0.078125
- adapter_down_panels: bfloat16 [2, 8, 5376, 64], P('segment', 'seq', 'owner'), may hold values from -0.078125 to 0.078125
- adapter_up_panels: bfloat16 [2, 8, 64, 1024], P('segment', 'seq', None, 'owner'), may hold values from -0.75 to 0.75
- request_token_lengths: int32 [8], P('groups'), parts along dimension 0, may hold values from 1 to 128, 256 in all
- adapter_per_request: int32 [8], P('groups'), parts along dimension 0, may hold values from 0 to 7
- rank_per_adapter: int32 [8], replicated, may hold values from 16 to 64
- slot_per_adapter: int32 [8], replicated, may hold values from 0 to 7, each once
Outputs:
- layer_output: bfloat16 [2, 512, 2048], P('segment', ('groups', 'seq'), 'owner'), parts along dimension 1
The draws below stay inside these ranges and needn't reach their ends.
There are 2 independent parts, one for each index of `groups`. The reference program is written for one: setup_inputs(seed, part) draws one part's arguments, and reference() takes and returns one part's arrays. A program takes and returns all parts, laid end to end along the dimension named above; an argument that names none is the same for every part. Nothing has to cross between parts.
All inputs are finite; a program needn't handle non-finite values.
Results may differ from the reference program's by a relative error of at most 0.0065.
Values may be sent and summed in bfloat16 or wider, within the bound.
No kernel may reach another device: no remote copies, remote signals or barrier semaphores. Data moves between devices by JAX's collectives and lax.ppermute only.
A program may use at most 128 MiB of HBM per device.

```python
import math
import jax
import jax.numpy as jnp
import numpy as np
from jax import lax

TOK_DEV = 64
MODEL_WIDTH = 5376
WINDOW = 1024
HEADS = 16
KEY_VALUE_HEADS = 8
HEAD_SIZE = 128
MAX_RANK = 64
REQUESTS = 4
LAYER_COUNT = 2
SLOT_COUNT = 8
TOKEN_COUNT = 256


def draw_layer_input_rows(key, part):
    first_key, second_key, third_key = jax.random.split(key, 3)
    column_scale = jnp.exp(jax.random.uniform(second_key, (1, 1, MODEL_WIDTH), jnp.float32, math.log(0.3), math.log(3.0)))
    row_scale = jnp.exp(jax.random.uniform(third_key, (LAYER_COUNT, TOKEN_COUNT, 1), jnp.float32, math.log(0.5), math.log(2.0)))
    drawn = jnp.clip(jax.random.normal(first_key, (LAYER_COUNT, TOKEN_COUNT, MODEL_WIDTH), jnp.float32), -6.0, 6.0)
    return (drawn * column_scale * row_scale).astype(jnp.bfloat16)


def attention_pair(key):
    folded = jax.random.fold_in(key, 11)
    draw_query, draw_keys = jax.random.split(folded, 2)
    group_size = HEADS // KEY_VALUE_HEADS
    key_draw = jnp.clip(jax.random.normal(draw_keys, (LAYER_COUNT, TOKEN_COUNT, KEY_VALUE_HEADS, HEAD_SIZE), jnp.float32), -6.0, 6.0)
    queries = jnp.clip(jax.random.normal(draw_query, (LAYER_COUNT, TOKEN_COUNT, KEY_VALUE_HEADS, group_size, HEAD_SIZE), jnp.float32), -6.0, 6.0)
    return (queries.reshape(LAYER_COUNT, TOKEN_COUNT, HEADS * HEAD_SIZE), key_draw.reshape(LAYER_COUNT, TOKEN_COUNT, KEY_VALUE_HEADS * HEAD_SIZE))


def draw_encoded_query_rows(key, part):
    return attention_pair(key)[0].astype(jnp.bfloat16)


def draw_encoded_key_rows(key, part):
    return attention_pair(key)[1].astype(jnp.bfloat16)


def set_ends(array, key, low, high):
    shape = array.shape
    spot = [jax.random.randint(jax.random.fold_in(key, axis), (), 0, shape[axis]) for axis in range(len(shape))]
    array = array.at[tuple(spot)].set(low)
    longest = shape.index(max(shape))
    spot[longest] = (spot[longest] + 1) % shape[longest]
    return array.at[tuple(spot)].set(high)


def level_of(key, dims, shards, low, high):
    factor_of = 1.0
    for axis_at, shards_of in shards:
        steps = jax.random.uniform(jax.random.fold_in(jax.random.fold_in(key, 6), axis_at), (shards_of,), jnp.float32, low / len(shards), high / len(shards))
        factor_of = factor_of * jnp.repeat(jnp.exp(steps), dims[axis_at] // shards_of).reshape((-1,) + (1,) * (len(dims) - 1 - axis_at))
    return factor_of


def length_profile(amount, total, reach, skew):
    weights = [(1 << 20) // math.isqrt(standing ** skew) + 1 for standing in range(2, amount + 1)]
    surplus, holding = total - reach - (amount - 1), [1] * (amount - 1)
    while surplus > 0:
        free = [i for i in range(amount - 1) if holding[i] < reach]
        pool, remaining = sum([weights[i] for i in free]), surplus
        for i in free:
            addition = min(reach - holding[i], max(1, remaining * weights[i] // pool), surplus)
            holding[i] = holding[i] + addition
            surplus = surplus - addition
    return np.array([reach] + holding)


def uneven_parts(rng, amount, total, limit, slope):
    if amount == 2:
        one = jax.random.randint(rng, (), max(1, total - limit), min(limit, total - 1) + 1)
        return jnp.stack([one, total - one])
    tallies = jnp.asarray(length_profile(amount, total, limit, slope), jnp.int32)
    twos = (amount - 1) // 2
    source_of, sink = tallies[1:1 + 2 * twos:2], tallies[2:2 + 2 * twos:2]
    margin = jnp.minimum(source_of - 1, limit - sink)
    moved = jax.random.randint(jax.random.fold_in(rng, 1), (twos,), 0, 1 << 20) % (margin + 1)
    tallies = tallies.at[1:1 + 2 * twos:2].set(source_of - moved).at[2:2 + 2 * twos:2].set(sink + moved)
    return tallies[jax.random.permutation(jax.random.fold_in(rng, 2), amount)]


def normal_values(rng, extent, deviation, bound, cuts=(), kind=jnp.bfloat16):
    array = deviation * jax.random.normal(rng, extent, jnp.float32)
    if cuts:
        array = array * level_of(rng, extent, cuts, -0.22, 0.18)
    return jnp.clip(array, -bound, bound).astype(kind)


def setup_inputs(seed: int = 0, part: int = 0) -> dict:
    arg_keys = jax.random.split(jax.random.key(seed), 12)
    own_keys = jax.random.split(jax.random.fold_in(arg_keys[11], part), 12)
    return {
        "layer_input_rows": draw_layer_input_rows(jax.random.fold_in(jax.random.fold_in(arg_keys[11], part), 71), part),
        "encoded_query_rows": draw_encoded_query_rows(jax.random.fold_in(jax.random.fold_in(arg_keys[11], part), 71), part),
        "encoded_key_rows": draw_encoded_key_rows(jax.random.fold_in(jax.random.fold_in(arg_keys[11], part), 71), part),
        "layer_norm_gain": jnp.clip(1.0 + 0.15 * jax.random.normal(arg_keys[3], (LAYER_COUNT, MODEL_WIDTH), jnp.float32), 0.25, 1.75),
        "base_value_matrix": normal_values(arg_keys[4], (LAYER_COUNT, MODEL_WIDTH, KEY_VALUE_HEADS * HEAD_SIZE), MODEL_WIDTH ** -0.5, 0.078125, ((0, 2), (1, 8))),
        "adapter_down_panels": normal_values(arg_keys[5], (LAYER_COUNT, SLOT_COUNT, MODEL_WIDTH, MAX_RANK), MODEL_WIDTH ** -0.5, 0.078125, ((0, 2), (1, 4), (2, 2))),
        "adapter_up_panels": normal_values(arg_keys[6], (LAYER_COUNT, SLOT_COUNT, MAX_RANK, KEY_VALUE_HEADS * HEAD_SIZE), MAX_RANK ** -0.5, 0.75, ((0, 2), (1, 4), (3, 2))),
        "request_token_lengths": uneven_parts(own_keys[7], REQUESTS, TOKEN_COUNT, TOKEN_COUNT // 2, 2).astype(jnp.int32),
        "adapter_per_request": set_ends(jax.random.randint(own_keys[8], (REQUESTS,), 0, SLOT_COUNT), jax.random.fold_in(own_keys[8], 1), 0, SLOT_COUNT - 1).astype(jnp.int32),
        "rank_per_adapter": set_ends(jax.random.randint(arg_keys[9], (SLOT_COUNT,), MAX_RANK // 4, MAX_RANK + 1), jax.random.fold_in(arg_keys[9], 1), MAX_RANK // 4, MAX_RANK).astype(jnp.int32),
        "slot_per_adapter": jax.random.permutation(arg_keys[10], SLOT_COUNT).astype(jnp.int32),
    }


query_scale = 168.0 ** (-0.5)
adapter_strength = 32.0
norm_eps = 1e-06

def requests_of(positions, request_token_lengths):
    request_ends = jnp.cumsum(request_token_lengths).astype(jnp.int32)
    return lax.optimization_barrier(jnp.sum((positions[:, None] >= request_ends[None, :]).astype(jnp.int32), axis=1))

def attend(queries, key_block_all, value_block_all, request_lookup):
    group_size = HEADS // KEY_VALUE_HEADS
    key_width = key_block_all.shape[1]
    keys_padded = jnp.concatenate([jnp.zeros((WINDOW, key_width), key_block_all.dtype), key_block_all], axis=0)
    values_padded = jnp.concatenate([jnp.zeros((WINDOW, key_width), value_block_all.dtype), value_block_all], axis=0)
    request_padded = jnp.concatenate([jnp.full((WINDOW,), -1, jnp.int32), request_lookup.astype(jnp.int32)], axis=0)
    key_span = WINDOW + TOK_DEV

    def one_block(block_index):
        first_row = (block_index * TOK_DEV).astype(jnp.int32)
        query_block = lax.dynamic_slice_in_dim(queries, first_row, TOK_DEV, 0).astype(jnp.float32)
        query_block = query_block.reshape(TOK_DEV, KEY_VALUE_HEADS, group_size, HEAD_SIZE)
        key_block = lax.dynamic_slice_in_dim(keys_padded, first_row, key_span, 0).astype(jnp.float32)
        key_block = key_block.reshape(key_span, KEY_VALUE_HEADS, HEAD_SIZE)
        value_block = lax.dynamic_slice_in_dim(values_padded, first_row, key_span, 0).astype(jnp.float32)
        value_block = value_block.reshape(key_span, KEY_VALUE_HEADS, HEAD_SIZE)
        own_requests = lax.dynamic_slice_in_dim(request_lookup.astype(jnp.int32), first_row, TOK_DEV, 0)
        seen_requests = lax.dynamic_slice_in_dim(request_padded, first_row, key_span, 0)
        query_place = first_row + jnp.arange(TOK_DEV, dtype=jnp.int32)
        key_place = first_row - WINDOW + jnp.arange(key_span, dtype=jnp.int32)
        live_mask = (key_place[None, :] <= query_place[:, None]) & (key_place[None, :] > query_place[:, None] - WINDOW)
        live_mask = live_mask & (seen_requests[None, :] == own_requests[:, None])
        scores = jnp.einsum('tgcd,jgd->gctj', query_block, key_block) * query_scale
        scores = jnp.where(live_mask[None, None], scores, jnp.float32(-1e+30))
        row_max = lax.optimization_barrier(jnp.max(scores, axis=-1, keepdims=True))
        weights = jnp.exp(scores - row_max)
        row_total = lax.optimization_barrier(jnp.sum(weights, axis=-1, keepdims=True))
        softmax_rows = (weights / row_total).astype(jnp.bfloat16)
        mixed_heads = jnp.einsum('gctj,jgd->tgcd', softmax_rows.astype(jnp.float32), value_block)
        return mixed_heads.astype(jnp.bfloat16).reshape(TOK_DEV, HEADS * HEAD_SIZE)
    blocks = lax.map(one_block, jnp.arange(TOKEN_COUNT // TOK_DEV, dtype=jnp.int32))
    return blocks.reshape(TOKEN_COUNT, HEADS * HEAD_SIZE)

def reference(layer_input_rows, encoded_query_rows, encoded_key_rows, layer_norm_gain, base_value_matrix, adapter_down_panels, adapter_up_panels, request_token_lengths, adapter_per_request, rank_per_adapter, slot_per_adapter):
    positions = jnp.arange(TOKEN_COUNT, dtype=jnp.int32)
    request_lookup = requests_of(positions, request_token_lengths)
    columns = jnp.arange(MAX_RANK, dtype=jnp.int32)
    outputs = []
    for layer_number in range(LAYER_COUNT):
        wide_rows = layer_input_rows[layer_number].astype(jnp.float32)
        normalized_rows = wide_rows * lax.rsqrt(lax.optimization_barrier(jnp.mean(wide_rows * wide_rows, axis=1, keepdims=True)) + norm_eps)
        normalized_rows = (normalized_rows * layer_norm_gain[layer_number][None, :]).astype(jnp.bfloat16)
        value_base_rows = jnp.dot(normalized_rows, base_value_matrix[layer_number], preferred_element_type=jnp.float32)
        reduced_rows = jnp.zeros((TOKEN_COUNT, MAX_RANK), jnp.float32)
        for request_number in range(REQUESTS):
            adapter_id = adapter_per_request[request_number]
            slot_number = slot_per_adapter[adapter_id]
            rank_value = rank_per_adapter[adapter_id]
            keep_mask = (request_lookup == request_number)[:, None] & (columns < rank_value)[None, :]
            matrix_product = jnp.dot(normalized_rows, adapter_down_panels[layer_number, slot_number], preferred_element_type=jnp.float32)
            reduced_rows = reduced_rows + jnp.where(keep_mask, matrix_product, jnp.float32(0.0))
        reduced_rows = reduced_rows.astype(jnp.bfloat16)
        adapter_value = jnp.zeros((TOKEN_COUNT, KEY_VALUE_HEADS * HEAD_SIZE), jnp.float32)
        for request_number in range(REQUESTS):
            adapter_id = adapter_per_request[request_number]
            slot_number = slot_per_adapter[adapter_id]
            adapter_scale = adapter_strength / rank_per_adapter[adapter_id].astype(jnp.float32)
            raised_rows = jnp.dot(reduced_rows, adapter_up_panels[layer_number, slot_number], preferred_element_type=jnp.float32)
            adapter_value = adapter_value + jnp.where((request_lookup == request_number)[:, None], adapter_scale * raised_rows, jnp.float32(0.0))
        value_output_rows = (value_base_rows + adapter_value).astype(jnp.bfloat16)
        outputs.append(attend(encoded_query_rows[layer_number], encoded_key_rows[layer_number], value_output_rows, request_lookup))
    return jnp.stack(outputs)
```

```python
import functools

import jax
import jax.numpy as jnp
from jax import lax
from jax.experimental import pallas as pl
from jax.experimental.pallas import tpu as pltpu
from jax.sharding import PartitionSpec as P

WINDOW = 1024
HEADS = 16
KEY_VALUE_HEADS = 8
HEAD_SIZE = 128
LANES = 128

query_scale = 168.0 ** (-0.5)
adapter_strength = 32.0
norm_eps = 1e-06

VMEM = pl.BlockSpec(memory_space=pltpu.VMEM)
SMEM = pl.BlockSpec(memory_space=pltpu.SMEM)
ANY = pl.BlockSpec(memory_space=pl.ANY)
PARAMS = pltpu.CompilerParams(vmem_limit_bytes=32 * 1024 * 1024)
bf16 = jnp.bfloat16
f32 = jnp.float32


def turn(value, axis, steps):
    count = lax.axis_size(axis)
    return lax.ppermute(value, axis, [(i, (i + steps) % count) for i in range(count)])


class Sizes:
    def __init__(self, x, queries, down, up, requests):
        self.seq = lax.axis_size("seq")
        self.groups = lax.axis_size("groups")
        self.rows = x.shape[0]
        self.rows_half = self.rows // 2
        self.width = x.shape[1]
        self.half = down.shape[1]
        self.side = self.seq // 2
        self.features = self.width // self.seq
        self.slots_here, self.rank = down.shape[0], down.shape[2]
        self.requests = requests
        self.heads_here = up.shape[2] // HEAD_SIZE
        self.group_size = HEADS // KEY_VALUE_HEADS
        self.tokens = self.rows * self.seq
        tiles = [
            -(-((i * self.features) % LANES + self.features) // LANES) for i in range(self.side)
        ]
        self.tiles = max(tiles)
        self.span = self.tiles * LANES

    def fits(self):
        return (
            lax.axis_size("owner") == 2
            and self.seq % 2 == 0
            and self.half % LANES == 0
            and self.half * 2 == self.width
            and self.heads_here == self.seq
            and self.slots_here == self.groups
            and self.features % 32 == 0
            and self.rows % 64 == 0
            and 2 * self.rank == LANES
        )

    def start_in_half(self, i):
        return jnp.minimum((i * self.features) // LANES, self.half // LANES - self.tiles) * LANES

    def start(self, chip):
        return (chip // self.side) * self.half + self.start_in_half(chip % self.side)


def request_column(sz, lengths, position):
    found = jnp.zeros_like(position)
    end = jnp.int32(0)
    for r in range(sz.requests):
        end = end + lengths[r]
        found = found + (position >= end).astype(jnp.int32)
    return found


def panels_kernel(sz, down, *outs_and_sem):
    outs, sem = outs_and_sem[:-1], outs_and_sem[-1]
    here, group = lax.axis_index("seq"), lax.axis_index("groups")
    copies = []
    for m, out in enumerate(outs):
        first = pl.multiple_of(sz.start_in_half((here + m) % sz.side), LANES)
        copies.append(
            pltpu.make_async_copy(down.at[group, :, pl.ds(first, sz.span)], out, sem.at[m])
        )
    for copy in copies:
        copy.start()
    for copy in copies:
        copy.wait()


def norm_kernel(sz, x, gain, *outs_and_scratch):
    outs, whole = outs_and_scratch[:-1], outs_and_scratch[-1]
    here, core = lax.axis_index("seq"), lax.axis_index("owner")
    rows = x[pl.ds(pl.multiple_of(core * sz.rows_half, sz.rows_half), sz.rows_half), :]
    rows = rows.astype(f32)
    rows = rows * lax.rsqrt(jnp.mean(rows * rows, axis=1, keepdims=True) + norm_eps)
    whole[...] = (rows * gain[...]).astype(bf16)
    lane = lax.broadcasted_iota(jnp.int32, (sz.rows_half, sz.span), 1)
    for k, out in enumerate(outs):
        chip = (here + k) % sz.seq
        first = pl.multiple_of(sz.start(chip), LANES)
        skip = chip * sz.features - first
        piece = whole[:, pl.ds(first, sz.span)]
        live = (lane >= skip) & (lane < skip + sz.features)
        out[...] = jnp.where(live, piece.astype(f32), 0.0).astype(bf16)


def heads_kernel(sz, queries, keys, up, *outs_and_sem):
    outs, sem = outs_and_sem[:-1], outs_and_sem[-1]
    here = lax.axis_index("seq")
    copies = []
    for k, out in enumerate(outs):
        head = (here + k) % sz.seq
        parts = []
        for c in range(sz.group_size):
            first = pl.multiple_of((head * sz.group_size + c) * HEAD_SIZE, HEAD_SIZE)
            parts.append(queries.at[:, pl.ds(first, HEAD_SIZE)])
        first = pl.multiple_of(head * HEAD_SIZE, HEAD_SIZE)
        parts.append(keys.at[:, pl.ds(first, HEAD_SIZE)])
        for j in range(sz.slots_here):
            parts.append(up.at[j, :, pl.ds(first, HEAD_SIZE)])
        at = 0
        for part in parts:
            size = part.shape[0]
            copies.append(
                pltpu.make_async_copy(part, out.at[pl.ds(at, size)], sem.at[len(copies)])
            )
            at += size
    for copy in copies:
        copy.start()
    for copy in copies:
        copy.wait()


def softmax_kernel(sz, lengths, *refs):
    pieces, out = refs[: sz.seq], refs[sz.seq]
    query, key = refs[sz.seq + 1 :]
    here = lax.axis_index("seq")
    for k, piece in enumerate(pieces):
        chip = (here + sz.seq - k) % sz.seq
        place = pl.ds(pl.multiple_of(chip * sz.rows, sz.rows), sz.rows)
        for c in range(sz.group_size):
            query[c, place, :] = piece[c * sz.rows : (c + 1) * sz.rows]
        key[place, :] = piece[sz.group_size * sz.rows : (sz.group_size + 1) * sz.rows]
    shape = (sz.tokens, sz.tokens)
    mine = lax.broadcasted_iota(jnp.int32, shape, 0)
    theirs = lax.broadcasted_iota(jnp.int32, shape, 1)
    live = (theirs <= mine) & (theirs > mine - WINDOW)
    live = live & (request_column(sz, lengths, mine) == request_column(sz, lengths, theirs))
    for c in range(sz.group_size):
        scores = lax.dot_general(
            query[c], key[...], (((1,), (1,)), ((), ())), preferred_element_type=f32
        )
        scores = jnp.where(live, scores * query_scale, -1e30)
        weights = jnp.exp(scores - jnp.max(scores, axis=1, keepdims=True))
        out[c] = (weights / jnp.sum(weights, axis=1, keepdims=True)).astype(bf16)


def project_kernel(sz, lengths, adapters, ranks, slots, base, base_other, *refs):
    pieces, refs = refs[: sz.seq], refs[sz.seq :]
    count = 2 * sz.groups * sz.side
    panels, refs = refs[:count], refs[count:]
    outs, (rows, matrix, picked, product, base_sem, panel_sem) = refs[: sz.seq], refs[sz.seq :]
    here, core, group = (lax.axis_index(a) for a in ("seq", "owner", "groups"))
    depth = base.shape[0]
    skip = here * sz.features - sz.start(here)
    spare = sz.span - sz.features
    matrix[0:spare] = jnp.zeros((spare, matrix.shape[1]), bf16)
    matrix[sz.span - spare :] = jnp.zeros((spare, matrix.shape[1]), bf16)
    copies = []
    for j, (ref, owner) in enumerate(((base, core), (base_other, 1 - core))):
        first = pl.multiple_of(skip + owner * depth, 16)
        copies.append(
            pltpu.make_async_copy(ref, matrix.at[pl.ds(first, depth)], base_sem.at[j])
        )
        copies[-1].start()
    rank_of = []
    for r in range(sz.requests):
        adapter = adapters[r]
        slot = slots[adapter]
        rank_of.append(ranks[adapter])
        chip = slot // sz.slots_here
        other = jnp.where(chip // sz.side == core, 0, 1)
        away = lax.rem(slot % sz.slots_here - group + sz.groups, sz.groups)
        m = lax.rem(here % sz.side - chip % sz.side + sz.side, sz.side)
        index = (other * sz.groups + away) * sz.side + m
        for p, panel in enumerate(panels):

            @pl.when(index == p)
            def _(panel=panel, r=r):
                pltpu.make_async_copy(
                    panel, picked.at[pl.ds(r * sz.rank, sz.rank)], panel_sem.at[r]
                ).start()

    for k, piece in enumerate(pieces):
        chip = (here + sz.seq - k) % sz.seq
        rows[pl.ds(pl.multiple_of(chip * sz.rows_half, sz.rows_half), sz.rows_half), :] = piece[...]
    for r in range(sz.requests):
        pltpu.make_async_copy(
            panels[0], picked.at[pl.ds(r * sz.rank, sz.rank)], panel_sem.at[r]
        ).wait()
    low = lax.dot_general(
        rows[...], picked[...], (((1,), (1,)), ((), ())), preferred_element_type=f32
    )
    count = sz.seq * sz.rows_half
    row = lax.broadcasted_iota(jnp.int32, (count, sz.rank), 0)
    column = lax.broadcasted_iota(jnp.int32, (count, sz.rank), 1)
    position = (row // sz.rows_half) * sz.rows + core * sz.rows_half + row % sz.rows_half
    request = request_column(sz, lengths, position)
    reduced = jnp.zeros((count, sz.rank), f32)
    for r in range(sz.requests):
        keep = (request == r) & (column < rank_of[r])
        reduced = reduced + jnp.where(keep, low[:, r * sz.rank : (r + 1) * sz.rank], 0.0)
    packed = jnp.concatenate([reduced[: count // 2], reduced[count // 2 :]], axis=1).astype(bf16)
    for copy in copies:
        copy.wait()
    product[...] = jnp.dot(rows[...], matrix[...], preferred_element_type=f32).astype(bf16)
    for k, out in enumerate(outs):
        head = (here + k) % sz.seq
        for j in range(2):
            first = pl.multiple_of((j * sz.heads_here + head) * HEAD_SIZE, HEAD_SIZE)
            out[j * count : (j + 1) * count] = product[:, pl.ds(first, HEAD_SIZE)]
        out[2 * count :] = packed


def add_kernel(sz, *refs):
    pieces, (kept, sent) = refs[: sz.seq], refs[sz.seq :]
    core = lax.axis_index("owner")
    count = sz.seq * sz.rows_half
    for out, head in ((kept, core), (sent, 1 - core)):
        place = pl.ds(pl.multiple_of(head * count, count), count)
        out[:count] = sum(piece[place, :].astype(f32) for piece in pieces).astype(bf16)
    low = sum(piece[2 * count :].astype(f32) for piece in pieces).astype(bf16)
    kept[count:] = low
    sent[count:] = low


def mix_kernel(sz, lengths, adapters, ranks, slots, kept, received, softmax, *refs):
    pieces, refs = refs[: sz.seq], refs[sz.seq :]
    outs, (base, low, wide, raise_all, raise_picked, mixed) = refs[: sz.seq], refs[sz.seq :]
    here, core = lax.axis_index("seq"), lax.axis_index("owner")
    count = sz.seq * sz.rows_half
    for ref, owner in ((kept, core), (received, 1 - core)):
        reduced = jnp.concatenate([ref[count:, : sz.rank], ref[count:, sz.rank :]], axis=0)
        for chip in range(sz.seq):
            place = pl.ds(
                pl.multiple_of(chip * sz.rows + owner * sz.rows_half, sz.rows_half), sz.rows_half
            )
            own = slice(chip * sz.rows_half, (chip + 1) * sz.rows_half)
            base[place, :] = ref[own]
            low[place, :] = reduced[own]
    panel_first = (sz.group_size + 1) * sz.rows
    for k, piece in enumerate(pieces):
        size = sz.slots_here * sz.rank
        raise_all[k * size : (k + 1) * size] = piece[panel_first : panel_first + size]
    position = lax.broadcasted_iota(jnp.int32, (sz.tokens, sz.rank), 0)
    request = request_column(sz, lengths, position)
    position = lax.broadcasted_iota(jnp.int32, (sz.tokens, HEAD_SIZE), 0)
    request_wide = request_column(sz, lengths, position)
    rank_here = jnp.ones((sz.tokens, HEAD_SIZE), jnp.int32)
    reduced = low[...].astype(f32)
    for r in range(sz.requests):
        adapter = adapters[r]
        slot = slots[adapter]
        rank_here = jnp.where(request_wide == r, ranks[adapter], rank_here)
        k = lax.rem(here - slot // sz.slots_here + sz.seq, sz.seq)
        first = (k * sz.slots_here + slot % sz.slots_here) * sz.rank
        own = slice(r * sz.rank, (r + 1) * sz.rank)
        raise_picked[own] = raise_all[pl.ds(pl.multiple_of(first, sz.rank), sz.rank), :]
        wide[:, own] = jnp.where(request == r, reduced, 0.0).astype(bf16)
    scale = adapter_strength / rank_here.astype(f32)
    raised = jnp.dot(wide[...], raise_picked[...], preferred_element_type=f32)
    values = (base[...].astype(f32) + scale * raised).astype(bf16)
    for c in range(sz.group_size):
        mixed[:, c * HEAD_SIZE : (c + 1) * HEAD_SIZE] = jnp.dot(
            softmax[c], values, preferred_element_type=f32
        ).astype(bf16)
    for k, out in enumerate(outs):
        chip = (here + k) % sz.seq
        out[...] = mixed[pl.ds(pl.multiple_of(chip * sz.rows, sz.rows), sz.rows), :]


def place_kernel(sz, *refs):
    pieces, out = refs[: sz.seq], refs[sz.seq]
    here = lax.axis_index("seq")
    wide = sz.group_size * HEAD_SIZE
    for k, piece in enumerate(pieces):
        head = (here + sz.seq - k) % sz.seq
        out[:, pl.ds(pl.multiple_of(head * wide, wide), wide)] = piece[...]


def by_heads(sz, x, queries, keys, gain, base, down, up, lengths, adapters, ranks, slots):
    count = sz.seq * sz.rows_half
    around = range(1, sz.seq)

    panel = jax.ShapeDtypeStruct((sz.rank, sz.span), bf16)
    sent = pl.pallas_call(
        functools.partial(panels_kernel, sz),
        out_shape=[panel] * sz.side,
        in_specs=[ANY],
        out_specs=[ANY] * sz.side,
        scratch_shapes=[pltpu.SemaphoreType.DMA((sz.side,))],
        compiler_params=PARAMS,
        name="panels_out",
    )(jnp.swapaxes(down, 1, 2))
    own_line = []
    for m in range(sz.side):
        pairs = [
            (h * 2 + c, (c * sz.side + (h + m) % sz.side) * 2 + h // sz.side)
            for h in range(sz.seq)
            for c in range(2)
        ]
        own_line.append(lax.ppermute(sent[m], ("seq", "owner"), pairs))

    rows_out = pl.pallas_call(
        functools.partial(norm_kernel, sz),
        out_shape=[jax.ShapeDtypeStruct((sz.rows_half, sz.span), bf16)] * sz.seq,
        in_specs=[VMEM, VMEM],
        out_specs=[VMEM] * sz.seq,
        scratch_shapes=[pltpu.VMEM((sz.rows_half, sz.width), bf16)],
        compiler_params=PARAMS,
        name="norm_rows",
    )(x, gain)
    rows_in = [rows_out[0]] + [turn(rows_out[k], "seq", k) for k in around]
    base_other = turn(base, "owner", 1)

    here_panels = list(own_line)
    for k in range(1, sz.groups):
        here_panels += [turn(p, "groups", sz.groups - k) for p in own_line]
    all_panels = here_panels + [turn(p, "owner", 1) for p in here_panels]

    heads_rows = (sz.group_size + 1) * sz.rows + sz.slots_here * sz.rank
    parts = sz.group_size + 1 + sz.slots_here
    heads_out = pl.pallas_call(
        functools.partial(heads_kernel, sz),
        out_shape=[jax.ShapeDtypeStruct((heads_rows, HEAD_SIZE), bf16)] * sz.seq,
        in_specs=[ANY] * 3,
        out_specs=[ANY] * sz.seq,
        scratch_shapes=[pltpu.SemaphoreType.DMA((parts * sz.seq,))],
        compiler_params=PARAMS,
        name="heads_out",
    )(queries, keys, up)
    heads_in = [heads_out[0]] + [turn(heads_out[k], "seq", k) for k in around]

    softmax = pl.pallas_call(
        functools.partial(softmax_kernel, sz),
        out_shape=jax.ShapeDtypeStruct((sz.group_size, sz.tokens, sz.tokens), bf16),
        in_specs=[SMEM] + [VMEM] * sz.seq,
        out_specs=VMEM,
        scratch_shapes=[
            pltpu.VMEM((sz.group_size, sz.tokens, HEAD_SIZE), bf16),
            pltpu.VMEM((sz.tokens, HEAD_SIZE), bf16),
        ],
        compiler_params=PARAMS,
        name="softmax_rows",
    )(lengths, *heads_in)

    partial_rows = 2 * count + count // 2
    partial_out = pl.pallas_call(
        functools.partial(project_kernel, sz),
        out_shape=[jax.ShapeDtypeStruct((partial_rows, HEAD_SIZE), bf16)] * sz.seq,
        in_specs=[SMEM] * 4 + [ANY] * 2 + [VMEM] * sz.seq + [ANY] * len(all_panels),
        out_specs=[VMEM] * sz.seq,
        scratch_shapes=[
            pltpu.VMEM((count, sz.span), bf16),
            pltpu.VMEM((sz.span, base.shape[1]), bf16),
            pltpu.VMEM((sz.requests * sz.rank, sz.span), bf16),
            pltpu.VMEM((count, base.shape[1]), bf16),
            pltpu.SemaphoreType.DMA((2,)),
            pltpu.SemaphoreType.DMA((sz.requests,)),
        ],
        compiler_params=PARAMS,
        name="project",
    )(lengths, adapters, ranks, slots, base, base_other, *rows_in, *all_panels)
    partial_in = [partial_out[0]] + [turn(partial_out[k], "seq", k) for k in around]

    half_shape = jax.ShapeDtypeStruct((count + count // 2, HEAD_SIZE), bf16)
    kept, sent = pl.pallas_call(
        functools.partial(add_kernel, sz),
        out_shape=[half_shape] * 2,
        in_specs=[VMEM] * sz.seq,
        out_specs=[VMEM] * 2,
        compiler_params=PARAMS,
        name="add_partials",
    )(*partial_in)
    received = turn(sent, "owner", 1)

    wide = sz.group_size * HEAD_SIZE
    mixed = pl.pallas_call(
        functools.partial(mix_kernel, sz),
        out_shape=[jax.ShapeDtypeStruct((sz.rows, wide), bf16)] * sz.seq,
        in_specs=[SMEM] * 4 + [VMEM] * (3 + sz.seq),
        out_specs=[VMEM] * sz.seq,
        scratch_shapes=[
            pltpu.VMEM((sz.tokens, HEAD_SIZE), bf16),
            pltpu.VMEM((sz.tokens, sz.rank), bf16),
            pltpu.VMEM((sz.tokens, sz.requests * sz.rank), bf16),
            pltpu.VMEM((sz.seq * sz.slots_here * sz.rank, HEAD_SIZE), bf16),
            pltpu.VMEM((sz.requests * sz.rank, HEAD_SIZE), bf16),
            pltpu.VMEM((sz.tokens, wide), bf16),
        ],
        compiler_params=PARAMS,
        name="mix_values",
    )(lengths, adapters, ranks, slots, kept, received, softmax, *heads_in)
    mixed_in = [mixed[0]] + [turn(mixed[k], "seq", k) for k in around]
    return pl.pallas_call(
        functools.partial(place_kernel, sz),
        out_shape=jax.ShapeDtypeStruct((sz.rows, sz.seq * wide), bf16),
        in_specs=[VMEM] * sz.seq,
        out_specs=VMEM,
        compiler_params=PARAMS,
        name="place_heads",
    )(*mixed_in)


def broadcast(x, axis, root):
    mine = lax.axis_index(axis) == root
    return lax.psum(jnp.where(mine, x, jnp.zeros_like(x)), axis)


def from_behind(value, axis, steps):
    count = lax.axis_size(axis)
    first, last = (max(0, -steps), min(count, count - steps))
    return lax.ppermute(value, axis, [(source, source + steps) for source in range(first, last)])


def by_tokens(
    layer_input_rows,
    encoded_query_rows,
    encoded_key_rows,
    layer_norm_gain,
    base_value_matrix,
    adapter_down_panels,
    adapter_up_panels,
    request_token_lengths,
    adapter_per_request,
    rank_per_adapter,
    slot_per_adapter,
):
    hidden = layer_input_rows[0]
    row_count = hidden.shape[0]
    seq_now = lax.axis_index("seq")
    owner_now = lax.axis_index("owner")
    reach_count = min(WINDOW // row_count, lax.axis_size("seq") - 1)
    requests = request_token_lengths.shape[0]
    library = slot_per_adapter.shape[0]
    slots_here = adapter_down_panels.shape[1]
    rows_halved = adapter_down_panels.shape[2]
    rank_span_width = adapter_down_panels.shape[3]
    key_value_halved = adapter_up_panels.shape[3]
    group_size = HEADS // KEY_VALUE_HEADS
    request_ends = jnp.cumsum(request_token_lengths)
    position = seq_now * row_count + jnp.arange(row_count, dtype=jnp.int32)
    context = seq_now * row_count + jnp.arange(-reach_count * row_count, row_count, dtype=jnp.int32)
    request_lookup = jnp.sum((position[:, None] >= request_ends[None, :]).astype(jnp.int32), axis=1)
    request_ctx = jnp.sum((context[:, None] >= request_ends[None, :]).astype(jnp.int32), axis=1)
    live_mask = (context[None, :] <= position[:, None]) & (
        context[None, :] > position[:, None] - WINDOW
    )
    live_mask = (
        live_mask & (context[None, :] >= 0) & (request_ctx[None, :] == request_lookup[:, None])
    )
    choose = adapter_per_request[:, None] == jnp.arange(library, dtype=jnp.int32)[None, :]
    slot_of = jnp.sum(jnp.where(choose, slot_per_adapter[None, :], 0), axis=1)
    rank_lookup = jnp.sum(jnp.where(choose, rank_per_adapter[None, :], 0), axis=1)
    scale_lookup = adapter_strength / rank_lookup.astype(jnp.float32)
    in_request = request_lookup[:, None] == jnp.arange(requests, dtype=jnp.int32)[None, :]
    column_live = jnp.arange(rank_span_width, dtype=jnp.int32)[None, :] < rank_lookup[:, None]
    row_gain_weight = jnp.where(in_request, scale_lookup[None, :], jnp.float32(0.0))
    down_panel_here = adapter_down_panels[0]
    up_panel_here = adapter_up_panels[0]
    queries = encoded_query_rows[0]
    keys_own = encoded_key_rows[0]
    key_heads = keys_own.shape[1] // HEAD_SIZE
    wide_rows = hidden.astype(jnp.float32)
    normalized_rows = wide_rows * lax.rsqrt(
        jnp.mean(wide_rows * wide_rows, axis=1, keepdims=True) + norm_eps
    )
    normalized_rows = (normalized_rows * layer_norm_gain[0][None, :]).astype(jnp.bfloat16)
    normed_half = lax.dynamic_slice_in_dim(normalized_rows, owner_now * rows_halved, rows_halved, 1)
    full_value = jnp.dot(
        normalized_rows,
        lax.all_gather(base_value_matrix[0], ("seq", "owner"), axis=0, tiled=True),
        preferred_element_type=jnp.float32,
    )
    value_base_rows = lax.dynamic_slice_in_dim(
        full_value, owner_now * key_value_halved, key_value_halved, 1
    )

    def fetch_one(reduced_rows, request_index):
        owner_slot = slot_of[request_index]
        holder = owner_slot // slots_here
        local_slot = owner_slot % slots_here
        down_local = lax.dynamic_slice_in_dim(down_panel_here, local_slot, 1, 0)
        up_local = lax.dynamic_slice_in_dim(up_panel_here, local_slot, 1, 0)
        down_piece, up_piece = (
            broadcast(down_local, "seq", holder),
            broadcast(up_local, "seq", holder),
        )
        keep_mask = in_request[:, request_index][:, None] & column_live[request_index][None, :]
        matrix_product = jnp.dot(normed_half, down_piece[0], preferred_element_type=jnp.float32)
        return (reduced_rows + jnp.where(keep_mask, matrix_product, jnp.float32(0.0)), up_piece[0])

    start_low = jnp.zeros((row_count, rank_span_width), jnp.float32)
    reduced_rows, panels_up = lax.scan(fetch_one, start_low, jnp.arange(requests, dtype=jnp.int32))
    reduced_rows = lax.psum(reduced_rows, "owner").astype(jnp.bfloat16)
    raised_rows = jnp.einsum(
        "tr,qrk->qtk", reduced_rows, panels_up, preferred_element_type=jnp.float32
    )
    adapter_value = jnp.sum(row_gain_weight.T[:, :, None] * raised_rows, axis=0)
    value_output_rows = (value_base_rows + adapter_value).astype(jnp.bfloat16)
    key_parts = []
    value_parts = []
    for shift_by in range(reach_count, 0, -1):
        key_piece, value_piece = from_behind((keys_own, value_output_rows), "seq", shift_by)
        key_parts.append(key_piece)
        value_parts.append(value_piece)
    keys_all = jnp.concatenate(key_parts + [keys_own], axis=0)
    values_all = jnp.concatenate(value_parts + [value_output_rows], axis=0)
    query_view = queries.reshape(row_count, key_heads, group_size, HEAD_SIZE)
    key_view = keys_all.reshape(-1, key_heads, HEAD_SIZE)
    value_view = values_all.reshape(-1, key_heads, HEAD_SIZE)
    head_outputs = []
    for head_index in range(key_heads):
        query_head = query_view[:, head_index]
        scores = (
            jnp.einsum(
                "tcd,jd->ctj",
                query_head,
                key_view[:, head_index],
                preferred_element_type=jnp.float32,
            )
            * query_scale
        )
        scores = jnp.where(live_mask[None], scores, jnp.float32(-1e30))
        row_max = jnp.max(scores, axis=-1, keepdims=True)
        weights = jnp.exp(scores - row_max)
        row_total = jnp.sum(weights, axis=-1, keepdims=True)
        softmax_rows = (weights / row_total).astype(jnp.bfloat16)
        mixed = jnp.einsum(
            "ctj,jd->tcd",
            softmax_rows,
            value_view[:, head_index],
            preferred_element_type=jnp.float32,
        )
        head_outputs.append(mixed.astype(jnp.bfloat16).reshape(row_count, group_size * HEAD_SIZE))
    result = jnp.concatenate(head_outputs, axis=1)
    return result[None]


def per_device(
    layer_input_rows,
    encoded_query_rows,
    encoded_key_rows,
    layer_norm_gain,
    base_value_matrix,
    adapter_down_panels,
    adapter_up_panels,
    request_token_lengths,
    adapter_per_request,
    rank_per_adapter,
    slot_per_adapter,
):
    sz = Sizes(
        layer_input_rows[0],
        encoded_query_rows[0],
        adapter_down_panels[0],
        adapter_up_panels[0],
        request_token_lengths.shape[0],
    )
    scalars = (request_token_lengths, adapter_per_request, rank_per_adapter, slot_per_adapter)
    if not sz.fits():
        return by_tokens(
            layer_input_rows,
            encoded_query_rows,
            encoded_key_rows,
            layer_norm_gain,
            base_value_matrix,
            adapter_down_panels,
            adapter_up_panels,
            *scalars,
        )
    return by_heads(
        sz,
        layer_input_rows[0],
        encoded_query_rows[0],
        encoded_key_rows[0],
        layer_norm_gain,
        base_value_matrix[0],
        adapter_down_panels[0],
        adapter_up_panels[0],
        *scalars,
    )[None]


def solution(mesh):
    in_specs = (
        P("segment", ("groups", "seq"), None),
        P("segment", ("groups", "seq"), "owner"),
        P("segment", ("groups", "seq"), "owner"),
        P("segment", None),
        P("segment", ("seq", "owner"), None),
        P("segment", "seq", "owner", None),
        P("segment", "seq", None, "owner"),
        P("groups"),
        P("groups"),
        P(),
        P(),
    )
    out_specs = P("segment", ("groups", "seq"), "owner")
    return jax.shard_map(
        per_device, mesh=mesh, in_specs=in_specs, out_specs=out_specs, check_vma=False
    )
```

```python
import functools

import jax
import jax.numpy as jnp
from jax import lax
from jax.experimental import pallas as pl
from jax.experimental.pallas import tpu as pltpu
from jax.sharding import PartitionSpec as P

WINDOW = 1024
HEADS = 16
KEY_VALUE_HEADS = 8
HEAD_SIZE = 128
LANES = 128

query_scale = 168.0 ** (-0.5)
adapter_strength = 32.0
norm_eps = 1e-06

VMEM = pl.BlockSpec(memory_space=pltpu.VMEM)
SMEM = pl.BlockSpec(memory_space=pltpu.SMEM)
ANY = pl.BlockSpec(memory_space=pl.ANY)
HBM = pl.BlockSpec(memory_space=pltpu.HBM)
PARAMS = pltpu.CompilerParams(vmem_limit_bytes=16 * 1024 * 1024)
FIRST = pltpu.CompilerParams(vmem_limit_bytes=60 * 1024 * 1024)
bf16 = jnp.bfloat16
f32 = jnp.float32


def swap(value, axis, mask):
    return lax.ppermute(value, axis, [(i, i ^ mask) for i in range(lax.axis_size(axis))])


class Sizes:
    def __init__(self, x, queries, down, up, requests):
        self.seq = lax.axis_size("seq")
        self.groups = lax.axis_size("groups")
        self.rows = x.shape[0]
        self.rows_half = self.rows // 2
        self.width = x.shape[1]
        self.half = down.shape[1]
        self.side = self.seq // 2
        self.features = self.width // self.seq
        self.slots_here, self.rank = down.shape[0], down.shape[2]
        self.requests = requests
        self.heads_here = up.shape[2] // HEAD_SIZE
        self.group_size = HEADS // KEY_VALUE_HEADS
        self.tokens = self.rows * self.seq
        tiles = [
            -(-((i * self.features) % LANES + self.features) // LANES) for i in range(self.side)
        ]
        self.tiles = max(tiles)
        self.span = self.tiles * LANES

    def fits(self):
        return (
            lax.axis_size("owner") == 2
            and self.seq & (self.seq - 1) == 0
            and self.groups & (self.groups - 1) == 0
            and self.half % LANES == 0
            and self.half * 2 == self.width
            and self.heads_here == self.seq
            and self.slots_here == self.groups
            and self.features % 32 == 0
            and self.rows % 64 == 0
            and self.rank % self.rows_half == 0
            and self.pieces() * LANES <= self.span
            and 2 * self.rank == LANES
        )

    def pieces(self):
        return ((self.group_size + 1) * self.rows + self.slots_here * self.rank) // self.rows_half

    def start_in_half(self, i):
        return jnp.minimum((i * self.features) // LANES, self.half // LANES - self.tiles) * LANES

    def start(self, chip):
        return (chip // self.side) * self.half + self.start_in_half(chip % self.side)


def request_column(sz, table, position):
    found = jnp.zeros_like(position)
    for r in range(sz.requests):
        found = found + (position >= table[0, r]).astype(jnp.int32)
    return found


def table_kernel(sz, lengths, adapters, ranks, slots, out):
    here, core, group = (lax.axis_index(a) for a in ("seq", "owner", "groups"))
    end = jnp.int32(0)
    for r in range(sz.requests):
        end = end + lengths[r]
        adapter = adapters[r]
        slot = slots[adapter]
        chip, local = slot // sz.slots_here, slot % sz.slots_here
        other = jnp.where(chip // sz.side == core, 0, 1)
        m = (here % sz.side) ^ (chip % sz.side)
        out[0, r] = end
        out[1, r] = ranks[adapter]
        out[2, r] = (other * sz.groups + (local ^ group)) * sz.side + m
        out[3, r] = ((here ^ chip) * sz.slots_here + local) * sz.rank


def panels_kernel(sz, down, *outs_and_sem):
    outs, sem = outs_and_sem[:-1], outs_and_sem[-1]
    here, group = lax.axis_index("seq"), lax.axis_index("groups")
    copies = []
    for m, out in enumerate(outs):
        first = pl.multiple_of(sz.start_in_half((here % sz.side) ^ m), LANES)
        copies.append(
            pltpu.make_async_copy(down.at[group, :, pl.ds(first, sz.span)], out, sem.at[m])
        )
    for copy in copies:
        copy.start()
    for copy in copies:
        copy.wait()


def norm_kernel(sz, x, gain, queries, keys, up, *outs_and_scratch):
    outs, scratch = outs_and_scratch[: sz.seq], outs_and_scratch[sz.seq :]
    taken, gains, query, key, raised, whole, sem = scratch
    here, core = lax.axis_index("seq"), lax.axis_index("owner")
    place = pl.ds(pl.multiple_of(core * sz.rows_half, sz.rows_half), sz.rows_half)
    pairs = ((x.at[place], taken), (gain, gains), (queries, query), (keys, key), (up, raised))
    copies = [pltpu.make_async_copy(a, b, sem.at[i]) for i, (a, b) in enumerate(pairs)]
    for copy in copies:
        copy.start()
    for copy in copies[:2]:
        copy.wait()
    rows = taken[...].astype(f32)
    rows = rows * lax.rsqrt(jnp.mean(rows * rows, axis=1, keepdims=True) + norm_eps)
    whole[...] = (rows * gains[...]).astype(bf16)
    lane = lax.broadcasted_iota(jnp.int32, (sz.rows_half, sz.span), 1)
    for copy in copies[2:]:
        copy.wait()
    for k, out in enumerate(outs):
        head = here ^ k
        first = pl.multiple_of(sz.start(head), LANES)
        skip = head * sz.features - first
        piece = whole[:, pl.ds(first, sz.span)]
        live = (lane >= skip) & (lane < skip + sz.features)
        out[: sz.rows_half] = jnp.where(live, piece.astype(f32), 0.0).astype(bf16)
        parts = []
        for c in range(sz.group_size):
            first = pl.multiple_of((head * sz.group_size + c) * HEAD_SIZE, HEAD_SIZE)
            parts.append(query[:, pl.ds(first, HEAD_SIZE)])
        first = pl.multiple_of(head * HEAD_SIZE, HEAD_SIZE)
        parts.append(key[:, pl.ds(first, HEAD_SIZE)])
        for j in range(sz.slots_here):
            parts.append(raised[j, :, pl.ds(first, HEAD_SIZE)])
        at = 0
        for part in parts:
            for top in range(0, part.shape[0], sz.rows_half):
                out[sz.rows_half :, at : at + HEAD_SIZE] = part[top : top + sz.rows_half]
                at += HEAD_SIZE
        if at < sz.span:
            out[sz.rows_half :, at:] = jnp.zeros((sz.rows_half, sz.span - at), bf16)


def unpack(sz, piece, out, part, first, size):
    for top in range(0, size, sz.rows_half):
        lanes = slice((part + top // sz.rows_half) * HEAD_SIZE, (part + top // sz.rows_half + 1) * HEAD_SIZE)
        place = pl.ds(pl.multiple_of(first + top, sz.rows_half), sz.rows_half)
        out[place, :] = piece[sz.rows_half :, lanes]


def softmax_kernel(sz, table, *refs):
    pieces, out = refs[: sz.seq], refs[sz.seq]
    query, key = refs[sz.seq + 1 :]
    here = lax.axis_index("seq")
    parts = sz.rows // sz.rows_half
    for k, piece in enumerate(pieces):
        first = (here ^ k) * sz.rows
        for c in range(sz.group_size):
            unpack(sz, piece, query.at[c], c * parts, first, sz.rows)
        unpack(sz, piece, key, sz.group_size * parts, first, sz.rows)
    shape = (sz.tokens, sz.tokens)
    mine = lax.broadcasted_iota(jnp.int32, shape, 0)
    theirs = lax.broadcasted_iota(jnp.int32, shape, 1)
    live = (theirs <= mine) & (theirs > mine - WINDOW)
    live = live & (request_column(sz, table, mine) == request_column(sz, table, theirs))
    for c in range(sz.group_size):
        scores = lax.dot_general(
            query[c], key[...], (((1,), (1,)), ((), ())), preferred_element_type=f32
        )
        scores = jnp.where(live, scores * query_scale, -1e30)
        weights = jnp.exp(scores - jnp.max(scores, axis=1, keepdims=True))
        out[c] = (weights / jnp.sum(weights, axis=1, keepdims=True)).astype(bf16)


def matrix_kernel(sz, base, base_other, out, sem):
    here, core = lax.axis_index("seq"), lax.axis_index("owner")
    depth, wide = base.shape[0], out.shape[1]
    skip = here * sz.features - sz.start(here)
    spare = sz.span - sz.features
    out[0:spare] = jnp.zeros((spare, wide), bf16)
    out[sz.span - spare :] = jnp.zeros((spare, wide), bf16)
    columns = pl.ds(pl.multiple_of(core * wide, wide), wide)
    copies = []
    for j, (ref, owner) in enumerate(((base, core), (base_other, 1 - core))):
        place = pl.ds(pl.multiple_of(skip + owner * depth, 16), depth)
        copies.append(pltpu.make_async_copy(ref.at[:, columns], out.at[place], sem.at[j]))
        copies[-1].start()
    for copy in copies:
        copy.wait()


def gather_kernel(sz, *refs):
    pieces, out = refs[: sz.seq], refs[sz.seq]
    here = lax.axis_index("seq")
    for k, piece in enumerate(pieces):
        first = pl.multiple_of((here ^ k) * sz.rows_half, sz.rows_half)
        out[pl.ds(first, sz.rows_half), :] = piece[: sz.rows_half]


def project_kernel(sz, table, matrix, own, other, *refs):
    count = 2 * sz.groups * sz.side
    panels, refs = refs[:count], refs[count:]
    outs, (rows, stacked, product) = refs[: sz.seq], refs[sz.seq :]
    here, core = lax.axis_index("seq"), lax.axis_index("owner")
    for p, panel in enumerate(panels):
        stacked[p * sz.rank : (p + 1) * sz.rank] = panel[...]
    for ref, owner in ((own, core), (other, 1 - core)):
        for chip in range(sz.seq):
            first = pl.multiple_of(chip * sz.rows + owner * sz.rows_half, sz.rows_half)
            rows[pl.ds(first, sz.rows_half), :] = ref[
                chip * sz.rows_half : (chip + 1) * sz.rows_half
            ]
    product[...] = jnp.dot(rows[...], matrix[...], preferred_element_type=f32).astype(bf16)
    for k, out in enumerate(outs):
        first = pl.multiple_of((here ^ k) * HEAD_SIZE, HEAD_SIZE)
        out[: sz.tokens] = product[:, pl.ds(first, HEAD_SIZE)]
    low = lax.dot_general(
        rows[...], stacked[...], (((1,), (1,)), ((), ())), preferred_element_type=f32
    )
    shape = (sz.tokens, sz.rank)
    request = request_column(sz, table, lax.broadcasted_iota(jnp.int32, shape, 0))
    column = lax.broadcasted_iota(jnp.int32, shape, 1)
    panel_here = jnp.full(shape, -1)
    for r in range(sz.requests):
        panel_here = jnp.where((request == r) & (column < table[1, r]), table[2, r], panel_here)
    reduced = jnp.zeros(shape, f32)
    for p in range(count):
        reduced = jnp.where(panel_here == p, low[:, p * sz.rank : (p + 1) * sz.rank], reduced)
    half = sz.tokens // 2
    packed = jnp.concatenate([reduced[:half], reduced[half:]], axis=1).astype(bf16)
    for out in outs:
        out[sz.tokens :] = packed


def mix_kernel(sz, table, softmax, *refs):
    pieces, refs = refs[: sz.seq], refs[sz.seq :]
    partials, refs = refs[: sz.seq], refs[sz.seq :]
    outs, (wide, raise_all, raise_picked, mixed) = refs[: sz.seq], refs[sz.seq :]
    here = lax.axis_index("seq")
    parts = (sz.group_size + 1) * (sz.rows // sz.rows_half)
    for k, piece in enumerate(pieces):
        size = sz.slots_here * sz.rank
        unpack(sz, piece, raise_all, parts, k * size, size)
    position = lax.broadcasted_iota(jnp.int32, (sz.tokens, sz.rank), 0)
    request = request_column(sz, table, position)
    position = lax.broadcasted_iota(jnp.int32, (sz.tokens, HEAD_SIZE), 0)
    request_wide = request_column(sz, table, position)
    rank_here = jnp.ones((sz.tokens, HEAD_SIZE), jnp.int32)
    low = sum(partial[sz.tokens :].astype(f32) for partial in partials)
    low = jnp.concatenate([low[:, : sz.rank], low[:, sz.rank :]], axis=0)
    for r in range(sz.requests):
        rank_here = jnp.where(request_wide == r, table[1, r], rank_here)
        own = slice(r * sz.rank, (r + 1) * sz.rank)
        raise_picked[own] = raise_all[pl.ds(pl.multiple_of(table[3, r], sz.rank), sz.rank), :]
        wide[:, own] = jnp.where(request == r, low, 0.0).astype(bf16)
    scale = adapter_strength / rank_here.astype(f32)
    raised = jnp.dot(wide[...], raise_picked[...], preferred_element_type=f32)
    base = sum(partial[: sz.tokens].astype(f32) for partial in partials)
    values = (base + scale * raised).astype(bf16)
    for c in range(sz.group_size):
        mixed[:, c * HEAD_SIZE : (c + 1) * HEAD_SIZE] = jnp.dot(
            softmax[c], values, preferred_element_type=f32
        ).astype(bf16)
    for k, out in enumerate(outs):
        chip = here ^ k
        out[...] = mixed[pl.ds(pl.multiple_of(chip * sz.rows, sz.rows), sz.rows), :]


def place_kernel(sz, *refs):
    pieces, out = refs[: sz.seq], refs[sz.seq]
    here = lax.axis_index("seq")
    wide = sz.group_size * HEAD_SIZE
    for k, piece in enumerate(pieces):
        head = here ^ k
        out[:, pl.ds(pl.multiple_of(head * wide, wide), wide)] = piece[...]


def by_heads(sz, x, queries, keys, gain, base, down, up, lengths, adapters, ranks, slots):
    around = range(1, sz.seq)
    half_columns = base.shape[1] // 2
    spread = (2 * sz.rows_half, sz.span)

    def call(kernel, name, ins, outs, args, scratch=(), params=PARAMS):
        return pl.pallas_call(
            functools.partial(kernel, sz),
            out_shape=[jax.ShapeDtypeStruct(shape, dtype) for shape, dtype, _ in outs],
            in_specs=ins,
            out_specs=[spec for _, _, spec in outs],
            scratch_shapes=list(scratch),
            compiler_params=params,
            name=name,
        )(*args)

    panels_out = call(
        panels_kernel,
        "panels_out",
        [HBM],
        [((sz.rank, sz.span), bf16, VMEM)] * sz.side,
        (jnp.swapaxes(down, 1, 2),),
        (pltpu.SemaphoreType.DMA((sz.side,)),),
        FIRST,
    )
    panels = []
    for m in range(sz.side):
        pairs = [
            (h * 2 + c, (c * sz.side + ((h % sz.side) ^ m)) * 2 + h // sz.side)
            for h in range(sz.seq)
            for c in range(2)
        ]
        panels.append(lax.ppermute(panels_out[m], ("seq", "owner"), pairs))
    x, _ = lax.optimization_barrier((x, panels_out[0]))
    rows_out = call(
        norm_kernel,
        "norm_rows",
        [HBM] * 5,
        [(spread, bf16, VMEM)] * sz.seq,
        (x, gain, queries, keys, up),
        (
            pltpu.VMEM((sz.rows_half, sz.width), bf16),
            pltpu.VMEM((1, sz.width), f32),
            pltpu.VMEM(queries.shape, bf16),
            pltpu.VMEM(keys.shape, bf16),
            pltpu.VMEM(up.shape, bf16),
            pltpu.VMEM((sz.rows_half, sz.width), bf16),
            pltpu.SemaphoreType.DMA((5,)),
        ),
        FIRST,
    )
    rows_in = [rows_out[0]] + [swap(rows_out[k], "seq", k) for k in around]

    (table,) = call(
        table_kernel,
        "table",
        [SMEM] * 4,
        [((4, sz.requests), jnp.int32, SMEM)],
        (lengths, adapters, ranks, slots),
    )
    (matrix,) = call(
        matrix_kernel,
        "matrix_rows",
        [HBM, ANY],
        [((sz.span, half_columns), bf16, VMEM)],
        (base, swap(base, "owner", 1)),
        (pltpu.SemaphoreType.DMA((2,)),),
    )

    panels, rows_out = lax.optimization_barrier((panels, rows_out))
    panels = panels + [swap(p, "groups", k) for k in range(1, sz.groups) for p in panels]
    panels = panels + [swap(p, "owner", 1) for p in panels]
    rows_in, table, matrix, panels = lax.optimization_barrier((rows_in, table, matrix, panels))
    (own,) = call(
        gather_kernel,
        "gather_rows",
        [VMEM] * sz.seq,
        [((sz.seq * sz.rows_half, sz.span), bf16, VMEM)],
        rows_in,
    )
    other = swap(own, "owner", 1)
    (softmax,) = call(
        softmax_kernel,
        "softmax_rows",
        [SMEM] + [VMEM] * sz.seq,
        [((sz.group_size, sz.tokens, sz.tokens), bf16, VMEM)],
        (table, *rows_in),
        (
            pltpu.VMEM((sz.group_size, sz.tokens, HEAD_SIZE), bf16),
            pltpu.VMEM((sz.tokens, HEAD_SIZE), bf16),
        ),
    )

    partial_shape = (sz.tokens + sz.tokens // 2, HEAD_SIZE)
    partial_out = call(
        project_kernel,
        "project",
        [SMEM] + [VMEM] * (3 + len(panels)),
        [(partial_shape, bf16, VMEM)] * sz.seq,
        (table, matrix, own, other, *panels),
        (
            pltpu.VMEM((sz.tokens, sz.span), bf16),
            pltpu.VMEM((len(panels) * sz.rank, sz.span), bf16),
            pltpu.VMEM((sz.tokens, half_columns), bf16),
        ),
    )
    partial_in = [partial_out[0]] + [swap(partial_out[k], "seq", k) for k in around]
    wide = sz.group_size * HEAD_SIZE
    mixed = call(
        mix_kernel,
        "mix_values",
        [SMEM] + [VMEM] * (1 + 2 * sz.seq),
        [((sz.rows, wide), bf16, VMEM)] * sz.seq,
        (table, softmax, *rows_in, *partial_in),
        (
            pltpu.VMEM((sz.tokens, sz.requests * sz.rank), bf16),
            pltpu.VMEM((sz.seq * sz.slots_here * sz.rank, HEAD_SIZE), bf16),
            pltpu.VMEM((sz.requests * sz.rank, HEAD_SIZE), bf16),
            pltpu.VMEM((sz.tokens, wide), bf16),
        ),
    )
    mixed_in = [mixed[0]] + [swap(mixed[k], "seq", k) for k in around]
    (result,) = call(
        place_kernel,
        "place_heads",
        [VMEM] * sz.seq,
        [((sz.rows, sz.seq * wide), bf16, VMEM)],
        mixed_in,
    )
    return result


def broadcast(x, axis, root):
    mine = lax.axis_index(axis) == root
    return lax.psum(jnp.where(mine, x, jnp.zeros_like(x)), axis)


def from_behind(value, axis, steps):
    count = lax.axis_size(axis)
    first, last = (max(0, -steps), min(count, count - steps))
    return lax.ppermute(value, axis, [(source, source + steps) for source in range(first, last)])


def by_tokens(
    layer_input_rows,
    encoded_query_rows,
    encoded_key_rows,
    layer_norm_gain,
    base_value_matrix,
    adapter_down_panels,
    adapter_up_panels,
    request_token_lengths,
    adapter_per_request,
    rank_per_adapter,
    slot_per_adapter,
):
    hidden = layer_input_rows[0]
    row_count = hidden.shape[0]
    seq_now = lax.axis_index("seq")
    owner_now = lax.axis_index("owner")
    reach_count = min(WINDOW // row_count, lax.axis_size("seq") - 1)
    requests = request_token_lengths.shape[0]
    library = slot_per_adapter.shape[0]
    slots_here = adapter_down_panels.shape[1]
    rows_halved = adapter_down_panels.shape[2]
    rank_span_width = adapter_down_panels.shape[3]
    key_value_halved = adapter_up_panels.shape[3]
    group_size = HEADS // KEY_VALUE_HEADS
    request_ends = jnp.cumsum(request_token_lengths)
    position = seq_now * row_count + jnp.arange(row_count, dtype=jnp.int32)
    context = seq_now * row_count + jnp.arange(-reach_count * row_count, row_count, dtype=jnp.int32)
    request_lookup = jnp.sum((position[:, None] >= request_ends[None, :]).astype(jnp.int32), axis=1)
    request_ctx = jnp.sum((context[:, None] >= request_ends[None, :]).astype(jnp.int32), axis=1)
    live_mask = (context[None, :] <= position[:, None]) & (
        context[None, :] > position[:, None] - WINDOW
    )
    live_mask = (
        live_mask & (context[None, :] >= 0) & (request_ctx[None, :] == request_lookup[:, None])
    )
    choose = adapter_per_request[:, None] == jnp.arange(library, dtype=jnp.int32)[None, :]
    slot_of = jnp.sum(jnp.where(choose, slot_per_adapter[None, :], 0), axis=1)
    rank_lookup = jnp.sum(jnp.where(choose, rank_per_adapter[None, :], 0), axis=1)
    scale_lookup = adapter_strength / rank_lookup.astype(jnp.float32)
    in_request = request_lookup[:, None] == jnp.arange(requests, dtype=jnp.int32)[None, :]
    column_live = jnp.arange(rank_span_width, dtype=jnp.int32)[None, :] < rank_lookup[:, None]
    row_gain_weight = jnp.where(in_request, scale_lookup[None, :], jnp.float32(0.0))
    down_panel_here = adapter_down_panels[0]
    up_panel_here = adapter_up_panels[0]
    queries = encoded_query_rows[0]
    keys_own = encoded_key_rows[0]
    key_heads = keys_own.shape[1] // HEAD_SIZE
    wide_rows = hidden.astype(jnp.float32)
    normalized_rows = wide_rows * lax.rsqrt(
        jnp.mean(wide_rows * wide_rows, axis=1, keepdims=True) + norm_eps
    )
    normalized_rows = (normalized_rows * layer_norm_gain[0][None, :]).astype(jnp.bfloat16)
    normed_half = lax.dynamic_slice_in_dim(normalized_rows, owner_now * rows_halved, rows_halved, 1)
    full_value = jnp.dot(
        normalized_rows,
        lax.all_gather(base_value_matrix[0], ("seq", "owner"), axis=0, tiled=True),
        preferred_element_type=jnp.float32,
    )
    value_base_rows = lax.dynamic_slice_in_dim(
        full_value, owner_now * key_value_halved, key_value_halved, 1
    )

    def fetch_one(reduced_rows, request_index):
        owner_slot = slot_of[request_index]
        holder = owner_slot // slots_here
        local_slot = owner_slot % slots_here
        down_local = lax.dynamic_slice_in_dim(down_panel_here, local_slot, 1, 0)
        up_local = lax.dynamic_slice_in_dim(up_panel_here, local_slot, 1, 0)
        down_piece, up_piece = (
            broadcast(down_local, "seq", holder),
            broadcast(up_local, "seq", holder),
        )
        keep_mask = in_request[:, request_index][:, None] & column_live[request_index][None, :]
        matrix_product = jnp.dot(normed_half, down_piece[0], preferred_element_type=jnp.float32)
        return (reduced_rows + jnp.where(keep_mask, matrix_product, jnp.float32(0.0)), up_piece[0])

    start_low = jnp.zeros((row_count, rank_span_width), jnp.float32)
    reduced_rows, panels_up = lax.scan(fetch_one, start_low, jnp.arange(requests, dtype=jnp.int32))
    reduced_rows = lax.psum(reduced_rows, "owner").astype(jnp.bfloat16)
    raised_rows = jnp.einsum(
        "tr,qrk->qtk", reduced_rows, panels_up, preferred_element_type=jnp.float32
    )
    adapter_value = jnp.sum(row_gain_weight.T[:, :, None] * raised_rows, axis=0)
    value_output_rows = (value_base_rows + adapter_value).astype(jnp.bfloat16)
    key_parts = []
    value_parts = []
    for shift_by in range(reach_count, 0, -1):
        key_piece, value_piece = from_behind((keys_own, value_output_rows), "seq", shift_by)
        key_parts.append(key_piece)
        value_parts.append(value_piece)
    keys_all = jnp.concatenate(key_parts + [keys_own], axis=0)
    values_all = jnp.concatenate(value_parts + [value_output_rows], axis=0)
    query_view = queries.reshape(row_count, key_heads, group_size, HEAD_SIZE)
    key_view = keys_all.reshape(-1, key_heads, HEAD_SIZE)
    value_view = values_all.reshape(-1, key_heads, HEAD_SIZE)
    head_outputs = []
    for head_index in range(key_heads):
        query_head = query_view[:, head_index]
        scores = (
            jnp.einsum(
                "tcd,jd->ctj",
                query_head,
                key_view[:, head_index],
                preferred_element_type=jnp.float32,
            )
            * query_scale
        )
        scores = jnp.where(live_mask[None], scores, jnp.float32(-1e30))
        row_max = jnp.max(scores, axis=-1, keepdims=True)
        weights = jnp.exp(scores - row_max)
        row_total = jnp.sum(weights, axis=-1, keepdims=True)
        softmax_rows = (weights / row_total).astype(jnp.bfloat16)
        mixed = jnp.einsum(
            "ctj,jd->tcd",
            softmax_rows,
            value_view[:, head_index],
            preferred_element_type=jnp.float32,
        )
        head_outputs.append(mixed.astype(jnp.bfloat16).reshape(row_count, group_size * HEAD_SIZE))
    result = jnp.concatenate(head_outputs, axis=1)
    return result[None]


def per_device(
    layer_input_rows,
    encoded_query_rows,
    encoded_key_rows,
    layer_norm_gain,
    base_value_matrix,
    adapter_down_panels,
    adapter_up_panels,
    request_token_lengths,
    adapter_per_request,
    rank_per_adapter,
    slot_per_adapter,
):
    sz = Sizes(
        layer_input_rows[0],
        encoded_query_rows[0],
        adapter_down_panels[0],
        adapter_up_panels[0],
        request_token_lengths.shape[0],
    )
    scalars = (request_token_lengths, adapter_per_request, rank_per_adapter, slot_per_adapter)
    if not sz.fits():
        return by_tokens(
            layer_input_rows,
            encoded_query_rows,
            encoded_key_rows,
            layer_norm_gain,
            base_value_matrix,
            adapter_down_panels,
            adapter_up_panels,
            *scalars,
        )
    return by_heads(
        sz,
        layer_input_rows[0],
        encoded_query_rows[0],
        encoded_key_rows[0],
        layer_norm_gain,
        base_value_matrix[0],
        adapter_down_panels[0],
        adapter_up_panels[0],
        *scalars,
    )[None]


def solution(mesh):
    in_specs = (
        P("segment", ("groups", "seq"), None),
        P("segment", ("groups", "seq"), "owner"),
        P("segment", ("groups", "seq"), "owner"),
        P("segment", None),
        P("segment", ("seq", "owner"), None),
        P("segment", "seq", "owner", None),
        P("segment", "seq", None, "owner"),
        P("groups"),
        P("groups"),
        P(),
        P(),
    )
    out_specs = P("segment", ("groups", "seq"), "owner")
    return jax.shard_map(
        per_device, mesh=mesh, in_specs=in_specs, out_specs=out_specs, check_vma=False
    )
```

```python
import functools

import jax
import jax.numpy as jnp
from jax import lax
from jax.experimental import pallas as pl
from jax.experimental.pallas import tpu as pltpu
from jax.sharding import PartitionSpec as P

WINDOW = 1024
HEADS = 16
KEY_VALUE_HEADS = 8
HEAD_SIZE = 128
LANES = 128

query_scale = 168.0 ** (-0.5)
adapter_strength = 32.0
norm_eps = 1e-06

VMEM = pl.BlockSpec(memory_space=pltpu.VMEM)
SMEM = pl.BlockSpec(memory_space=pltpu.SMEM)
ANY = pl.BlockSpec(memory_space=pl.ANY)
HBM = pl.BlockSpec(memory_space=pltpu.HBM)
PARAMS = pltpu.CompilerParams(vmem_limit_bytes=16 * 1024 * 1024)
FIRST = pltpu.CompilerParams(vmem_limit_bytes=60 * 1024 * 1024)
bf16 = jnp.bfloat16
f32 = jnp.float32


def swap(value, axis, mask):
    return lax.ppermute(value, axis, [(i, i ^ mask) for i in range(lax.axis_size(axis))])


class Sizes:
    def __init__(self, x, queries, down, up, requests):
        self.seq = lax.axis_size("seq")
        self.groups = lax.axis_size("groups")
        self.rows = x.shape[0]
        self.rows_half = self.rows // 2
        self.width = x.shape[1]
        self.half = down.shape[1]
        self.side = self.seq // 2
        self.features = self.width // self.seq
        self.slots_here, self.rank = down.shape[0], down.shape[2]
        self.requests = requests
        self.heads_here = up.shape[2] // HEAD_SIZE
        self.group_size = HEADS // KEY_VALUE_HEADS
        self.tokens = self.rows * self.seq
        self.order = [0, 3, 2, 1]
        tiles = [
            -(-((i * self.features) % LANES + self.features) // LANES) for i in range(self.side)
        ]
        self.tiles = max(tiles)
        self.span = self.tiles * LANES

    def fits(self):
        return (
            lax.axis_size("owner") == 2
            and self.seq & (self.seq - 1) == 0
            and self.groups & (self.groups - 1) == 0
            and self.half % LANES == 0
            and self.half * 2 == self.width
            and self.heads_here == self.seq
            and self.slots_here == self.groups
            and self.features % 32 == 0
            and self.rows % 64 == 0
            and self.rank % self.rows_half == 0
            and self.pieces() * LANES <= self.span
            and 2 * self.rank == LANES
        )

    def pieces(self):
        return ((self.group_size + 1) * self.rows + self.slots_here * self.rank) // self.rows_half

    def start_in_half(self, i):
        return jnp.minimum((i * self.features) // LANES, self.half // LANES - self.tiles) * LANES

    def start(self, chip):
        return (chip // self.side) * self.half + self.start_in_half(chip % self.side)


def request_column(sz, table, position):
    found = jnp.zeros_like(position)
    for r in range(sz.requests):
        found = found + (position >= table[0, r]).astype(jnp.int32)
    return found


def table_kernel(sz, lengths, adapters, ranks, slots, piece, out, held, sem):
    here, core, group = (lax.axis_index(a) for a in ("seq", "owner", "groups"))
    copy = pltpu.make_async_copy(piece, held, sem)
    copy.start()
    end = jnp.int32(0)
    for r in range(sz.requests):
        end = end + lengths[r]
        adapter = adapters[r]
        slot = slots[adapter]
        chip, local = slot // sz.slots_here, slot % sz.slots_here
        other = jnp.where(chip // sz.side == core, 0, 1)
        m = (here % sz.side) ^ (chip % sz.side)
        out[0, r] = end
        out[1, r] = ranks[adapter]
        out[2, r] = (other * sz.groups + (local ^ group)) * sz.side + m
        out[3, r] = ((here ^ chip) * sz.slots_here + local) * sz.rank
    copy.wait()


def panels_kernel(sz, down, *outs_and_sem):
    outs, sem = outs_and_sem[:-1], outs_and_sem[-1]
    here, group = lax.axis_index("seq"), lax.axis_index("groups")
    copies = []
    for m, out in enumerate(outs):
        first = pl.multiple_of(sz.start_in_half((here % sz.side) ^ m), LANES)
        copies.append(
            pltpu.make_async_copy(down.at[group, :, pl.ds(first, sz.span)], out, sem.at[m])
        )
    for copy in copies:
        copy.start()
    for copy in copies:
        copy.wait()


def norm_kernel(sz, x, gain, queries, keys, up, *outs_and_scratch):
    outs, scratch = outs_and_scratch[: sz.seq], outs_and_scratch[sz.seq :]
    taken, gains, query, key, raised, whole, sem = scratch
    here, core = lax.axis_index("seq"), lax.axis_index("owner")
    place = pl.ds(pl.multiple_of(core * sz.rows_half, sz.rows_half), sz.rows_half)
    pairs = ((x.at[place], taken), (gain, gains), (queries, query), (keys, key), (up, raised))
    copies = [pltpu.make_async_copy(a, b, sem.at[i]) for i, (a, b) in enumerate(pairs)]
    for copy in copies:
        copy.start()
    for copy in copies[:2]:
        copy.wait()
    rows = taken[...].astype(f32)
    rows = rows * lax.rsqrt(jnp.mean(rows * rows, axis=1, keepdims=True) + norm_eps)
    whole[...] = (rows * gains[...]).astype(bf16)
    lane = lax.broadcasted_iota(jnp.int32, (sz.rows_half, sz.span), 1)
    for copy in copies[2:]:
        copy.wait()
    for k, out in enumerate(outs):
        head = here ^ k
        first = pl.multiple_of(sz.start(head), LANES)
        skip = head * sz.features - first
        piece = whole[:, pl.ds(first, sz.span)]
        live = (lane >= skip) & (lane < skip + sz.features)
        out[: sz.rows_half] = jnp.where(live, piece.astype(f32), 0.0).astype(bf16)
        parts = []
        for c in range(sz.group_size):
            first = pl.multiple_of((head * sz.group_size + c) * HEAD_SIZE, HEAD_SIZE)
            parts.append(query[:, pl.ds(first, HEAD_SIZE)])
        first = pl.multiple_of(head * HEAD_SIZE, HEAD_SIZE)
        parts.append(key[:, pl.ds(first, HEAD_SIZE)])
        for j in range(sz.slots_here):
            parts.append(raised[j, :, pl.ds(first, HEAD_SIZE)])
        at = 0
        for part in parts:
            for top in range(0, part.shape[0], sz.rows_half):
                out[sz.rows_half :, at : at + HEAD_SIZE] = part[top : top + sz.rows_half]
                at += HEAD_SIZE
        if at < sz.span:
            out[sz.rows_half :, at:] = jnp.zeros((sz.rows_half, sz.span - at), bf16)


def unpack(sz, piece, out, part, first, size):
    for top in range(0, size, sz.rows_half):
        lanes = slice((part + top // sz.rows_half) * HEAD_SIZE, (part + top // sz.rows_half + 1) * HEAD_SIZE)
        place = pl.ds(pl.multiple_of(first + top, sz.rows_half), sz.rows_half)
        out[place, :] = piece[sz.rows_half :, lanes]


def softmax_kernel(sz, table, *refs):
    pieces, out = refs[: sz.seq], refs[sz.seq]
    query, key = refs[sz.seq + 1 :]
    here = lax.axis_index("seq")
    parts = sz.rows // sz.rows_half
    for k, piece in zip(sz.order, pieces):
        first = (here ^ k) * sz.rows
        for c in range(sz.group_size):
            unpack(sz, piece, query.at[c], c * parts, first, sz.rows)
        unpack(sz, piece, key, sz.group_size * parts, first, sz.rows)
    shape = (sz.tokens, sz.tokens)
    mine = lax.broadcasted_iota(jnp.int32, shape, 0)
    theirs = lax.broadcasted_iota(jnp.int32, shape, 1)
    live = (theirs <= mine) & (theirs > mine - WINDOW)
    live = live & (request_column(sz, table, mine) == request_column(sz, table, theirs))
    for c in range(sz.group_size):
        scores = lax.dot_general(
            query[c], key[...], (((1,), (1,)), ((), ())), preferred_element_type=f32
        )
        scores = jnp.where(live, scores * query_scale, -1e30)
        weights = jnp.exp(scores - jnp.max(scores, axis=1, keepdims=True))
        out[c] = (weights / jnp.sum(weights, axis=1, keepdims=True)).astype(bf16)


def matrix_kernel(sz, base, base_other, out, sem):
    here, core = lax.axis_index("seq"), lax.axis_index("owner")
    depth, wide = base.shape[0], out.shape[1]
    skip = here * sz.features - sz.start(here)
    spare = sz.span - sz.features
    out[0:spare] = jnp.zeros((spare, wide), bf16)
    out[sz.span - spare :] = jnp.zeros((spare, wide), bf16)
    columns = pl.ds(pl.multiple_of(core * wide, wide), wide)
    copies = []
    for j, (ref, owner) in enumerate(((base, core), (base_other, 1 - core))):
        place = pl.ds(pl.multiple_of(skip + owner * depth, 16), depth)
        copies.append(pltpu.make_async_copy(ref.at[:, columns], out.at[place], sem.at[j]))
        copies[-1].start()
    for copy in copies:
        copy.wait()


def gather_kernel(sz, *refs):
    pieces, out = refs[: sz.seq], refs[sz.seq]
    here = lax.axis_index("seq")
    for k, piece in zip(sz.order, pieces):
        first = pl.multiple_of((here ^ k) * sz.rows_half, sz.rows_half)
        out[pl.ds(first, sz.rows_half), :] = piece[: sz.rows_half]


def project_half(sz, table, matrix, rows, stacked, owner):
    values = jnp.dot(rows[...], matrix[...], preferred_element_type=f32)
    low = lax.dot_general(
        rows[...], stacked[...], (((1,), (1,)), ((), ())), preferred_element_type=f32
    )
    shape = (sz.seq * sz.rows_half, sz.rank)
    row = lax.broadcasted_iota(jnp.int32, shape, 0)
    position = row // sz.rows_half * sz.rows + owner * sz.rows_half + row % sz.rows_half
    request = request_column(sz, table, position)
    column = lax.broadcasted_iota(jnp.int32, shape, 1)
    panel_here = jnp.full(shape, -1)
    for r in range(sz.requests):
        panel_here = jnp.where((request == r) & (column < table[1, r]), table[2, r], panel_here)
    reduced = jnp.zeros(shape, f32)
    for p in range(stacked.shape[0] // sz.rank):
        reduced = jnp.where(panel_here == p, low[:, p * sz.rank : (p + 1) * sz.rank], reduced)
    return values.astype(bf16), reduced


def project_own_kernel(sz, table, matrix, own, *refs):
    panels, (stacked, values, low) = refs[:-3], refs[-3:]
    for p, panel in enumerate(panels):
        stacked[p * sz.rank : (p + 1) * sz.rank] = panel[...]
    values[...], low[...] = project_half(
        sz, table, matrix, own, stacked, lax.axis_index("owner")
    )


def project_other_kernel(sz, table, matrix, other, stacked, values_own, low_own, *refs):
    outs, (product, reduced) = refs[: sz.seq], refs[sz.seq :]
    here, core = lax.axis_index("seq"), lax.axis_index("owner")
    values_other, low_other = project_half(sz, table, matrix, other, stacked, 1 - core)
    pairs = ((values_own[...], low_own[...], core), (values_other, low_other, 1 - core))
    for values, low, owner in pairs:
        for chip in range(sz.seq):
            first = pl.multiple_of(chip * sz.rows + owner * sz.rows_half, sz.rows_half)
            taken = slice(chip * sz.rows_half, (chip + 1) * sz.rows_half)
            product[pl.ds(first, sz.rows_half), :] = values[taken]
            reduced[pl.ds(first, sz.rows_half), :] = low[taken]
    half = sz.tokens // 2
    packed = jnp.concatenate([reduced[:half], reduced[half:]], axis=1).astype(bf16)
    for k, out in enumerate(outs):
        first = pl.multiple_of((here ^ k) * HEAD_SIZE, HEAD_SIZE)
        out[: sz.tokens] = product[:, pl.ds(first, HEAD_SIZE)]
        out[sz.tokens :] = packed


def mix_kernel(sz, table, softmax, *refs):
    pieces, refs = refs[: sz.seq], refs[sz.seq :]
    partials, refs = refs[: sz.seq], refs[sz.seq :]
    outs, (wide, raise_all, raise_picked, mixed) = refs[: sz.seq], refs[sz.seq :]
    here = lax.axis_index("seq")
    parts = (sz.group_size + 1) * (sz.rows // sz.rows_half)
    for k, piece in zip(sz.order, pieces):
        size = sz.slots_here * sz.rank
        unpack(sz, piece, raise_all, parts, k * size, size)
    position = lax.broadcasted_iota(jnp.int32, (sz.tokens, sz.rank), 0)
    request = request_column(sz, table, position)
    position = lax.broadcasted_iota(jnp.int32, (sz.tokens, HEAD_SIZE), 0)
    request_wide = request_column(sz, table, position)
    rank_here = jnp.ones((sz.tokens, HEAD_SIZE), jnp.int32)
    low = sum(partial[sz.tokens :].astype(f32) for partial in partials)
    low = jnp.concatenate([low[:, : sz.rank], low[:, sz.rank :]], axis=0)
    for r in range(sz.requests):
        rank_here = jnp.where(request_wide == r, table[1, r], rank_here)
        own = slice(r * sz.rank, (r + 1) * sz.rank)
        raise_picked[own] = raise_all[pl.ds(pl.multiple_of(table[3, r], sz.rank), sz.rank), :]
        wide[:, own] = jnp.where(request == r, low, 0.0).astype(bf16)
    scale = adapter_strength / rank_here.astype(f32)
    raised = jnp.dot(wide[...], raise_picked[...], preferred_element_type=f32)
    base = sum(partial[: sz.tokens].astype(f32) for partial in partials)
    values = (base + scale * raised).astype(bf16)
    for c in range(sz.group_size):
        mixed[:, c * HEAD_SIZE : (c + 1) * HEAD_SIZE] = jnp.dot(
            softmax[c], values, preferred_element_type=f32
        ).astype(bf16)
    for k, out in enumerate(outs):
        chip = here ^ k
        out[...] = mixed[pl.ds(pl.multiple_of(chip * sz.rows, sz.rows), sz.rows), :]


def place_kernel(sz, *refs):
    pieces, out = refs[: sz.seq], refs[sz.seq]
    here = lax.axis_index("seq")
    wide = sz.group_size * HEAD_SIZE
    for k, piece in zip(sz.order, pieces):
        head = here ^ k
        out[:, pl.ds(pl.multiple_of(head * wide, wide), wide)] = piece[...]


def by_heads(sz, x, queries, keys, gain, base, down, up, lengths, adapters, ranks, slots):
    around = range(1, sz.seq)
    half_columns = base.shape[1] // 2

    def ordered(values):
        return [values[k] for k in sz.order]

    spread = (2 * sz.rows_half, sz.span)

    def call(kernel, name, ins, outs, args, scratch=(), params=PARAMS):
        return pl.pallas_call(
            functools.partial(kernel, sz),
            out_shape=[jax.ShapeDtypeStruct(shape, dtype) for shape, dtype, _ in outs],
            in_specs=ins,
            out_specs=[spec for _, _, spec in outs],
            scratch_shapes=list(scratch),
            compiler_params=params,
            name=name,
        )(*args)

    panels_out = call(
        panels_kernel,
        "panels_out",
        [HBM],
        [((sz.rank, sz.span), bf16, VMEM)] * sz.side,
        (jnp.swapaxes(down, 1, 2),),
        (pltpu.SemaphoreType.DMA((sz.side,)),),
    )
    panels = []
    for m in range(sz.side):
        pairs = [
            (h * 2 + c, (c * sz.side + ((h % sz.side) ^ m)) * 2 + h // sz.side)
            for h in range(sz.seq)
            for c in range(2)
        ]
        panels.append(lax.ppermute(panels_out[m], ("seq", "owner"), pairs))
    x, _ = lax.optimization_barrier((x, panels_out[0]))
    rows_out = call(
        norm_kernel,
        "norm_rows",
        [HBM] * 5,
        [(spread, bf16, VMEM)] * sz.seq,
        (x, gain, queries, keys, up),
        (
            pltpu.VMEM((sz.rows_half, sz.width), bf16),
            pltpu.VMEM((1, sz.width), f32),
            pltpu.VMEM(queries.shape, bf16),
            pltpu.VMEM(keys.shape, bf16),
            pltpu.VMEM(up.shape, bf16),
            pltpu.VMEM((sz.rows_half, sz.width), bf16),
            pltpu.SemaphoreType.DMA((5,)),
        ),
        FIRST,
    )
    table, held = call(
        table_kernel,
        "table",
        [SMEM] * 4 + [ANY],
        [((4, sz.requests), jnp.int32, SMEM), (spread, bf16, VMEM)],
        (lengths, adapters, ranks, slots, rows_out[0]),
        (pltpu.SemaphoreType.DMA,),
    )
    (matrix,) = call(
        matrix_kernel,
        "matrix_rows",
        [HBM, ANY],
        [((sz.span, half_columns), bf16, VMEM)],
        (base, swap(base, "owner", 1)),
        (pltpu.SemaphoreType.DMA((2,)),),
    )
    rows_in = [held] + [swap(rows_out[k], "seq", k) for k in around]

    panels[0], table, matrix, held = lax.optimization_barrier((panels[0], table, matrix, held))
    rows_ready = rows_out[0]
    for m in range(sz.side):
        panels[m], rows_ready = lax.optimization_barrier((panels[m], rows_ready))
    rows_in[0] = held
    panels = panels + [swap(p, "groups", k) for k in range(1, sz.groups) for p in panels]
    panels = panels + [swap(p, "owner", 1) for p in panels]
    rows_ordered, panels = lax.optimization_barrier(([rows_in[k] for k in [0, 1, 3, 2]], panels))
    rows_in = [rows_ordered[[0, 1, 3, 2].index(k)] for k in range(sz.seq)]
    (own,) = call(
        gather_kernel,
        "gather_rows",
        [VMEM] * sz.seq,
        [((sz.seq * sz.rows_half, sz.span), bf16, VMEM)],
        ordered(rows_in),
    )
    other = swap(own, "owner", 1)
    (softmax,) = call(
        softmax_kernel,
        "softmax_rows",
        [SMEM] + [VMEM] * sz.seq,
        [((sz.group_size, sz.tokens, sz.tokens), bf16, VMEM)],
        (table, *ordered(rows_in)),
        (
            pltpu.VMEM((sz.group_size, sz.tokens, HEAD_SIZE), bf16),
            pltpu.VMEM((sz.tokens, HEAD_SIZE), bf16),
        ),
    )

    partial_shape = (sz.tokens + sz.tokens // 2, HEAD_SIZE)
    rows_half_all = sz.seq * sz.rows_half
    stacked, values_own, low_own = call(
        project_own_kernel,
        "project_own",
        [SMEM] + [VMEM] * (2 + len(panels)),
        [
            ((len(panels) * sz.rank, sz.span), bf16, VMEM),
            ((rows_half_all, half_columns), bf16, VMEM),
            ((rows_half_all, sz.rank), f32, VMEM),
        ],
        (table, matrix, own, *panels),
    )
    partial_out = call(
        project_other_kernel,
        "project_other",
        [SMEM] + [VMEM] * 5,
        [(partial_shape, bf16, VMEM)] * sz.seq,
        (table, matrix, other, stacked, values_own, low_own),
        (pltpu.VMEM((sz.tokens, half_columns), bf16), pltpu.VMEM((sz.tokens, sz.rank), f32)),
    )
    partial_in = [partial_out[0]] + [swap(partial_out[k], "seq", k) for k in around]
    wide = sz.group_size * HEAD_SIZE
    mixed = call(
        mix_kernel,
        "mix_values",
        [SMEM] + [VMEM] * (1 + 2 * sz.seq),
        [((sz.rows, wide), bf16, VMEM)] * sz.seq,
        (table, softmax, *ordered(rows_in), *ordered(partial_in)),
        (
            pltpu.VMEM((sz.tokens, sz.requests * sz.rank), bf16),
            pltpu.VMEM((sz.seq * sz.slots_here * sz.rank, HEAD_SIZE), bf16),
            pltpu.VMEM((sz.requests * sz.rank, HEAD_SIZE), bf16),
            pltpu.VMEM((sz.tokens, wide), bf16),
        ),
    )
    mixed_in = [mixed[0]] + [swap(mixed[k], "seq", k) for k in around]
    (result,) = call(
        place_kernel,
        "place_heads",
        [VMEM] * sz.seq,
        [((sz.rows, sz.seq * wide), bf16, VMEM)],
        ordered(mixed_in),
    )
    return result


def broadcast(x, axis, root):
    mine = lax.axis_index(axis) == root
    return lax.psum(jnp.where(mine, x, jnp.zeros_like(x)), axis)


def from_behind(value, axis, steps):
    count = lax.axis_size(axis)
    first, last = (max(0, -steps), min(count, count - steps))
    return lax.ppermute(value, axis, [(source, source + steps) for source in range(first, last)])


def by_tokens(
    layer_input_rows,
    encoded_query_rows,
    encoded_key_rows,
    layer_norm_gain,
    base_value_matrix,
    adapter_down_panels,
    adapter_up_panels,
    request_token_lengths,
    adapter_per_request,
    rank_per_adapter,
    slot_per_adapter,
):
    hidden = layer_input_rows[0]
    row_count = hidden.shape[0]
    seq_now = lax.axis_index("seq")
    owner_now = lax.axis_index("owner")
    reach_count = min(WINDOW // row_count, lax.axis_size("seq") - 1)
    requests = request_token_lengths.shape[0]
    library = slot_per_adapter.shape[0]
    slots_here = adapter_down_panels.shape[1]
    rows_halved = adapter_down_panels.shape[2]
    rank_span_width = adapter_down_panels.shape[3]
    key_value_halved = adapter_up_panels.shape[3]
    group_size = HEADS // KEY_VALUE_HEADS
    request_ends = jnp.cumsum(request_token_lengths)
    position = seq_now * row_count + jnp.arange(row_count, dtype=jnp.int32)
    context = seq_now * row_count + jnp.arange(-reach_count * row_count, row_count, dtype=jnp.int32)
    request_lookup = jnp.sum((position[:, None] >= request_ends[None, :]).astype(jnp.int32), axis=1)
    request_ctx = jnp.sum((context[:, None] >= request_ends[None, :]).astype(jnp.int32), axis=1)
    live_mask = (context[None, :] <= position[:, None]) & (
        context[None, :] > position[:, None] - WINDOW
    )
    live_mask = (
        live_mask & (context[None, :] >= 0) & (request_ctx[None, :] == request_lookup[:, None])
    )
    choose = adapter_per_request[:, None] == jnp.arange(library, dtype=jnp.int32)[None, :]
    slot_of = jnp.sum(jnp.where(choose, slot_per_adapter[None, :], 0), axis=1)
    rank_lookup = jnp.sum(jnp.where(choose, rank_per_adapter[None, :], 0), axis=1)
    scale_lookup = adapter_strength / rank_lookup.astype(jnp.float32)
    in_request = request_lookup[:, None] == jnp.arange(requests, dtype=jnp.int32)[None, :]
    column_live = jnp.arange(rank_span_width, dtype=jnp.int32)[None, :] < rank_lookup[:, None]
    row_gain_weight = jnp.where(in_request, scale_lookup[None, :], jnp.float32(0.0))
    down_panel_here = adapter_down_panels[0]
    up_panel_here = adapter_up_panels[0]
    queries = encoded_query_rows[0]
    keys_own = encoded_key_rows[0]
    key_heads = keys_own.shape[1] // HEAD_SIZE
    wide_rows = hidden.astype(jnp.float32)
    normalized_rows = wide_rows * lax.rsqrt(
        jnp.mean(wide_rows * wide_rows, axis=1, keepdims=True) + norm_eps
    )
    normalized_rows = (normalized_rows * layer_norm_gain[0][None, :]).astype(jnp.bfloat16)
    normed_half = lax.dynamic_slice_in_dim(normalized_rows, owner_now * rows_halved, rows_halved, 1)
    full_value = jnp.dot(
        normalized_rows,
        lax.all_gather(base_value_matrix[0], ("seq", "owner"), axis=0, tiled=True),
        preferred_element_type=jnp.float32,
    )
    value_base_rows = lax.dynamic_slice_in_dim(
        full_value, owner_now * key_value_halved, key_value_halved, 1
    )

    def fetch_one(reduced_rows, request_index):
        owner_slot = slot_of[request_index]
        holder = owner_slot // slots_here
        local_slot = owner_slot % slots_here
        down_local = lax.dynamic_slice_in_dim(down_panel_here, local_slot, 1, 0)
        up_local = lax.dynamic_slice_in_dim(up_panel_here, local_slot, 1, 0)
        down_piece, up_piece = (
            broadcast(down_local, "seq", holder),
            broadcast(up_local, "seq", holder),
        )
        keep_mask = in_request[:, request_index][:, None] & column_live[request_index][None, :]
        matrix_product = jnp.dot(normed_half, down_piece[0], preferred_element_type=jnp.float32)
        return (reduced_rows + jnp.where(keep_mask, matrix_product, jnp.float32(0.0)), up_piece[0])

    start_low = jnp.zeros((row_count, rank_span_width), jnp.float32)
    reduced_rows, panels_up = lax.scan(fetch_one, start_low, jnp.arange(requests, dtype=jnp.int32))
    reduced_rows = lax.psum(reduced_rows, "owner").astype(jnp.bfloat16)
    raised_rows = jnp.einsum(
        "tr,qrk->qtk", reduced_rows, panels_up, preferred_element_type=jnp.float32
    )
    adapter_value = jnp.sum(row_gain_weight.T[:, :, None] * raised_rows, axis=0)
    value_output_rows = (value_base_rows + adapter_value).astype(jnp.bfloat16)
    key_parts = []
    value_parts = []
    for shift_by in range(reach_count, 0, -1):
        key_piece, value_piece = from_behind((keys_own, value_output_rows), "seq", shift_by)
        key_parts.append(key_piece)
        value_parts.append(value_piece)
    keys_all = jnp.concatenate(key_parts + [keys_own], axis=0)
    values_all = jnp.concatenate(value_parts + [value_output_rows], axis=0)
    query_view = queries.reshape(row_count, key_heads, group_size, HEAD_SIZE)
    key_view = keys_all.reshape(-1, key_heads, HEAD_SIZE)
    value_view = values_all.reshape(-1, key_heads, HEAD_SIZE)
    head_outputs = []
    for head_index in range(key_heads):
        query_head = query_view[:, head_index]
        scores = (
            jnp.einsum(
                "tcd,jd->ctj",
                query_head,
                key_view[:, head_index],
                preferred_element_type=jnp.float32,
            )
            * query_scale
        )
        scores = jnp.where(live_mask[None], scores, jnp.float32(-1e30))
        row_max = jnp.max(scores, axis=-1, keepdims=True)
        weights = jnp.exp(scores - row_max)
        row_total = jnp.sum(weights, axis=-1, keepdims=True)
        softmax_rows = (weights / row_total).astype(jnp.bfloat16)
        mixed = jnp.einsum(
            "ctj,jd->tcd",
            softmax_rows,
            value_view[:, head_index],
            preferred_element_type=jnp.float32,
        )
        head_outputs.append(mixed.astype(jnp.bfloat16).reshape(row_count, group_size * HEAD_SIZE))
    result = jnp.concatenate(head_outputs, axis=1)
    return result[None]


def per_device(
    layer_input_rows,
    encoded_query_rows,
    encoded_key_rows,
    layer_norm_gain,
    base_value_matrix,
    adapter_down_panels,
    adapter_up_panels,
    request_token_lengths,
    adapter_per_request,
    rank_per_adapter,
    slot_per_adapter,
):
    sz = Sizes(
        layer_input_rows[0],
        encoded_query_rows[0],
        adapter_down_panels[0],
        adapter_up_panels[0],
        request_token_lengths.shape[0],
    )
    scalars = (request_token_lengths, adapter_per_request, rank_per_adapter, slot_per_adapter)
    if not sz.fits():
        return by_tokens(
            layer_input_rows,
            encoded_query_rows,
            encoded_key_rows,
            layer_norm_gain,
            base_value_matrix,
            adapter_down_panels,
            adapter_up_panels,
            *scalars,
        )
    return by_heads(
        sz,
        layer_input_rows[0],
        encoded_query_rows[0],
        encoded_key_rows[0],
        layer_norm_gain,
        base_value_matrix[0],
        adapter_down_panels[0],
        adapter_up_panels[0],
        *scalars,
    )[None]


def solution(mesh):
    in_specs = (
        P("segment", ("groups", "seq"), None),
        P("segment", ("groups", "seq"), "owner"),
        P("segment", ("groups", "seq"), "owner"),
        P("segment", None),
        P("segment", ("seq", "owner"), None),
        P("segment", "seq", "owner", None),
        P("segment", "seq", None, "owner"),
        P("groups"),
        P("groups"),
        P(),
        P(),
    )
    out_specs = P("segment", ("groups", "seq"), "owner")
    return jax.shard_map(
        per_device, mesh=mesh, in_specs=in_specs, out_specs=out_specs, check_vma=False
    )
```

```python
import functools

import jax
import jax.numpy as jnp
from jax import lax
from jax.experimental import pallas as pl
from jax.experimental.pallas import tpu as pltpu
from jax.sharding import PartitionSpec as P

WINDOW = 1024
HEADS = 16
KEY_VALUE_HEADS = 8
HEAD_SIZE = 128
LANES = 128

query_scale = 168.0 ** (-0.5)
adapter_strength = 32.0
norm_eps = 1e-06

VMEM = pl.BlockSpec(memory_space=pltpu.VMEM)
SMEM = pl.BlockSpec(memory_space=pltpu.SMEM)
ANY = pl.BlockSpec(memory_space=pl.ANY)
HBM = pl.BlockSpec(memory_space=pltpu.HBM)
PARAMS = pltpu.CompilerParams(vmem_limit_bytes=16 * 1024 * 1024)
FIRST = pltpu.CompilerParams(vmem_limit_bytes=60 * 1024 * 1024)
bf16 = jnp.bfloat16
f32 = jnp.float32


def swap(value, axis, mask):
    return lax.ppermute(value, axis, [(i, i ^ mask) for i in range(lax.axis_size(axis))])


class Sizes:
    def __init__(self, x, queries, down, up, requests):
        self.seq = lax.axis_size("seq")
        self.groups = lax.axis_size("groups")
        self.rows = x.shape[0]
        self.rows_half = self.rows // 2
        self.width = x.shape[1]
        self.half = down.shape[1]
        self.side = self.seq // 2
        self.features = self.width // self.seq
        self.slots_here, self.rank = down.shape[0], down.shape[2]
        self.requests = requests
        self.slot_bits = self.slots_here.bit_length() - 1
        self.side_bits = self.side.bit_length() - 1
        self.heads_here = up.shape[2] // HEAD_SIZE
        self.group_size = HEADS // KEY_VALUE_HEADS
        self.tokens = self.rows * self.seq
        self.order = [0, 3, 2, 1]
        self.order_sum = [0, 2, 1, 3]
        self.order_out = [0, 2, 3, 1]
        tiles = [
            -(-((i * self.features) % LANES + self.features) // LANES) for i in range(self.side)
        ]
        self.tiles = max(tiles)
        self.span = self.tiles * LANES

    def fits(self):
        return (
            lax.axis_size("owner") == 2
            and self.seq & (self.seq - 1) == 0
            and self.groups & (self.groups - 1) == 0
            and self.half % LANES == 0
            and self.half * 2 == self.width
            and self.heads_here == self.seq
            and self.slots_here == self.groups
            and self.features % 32 == 0
            and self.rows % 64 == 0
            and self.rank % self.rows_half == 0
            and self.pieces() * LANES <= self.span
            and 2 * self.rank == LANES
            and self.seq * self.rows_half == LANES
        )

    def pieces(self):
        return ((self.group_size + 1) * self.rows + self.slots_here * self.rank) // self.rows_half

    def start_in_half(self, i):
        return jnp.minimum((i * self.features) // LANES, self.half // LANES - self.tiles) * LANES

    def start(self, chip):
        return (chip // self.side) * self.half + self.start_in_half(chip % self.side)


def request_column(sz, table, position):
    found = jnp.zeros_like(position)
    for r in range(sz.requests):
        found = found + (position >= table[0, r]).astype(jnp.int32)
    return found


def token_at(sz, place):
    count = sz.seq * sz.rows_half
    owner = (place >= count).astype(jnp.int32)
    place = place - owner * count
    return place // sz.rows_half * sz.rows + owner * sz.rows_half + place % sz.rows_half


def table_kernel(sz, lengths, adapters, ranks, slots, piece, out, held, sem):
    here, core, group = (lax.axis_index(a) for a in ("seq", "owner", "groups"))
    copy = pltpu.make_async_copy(piece, held, sem)
    copy.start()
    end = jnp.int32(0)
    for r in range(sz.requests):
        end = end + lengths[r]
        adapter = adapters[r]
        slot = slots[adapter]
        chip, local = slot >> sz.slot_bits, slot & (sz.slots_here - 1)
        other = (chip >> sz.side_bits) ^ core
        m = (here ^ chip) & (sz.side - 1)
        out[0, r] = end
        out[1, r] = ranks[adapter]
        out[2, r] = (((other << sz.slot_bits) | (local ^ group)) << sz.side_bits) | m
        out[3, r] = ((here ^ chip) * sz.slots_here + local) * sz.rank
    copy.wait()


def panels_kernel(sz, down, *outs_and_sem):
    outs, sem = outs_and_sem[:-1], outs_and_sem[-1]
    here = lax.axis_index("seq")
    copies = []
    for m, out in enumerate(outs):
        first = pl.multiple_of(sz.start_in_half((here % sz.side) ^ m), LANES)
        copies.append(
            pltpu.make_async_copy(down.at[0, :, pl.ds(first, sz.span)], out, sem.at[m])
        )
    for copy in copies:
        copy.start()
    for copy in copies:
        copy.wait()


def norm_kernel(sz, x, gain, queries, keys, up, *outs_and_scratch):
    outs, scratch = outs_and_scratch[: sz.seq], outs_and_scratch[sz.seq :]
    taken, gains, query, key, raised, whole, sem = scratch
    here, core = lax.axis_index("seq"), lax.axis_index("owner")
    place = pl.ds(pl.multiple_of(core * sz.rows_half, sz.rows_half), sz.rows_half)
    pairs = ((x.at[place], taken), (gain, gains), (queries, query), (keys, key), (up, raised))
    copies = [pltpu.make_async_copy(a, b, sem.at[i]) for i, (a, b) in enumerate(pairs)]
    for copy in copies:
        copy.start()
    for copy in copies[:2]:
        copy.wait()
    rows = taken[...].astype(f32)
    rows = rows * lax.rsqrt(jnp.mean(rows * rows, axis=1, keepdims=True) + norm_eps)
    whole[...] = (rows * gains[...]).astype(bf16)
    lane = lax.broadcasted_iota(jnp.int32, (sz.rows_half, sz.span), 1)
    for copy in copies[2:]:
        copy.wait()
    for k, out in enumerate(outs):
        head = here ^ k
        first = pl.multiple_of(sz.start(head), LANES)
        skip = head * sz.features - first
        piece = whole[:, pl.ds(first, sz.span)]
        live = (lane >= skip) & (lane < skip + sz.features)
        out[: sz.rows_half] = jnp.where(live, piece.astype(f32), 0.0).astype(bf16)
        parts = []
        for c in range(sz.group_size):
            first = pl.multiple_of((head * sz.group_size + c) * HEAD_SIZE, HEAD_SIZE)
            parts.append(query[:, pl.ds(first, HEAD_SIZE)])
        first = pl.multiple_of(head * HEAD_SIZE, HEAD_SIZE)
        parts.append(key[:, pl.ds(first, HEAD_SIZE)])
        for j in range(sz.slots_here):
            parts.append(raised[j, :, pl.ds(first, HEAD_SIZE)])
        at = 0
        for part in parts:
            for top in range(0, part.shape[0], sz.rows_half):
                out[sz.rows_half :, at : at + HEAD_SIZE] = part[top : top + sz.rows_half]
                at += HEAD_SIZE
        if at < sz.span:
            out[sz.rows_half :, at:] = jnp.zeros((sz.rows_half, sz.span - at), bf16)


def unpack(sz, piece, out, part, first, size):
    for top in range(0, size, sz.rows_half):
        lanes = slice((part + top // sz.rows_half) * HEAD_SIZE, (part + top // sz.rows_half + 1) * HEAD_SIZE)
        place = pl.ds(pl.multiple_of(first + top, sz.rows_half), sz.rows_half)
        out[place, :] = piece[sz.rows_half :, lanes]


def softmax_kernel(sz, table, *refs):
    pieces, (out, raise_picked, scale, query, key, raise_all) = refs[: sz.seq], refs[sz.seq :]
    here = lax.axis_index("seq")
    parts = sz.rows // sz.rows_half
    for k, piece in zip(sz.order, pieces):
        first = (here ^ k) * sz.rows
        for c in range(sz.group_size):
            unpack(sz, piece, query.at[c], c * parts, first, sz.rows)
        for owner in range(parts):
            place = sz.seq * owner * sz.rows_half + (here ^ k) * sz.rows_half
            unpack(sz, piece, key, sz.group_size * parts + owner, place, sz.rows_half)
        size = sz.slots_here * sz.rank
        unpack(sz, piece, raise_all, (sz.group_size + 1) * parts, k * size, size)
    shape = scale.shape
    request = request_column(sz, table, token_at(sz, lax.broadcasted_iota(jnp.int32, shape, 0)))
    rank_here = jnp.ones(shape, jnp.int32)
    for r in range(sz.requests):
        rank_here = jnp.where(request == r, table[1, r], rank_here)
        first = pl.multiple_of(table[3, r], sz.rank)
        raise_picked[r * sz.rank : (r + 1) * sz.rank] = raise_all[pl.ds(first, sz.rank), :]
    scale[...] = adapter_strength / rank_here.astype(f32)
    shape = (sz.tokens, sz.tokens)
    mine = lax.broadcasted_iota(jnp.int32, shape, 0)
    theirs = token_at(sz, lax.broadcasted_iota(jnp.int32, shape, 1))
    live = (theirs <= mine) & (theirs > mine - WINDOW)
    live = live & (request_column(sz, table, mine) == request_column(sz, table, theirs))
    for c in range(sz.group_size):
        scores = lax.dot_general(
            query[c], key[...], (((1,), (1,)), ((), ())), preferred_element_type=f32
        )
        scores = jnp.where(live, scores * query_scale, -1e30)
        weights = jnp.exp(scores - jnp.max(scores, axis=1, keepdims=True))
        out[c * sz.tokens : (c + 1) * sz.tokens] = (
            weights / jnp.sum(weights, axis=1, keepdims=True)
        ).astype(bf16)


def matrix_kernel(sz, base, base_other, out, sem):
    here, core = lax.axis_index("seq"), lax.axis_index("owner")
    depth, wide = base.shape[0], out.shape[1]
    skip = here * sz.features - sz.start(here)
    spare = sz.span - sz.features
    out[0:spare] = jnp.zeros((spare, wide), bf16)
    out[sz.span - spare :] = jnp.zeros((spare, wide), bf16)
    columns = pl.ds(pl.multiple_of(core * wide, wide), wide)
    copies = []
    for j, (ref, owner) in enumerate(((base, core), (base_other, 1 - core))):
        place = pl.ds(pl.multiple_of(skip + owner * depth, 16), depth)
        copies.append(pltpu.make_async_copy(ref.at[:, columns], out.at[place], sem.at[j]))
        copies[-1].start()
    for copy in copies:
        copy.wait()


def gather_kernel(sz, *refs):
    pieces, out = refs[: sz.seq], refs[sz.seq]
    here = lax.axis_index("seq")
    for k, piece in zip(sz.order, pieces):
        first = pl.multiple_of((here ^ k) * sz.rows_half, sz.rows_half)
        out[pl.ds(first, sz.rows_half), :] = piece[: sz.rows_half]


def project_half(sz, table, matrix, rows, picked, owner):
    values = jnp.dot(rows[...], matrix[...], preferred_element_type=f32)
    low = lax.dot_general(
        picked[...], rows[...], (((1,), (1,)), ((), ())), preferred_element_type=f32
    )
    shape = (sz.rank, sz.seq * sz.rows_half)
    place = lax.broadcasted_iota(jnp.int32, shape, 1) + owner * shape[1]
    request = request_column(sz, table, token_at(sz, place))
    rank = lax.broadcasted_iota(jnp.int32, shape, 0)
    reduced = jnp.zeros(shape, f32)
    for r in range(sz.requests):
        live = (request == r) & (rank < table[1, r])
        reduced = jnp.where(live, low[r * sz.rank : (r + 1) * sz.rank], reduced)
    return values.astype(bf16), reduced.astype(bf16)


def project_own_kernel(sz, table, matrix, own, *refs):
    panels, (picked, values, low, stacked) = refs[:-4], refs[-4:]
    for p, panel in enumerate(panels):
        stacked[p * sz.rank : (p + 1) * sz.rank] = panel[...]
    for r in range(sz.requests):
        first = pl.multiple_of(table[2, r] * sz.rank, sz.rank)
        picked[r * sz.rank : (r + 1) * sz.rank] = stacked[pl.ds(first, sz.rank), :]
    values[...], low[...] = project_half(
        sz, table, matrix, own, picked, lax.axis_index("owner")
    )


def project_other_kernel(sz, table, matrix, other, picked, values_own, low_own, *refs):
    outs, values_other = refs[: sz.seq], refs[sz.seq]
    here, core = lax.axis_index("seq"), lax.axis_index("owner")
    values_other[...], low_other = project_half(sz, table, matrix, other, picked, 1 - core)
    count = sz.seq * sz.rows_half
    for k, out in enumerate(outs):
        columns = pl.ds(pl.multiple_of((here ^ k) * HEAD_SIZE, HEAD_SIZE), HEAD_SIZE)
        for values, low, owner in (
            (values_own, low_own[...], core),
            (values_other, low_other, 1 - core),
        ):
            first = pl.multiple_of(owner * count, count)
            out[pl.ds(first, count), :] = values[:, columns]
            first = pl.multiple_of(sz.tokens + owner * sz.rank, sz.rank)
            out[pl.ds(first, sz.rank), :] = low


def mix_kernel(sz, table, softmax, raise_picked, scale, *refs):
    partials, refs = refs[: sz.seq], refs[sz.seq :]
    outs, (wide, mixed) = refs[: sz.seq], refs[sz.seq :]
    here = lax.axis_index("seq")
    count = sz.seq * sz.rows_half
    low = sum(partial[sz.tokens :].astype(f32) for partial in partials)
    shape = (sz.rank, count)
    for owner in range(2):
        place = lax.broadcasted_iota(jnp.int32, shape, 1) + owner * count
        request = request_column(sz, table, token_at(sz, place))
        own = low[owner * sz.rank : (owner + 1) * sz.rank]
        for r in range(sz.requests):
            wide[r * sz.rank : (r + 1) * sz.rank, owner * count : (owner + 1) * count] = jnp.where(
                request == r, own, 0.0
            ).astype(bf16)
    raised = lax.dot_general(
        wide[...], raise_picked[...], (((0,), (0,)), ((), ())), preferred_element_type=f32
    )
    base = sum(partial[: sz.tokens].astype(f32) for partial in partials)
    values = (base + scale[...] * raised).astype(bf16)
    mixed[...] = jnp.dot(softmax[...], values, preferred_element_type=f32).astype(bf16)
    for k, out in enumerate(outs):
        for c in range(sz.group_size):
            first = pl.multiple_of(c * sz.tokens + (here ^ k) * sz.rows, sz.rows)
            out[:, c * HEAD_SIZE : (c + 1) * HEAD_SIZE] = mixed[pl.ds(first, sz.rows), :]


def place_kernel(sz, *refs):
    pieces, out = refs[: sz.seq], refs[sz.seq]
    here = lax.axis_index("seq")
    wide = sz.group_size * HEAD_SIZE
    for k, piece in zip(sz.order_out, pieces):
        head = here ^ k
        out[:, pl.ds(pl.multiple_of(head * wide, wide), wide)] = piece[...]


def by_heads(sz, x, queries, keys, gain, base, down, up, lengths, adapters, ranks, slots):
    around = range(1, sz.seq)
    half_columns = base.shape[1] // 2

    def ordered(values):
        return [values[k] for k in sz.order]

    spread = (2 * sz.rows_half, sz.span)

    def call(kernel, name, ins, outs, args, scratch=(), params=PARAMS, cost=None):
        return pl.pallas_call(
            functools.partial(kernel, sz),
            out_shape=[jax.ShapeDtypeStruct(shape, dtype) for shape, dtype, _ in outs],
            in_specs=ins,
            out_specs=[spec for _, _, spec in outs],
            scratch_shapes=list(scratch),
            compiler_params=params,
            cost_estimate=cost,
            name=name,
        )(*args)

    panels_out = call(
        panels_kernel,
        "panels_out",
        [HBM],
        [((sz.rank, sz.span), bf16, VMEM)] * sz.side,
        (lax.dynamic_index_in_dim(jnp.swapaxes(down, 1, 2), lax.axis_index("groups"), 0, True),),
        (pltpu.SemaphoreType.DMA((sz.side,)),),
    )
    panels = []
    for m in range(sz.side):
        pairs = [
            (h * 2 + c, (c * sz.side + ((h % sz.side) ^ m)) * 2 + h // sz.side)
            for h in range(sz.seq)
            for c in range(2)
        ]
        panels.append(lax.ppermute(panels_out[m], ("seq", "owner"), pairs))
    x, _ = lax.optimization_barrier((x, panels_out[0]))
    rows_out = call(
        norm_kernel,
        "norm_rows",
        [HBM] * 5,
        [(spread, bf16, VMEM)] * sz.seq,
        (x, gain, queries, keys, up),
        (
            pltpu.VMEM((sz.rows_half, sz.width), bf16),
            pltpu.VMEM((1, sz.width), f32),
            pltpu.VMEM(queries.shape, bf16),
            pltpu.VMEM(keys.shape, bf16),
            pltpu.VMEM(up.shape, bf16),
            pltpu.VMEM((sz.rows_half, sz.width), bf16),
            pltpu.SemaphoreType.DMA((5,)),
        ),
        FIRST,
    )
    table, held = call(
        table_kernel,
        "table",
        [SMEM] * 4 + [ANY],
        [((4, sz.requests), jnp.int32, SMEM), (spread, bf16, VMEM)],
        (lengths, adapters, ranks, slots, rows_out[0]),
        (pltpu.SemaphoreType.DMA,),
        cost=pl.CostEstimate(flops=0, bytes_accessed=64 * 1024 * 1024, transcendentals=0),
    )
    (matrix,) = call(
        matrix_kernel,
        "matrix_rows",
        [HBM, ANY],
        [((sz.span, half_columns), bf16, VMEM)],
        (base, swap(base, "owner", 1)),
        (pltpu.SemaphoreType.DMA((2,)),),
    )
    rows_in = [held] + [swap(rows_out[k], "seq", k) for k in around]

    panels[0], table, matrix = lax.optimization_barrier((panels[0], table, matrix))
    panels[1], held = lax.optimization_barrier((panels[1], held))
    rows_in[0] = held
    panels = panels + [swap(p, "groups", k) for k in range(1, sz.groups) for p in panels]
    panels = panels + [swap(p, "owner", 1) for p in panels]
    rows_ordered, panels = lax.optimization_barrier(([rows_in[k] for k in [0, 1, 3, 2]], panels))
    rows_in = [rows_ordered[[0, 1, 3, 2].index(k)] for k in range(sz.seq)]
    (own,) = call(
        gather_kernel,
        "gather_rows",
        [VMEM] * sz.seq,
        [((sz.seq * sz.rows_half, sz.span), bf16, VMEM)],
        ordered(rows_in),
    )
    other = swap(own, "owner", 1)
    softmax, raise_picked, scale = call(
        softmax_kernel,
        "softmax_rows",
        [SMEM] + [VMEM] * sz.seq,
        [
            ((sz.group_size * sz.tokens, sz.tokens), bf16, VMEM),
            ((sz.requests * sz.rank, HEAD_SIZE), bf16, VMEM),
            ((sz.tokens, HEAD_SIZE), f32, VMEM),
        ],
        (table, *ordered(rows_in)),
        (
            pltpu.VMEM((sz.group_size, sz.tokens, HEAD_SIZE), bf16),
            pltpu.VMEM((sz.tokens, HEAD_SIZE), bf16),
            pltpu.VMEM((sz.seq * sz.slots_here * sz.rank, HEAD_SIZE), bf16),
        ),
    )

    count = sz.seq * sz.rows_half
    partial_shape = (sz.tokens + 2 * sz.rank, HEAD_SIZE)
    picked, values_own, low_own = call(
        project_own_kernel,
        "project_own",
        [SMEM] + [VMEM] * (2 + len(panels)),
        [
            ((sz.requests * sz.rank, sz.span), bf16, VMEM),
            ((count, half_columns), bf16, VMEM),
            ((sz.rank, count), bf16, VMEM),
        ],
        (table, matrix, own, *panels),
        (pltpu.VMEM((len(panels) * sz.rank, sz.span), bf16),),
    )
    partial_out = call(
        project_other_kernel,
        "project_other",
        [SMEM] + [VMEM] * 5,
        [(partial_shape, bf16, VMEM)] * sz.seq,
        (table, matrix, other, picked, values_own, low_own),
        (pltpu.VMEM((count, half_columns), bf16),),
    )
    partial_in = [partial_out[0]] + [swap(partial_out[k], "seq", k) for k in around]
    wide = sz.group_size * HEAD_SIZE
    mixed = call(
        mix_kernel,
        "mix_values",
        [SMEM] + [VMEM] * (3 + sz.seq),
        [((sz.rows, wide), bf16, VMEM)] * sz.seq,
        (table, softmax, raise_picked, scale, *[partial_in[k] for k in sz.order_sum]),
        (
            pltpu.VMEM((sz.requests * sz.rank, sz.tokens), bf16),
            pltpu.VMEM((sz.group_size * sz.tokens, HEAD_SIZE), bf16),
        ),
    )
    mixed_in = [mixed[0]] + [swap(mixed[k], "seq", k) for k in around]
    (result,) = call(
        place_kernel,
        "place_heads",
        [VMEM] * sz.seq,
        [((sz.rows, sz.seq * wide), bf16, VMEM)],
        [mixed_in[k] for k in sz.order_out],
    )
    return result


def broadcast(x, axis, root):
    mine = lax.axis_index(axis) == root
    return lax.psum(jnp.where(mine, x, jnp.zeros_like(x)), axis)


def from_behind(value, axis, steps):
    count = lax.axis_size(axis)
    first, last = (max(0, -steps), min(count, count - steps))
    return lax.ppermute(value, axis, [(source, source + steps) for source in range(first, last)])


def by_tokens(
    layer_input_rows,
    encoded_query_rows,
    encoded_key_rows,
    layer_norm_gain,
    base_value_matrix,
    adapter_down_panels,
    adapter_up_panels,
    request_token_lengths,
    adapter_per_request,
    rank_per_adapter,
    slot_per_adapter,
):
    hidden = layer_input_rows[0]
    row_count = hidden.shape[0]
    seq_now = lax.axis_index("seq")
    owner_now = lax.axis_index("owner")
    reach_count = min(WINDOW // row_count, lax.axis_size("seq") - 1)
    requests = request_token_lengths.shape[0]
    library = slot_per_adapter.shape[0]
    slots_here = adapter_down_panels.shape[1]
    rows_halved = adapter_down_panels.shape[2]
    rank_span_width = adapter_down_panels.shape[3]
    key_value_halved = adapter_up_panels.shape[3]
    group_size = HEADS // KEY_VALUE_HEADS
    request_ends = jnp.cumsum(request_token_lengths)
    position = seq_now * row_count + jnp.arange(row_count, dtype=jnp.int32)
    context = seq_now * row_count + jnp.arange(-reach_count * row_count, row_count, dtype=jnp.int32)
    request_lookup = jnp.sum((position[:, None] >= request_ends[None, :]).astype(jnp.int32), axis=1)
    request_ctx = jnp.sum((context[:, None] >= request_ends[None, :]).astype(jnp.int32), axis=1)
    live_mask = (context[None, :] <= position[:, None]) & (
        context[None, :] > position[:, None] - WINDOW
    )
    live_mask = (
        live_mask & (context[None, :] >= 0) & (request_ctx[None, :] == request_lookup[:, None])
    )
    choose = adapter_per_request[:, None] == jnp.arange(library, dtype=jnp.int32)[None, :]
    slot_of = jnp.sum(jnp.where(choose, slot_per_adapter[None, :], 0), axis=1)
    rank_lookup = jnp.sum(jnp.where(choose, rank_per_adapter[None, :], 0), axis=1)
    scale_lookup = adapter_strength / rank_lookup.astype(jnp.float32)
    in_request = request_lookup[:, None] == jnp.arange(requests, dtype=jnp.int32)[None, :]
    column_live = jnp.arange(rank_span_width, dtype=jnp.int32)[None, :] < rank_lookup[:, None]
    row_gain_weight = jnp.where(in_request, scale_lookup[None, :], jnp.float32(0.0))
    down_panel_here = adapter_down_panels[0]
    up_panel_here = adapter_up_panels[0]
    queries = encoded_query_rows[0]
    keys_own = encoded_key_rows[0]
    key_heads = keys_own.shape[1] // HEAD_SIZE
    wide_rows = hidden.astype(jnp.float32)
    normalized_rows = wide_rows * lax.rsqrt(
        jnp.mean(wide_rows * wide_rows, axis=1, keepdims=True) + norm_eps
    )
    normalized_rows = (normalized_rows * layer_norm_gain[0][None, :]).astype(jnp.bfloat16)
    normed_half = lax.dynamic_slice_in_dim(normalized_rows, owner_now * rows_halved, rows_halved, 1)
    full_value = jnp.dot(
        normalized_rows,
        lax.all_gather(base_value_matrix[0], ("seq", "owner"), axis=0, tiled=True),
        preferred_element_type=jnp.float32,
    )
    value_base_rows = lax.dynamic_slice_in_dim(
        full_value, owner_now * key_value_halved, key_value_halved, 1
    )

    def fetch_one(reduced_rows, request_index):
        owner_slot = slot_of[request_index]
        holder = owner_slot // slots_here
        local_slot = owner_slot % slots_here
        down_local = lax.dynamic_slice_in_dim(down_panel_here, local_slot, 1, 0)
        up_local = lax.dynamic_slice_in_dim(up_panel_here, local_slot, 1, 0)
        down_piece, up_piece = (
            broadcast(down_local, "seq", holder),
            broadcast(up_local, "seq", holder),
        )
        keep_mask = in_request[:, request_index][:, None] & column_live[request_index][None, :]
        matrix_product = jnp.dot(normed_half, down_piece[0], preferred_element_type=jnp.float32)
        return (reduced_rows + jnp.where(keep_mask, matrix_product, jnp.float32(0.0)), up_piece[0])

    start_low = jnp.zeros((row_count, rank_span_width), jnp.float32)
    reduced_rows, panels_up = lax.scan(fetch_one, start_low, jnp.arange(requests, dtype=jnp.int32))
    reduced_rows = lax.psum(reduced_rows, "owner").astype(jnp.bfloat16)
    raised_rows = jnp.einsum(
        "tr,qrk->qtk", reduced_rows, panels_up, preferred_element_type=jnp.float32
    )
    adapter_value = jnp.sum(row_gain_weight.T[:, :, None] * raised_rows, axis=0)
    value_output_rows = (value_base_rows + adapter_value).astype(jnp.bfloat16)
    key_parts = []
    value_parts = []
    for shift_by in range(reach_count, 0, -1):
        key_piece, value_piece = from_behind((keys_own, value_output_rows), "seq", shift_by)
        key_parts.append(key_piece)
        value_parts.append(value_piece)
    keys_all = jnp.concatenate(key_parts + [keys_own], axis=0)
    values_all = jnp.concatenate(value_parts + [value_output_rows], axis=0)
    query_view = queries.reshape(row_count, key_heads, group_size, HEAD_SIZE)
    key_view = keys_all.reshape(-1, key_heads, HEAD_SIZE)
    value_view = values_all.reshape(-1, key_heads, HEAD_SIZE)
    head_outputs = []
    for head_index in range(key_heads):
        query_head = query_view[:, head_index]
        scores = (
            jnp.einsum(
                "tcd,jd->ctj",
                query_head,
                key_view[:, head_index],
                preferred_element_type=jnp.float32,
            )
            * query_scale
        )
        scores = jnp.where(live_mask[None], scores, jnp.float32(-1e30))
        row_max = jnp.max(scores, axis=-1, keepdims=True)
        weights = jnp.exp(scores - row_max)
        row_total = jnp.sum(weights, axis=-1, keepdims=True)
        softmax_rows = (weights / row_total).astype(jnp.bfloat16)
        mixed = jnp.einsum(
            "ctj,jd->tcd",
            softmax_rows,
            value_view[:, head_index],
            preferred_element_type=jnp.float32,
        )
        head_outputs.append(mixed.astype(jnp.bfloat16).reshape(row_count, group_size * HEAD_SIZE))
    result = jnp.concatenate(head_outputs, axis=1)
    return result[None]


def per_device(
    layer_input_rows,
    encoded_query_rows,
    encoded_key_rows,
    layer_norm_gain,
    base_value_matrix,
    adapter_down_panels,
    adapter_up_panels,
    request_token_lengths,
    adapter_per_request,
    rank_per_adapter,
    slot_per_adapter,
):
    sz = Sizes(
        layer_input_rows[0],
        encoded_query_rows[0],
        adapter_down_panels[0],
        adapter_up_panels[0],
        request_token_lengths.shape[0],
    )
    scalars = (request_token_lengths, adapter_per_request, rank_per_adapter, slot_per_adapter)
    if not sz.fits():
        return by_tokens(
            layer_input_rows,
            encoded_query_rows,
            encoded_key_rows,
            layer_norm_gain,
            base_value_matrix,
            adapter_down_panels,
            adapter_up_panels,
            *scalars,
        )
    return by_heads(
        sz,
        layer_input_rows[0],
        encoded_query_rows[0],
        encoded_key_rows[0],
        layer_norm_gain,
        base_value_matrix[0],
        adapter_down_panels[0],
        adapter_up_panels[0],
        *scalars,
    )[None]


def solution(mesh):
    in_specs = (
        P("segment", ("groups", "seq"), None),
        P("segment", ("groups", "seq"), "owner"),
        P("segment", ("groups", "seq"), "owner"),
        P("segment", None),
        P("segment", ("seq", "owner"), None),
        P("segment", "seq", "owner", None),
        P("segment", "seq", None, "owner"),
        P("groups"),
        P("groups"),
        P(),
        P(),
    )
    out_specs = P("segment", ("groups", "seq"), "owner")
    return jax.shard_map(
        per_device, mesh=mesh, in_specs=in_specs, out_specs=out_specs, check_vma=False
    )
```

```python
import functools

import jax
import jax.numpy as jnp
from jax import lax
from jax.experimental import pallas as pl
from jax.experimental.pallas import tpu as pltpu
from jax.sharding import PartitionSpec as P

WINDOW = 1024
HEADS = 16
KEY_VALUE_HEADS = 8
HEAD_SIZE = 128
LANES = 128

query_scale = 168.0 ** (-0.5)
adapter_strength = 32.0
norm_eps = 1e-06

VMEM = pl.BlockSpec(memory_space=pltpu.VMEM)
SMEM = pl.BlockSpec(memory_space=pltpu.SMEM)
ANY = pl.BlockSpec(memory_space=pl.ANY)
HBM = pl.BlockSpec(memory_space=pltpu.HBM)
PARAMS = pltpu.CompilerParams(vmem_limit_bytes=16 * 1024 * 1024)
FIRST = pltpu.CompilerParams(vmem_limit_bytes=60 * 1024 * 1024)
bf16 = jnp.bfloat16
f32 = jnp.float32


def swap(value, axis, mask):
    return lax.ppermute(value, axis, [(i, i ^ mask) for i in range(lax.axis_size(axis))])


class Sizes:
    def __init__(self, x, queries, down, up, requests):
        self.seq = lax.axis_size("seq")
        self.groups = lax.axis_size("groups")
        self.rows = x.shape[0]
        self.rows_half = self.rows // 2
        self.width = x.shape[1]
        self.half = down.shape[1]
        self.side = self.seq // 2
        self.features = self.width // self.seq
        self.slots_here, self.rank = down.shape[0], down.shape[2]
        self.requests = requests
        self.slot_bits = self.slots_here.bit_length() - 1
        self.side_bits = self.side.bit_length() - 1
        self.heads_here = up.shape[2] // HEAD_SIZE
        self.group_size = HEADS // KEY_VALUE_HEADS
        self.tokens = self.rows * self.seq
        rest = list(range(1, self.seq))
        self.order = [0] + rest[::-1]
        self.order_rows = [0] + rest[:1] + rest[:0:-1]
        self.order_sum = [0] + rest[1:2] + rest[:1] + rest[2:]
        tiles = [
            -(-((i * self.features) % LANES + self.features) // LANES) for i in range(self.side)
        ]
        self.tiles = max(tiles)
        self.span = self.tiles * LANES

    def fits(self):
        return (
            lax.axis_size("owner") == 2
            and self.seq & (self.seq - 1) == 0
            and self.groups & (self.groups - 1) == 0
            and self.half % LANES == 0
            and self.half * 2 == self.width
            and self.heads_here == self.seq
            and self.slots_here == self.groups
            and self.features % 32 == 0
            and self.rows % 64 == 0
            and self.rank % self.rows_half == 0
            and self.pieces() * LANES <= self.span
            and 2 * self.rank == LANES
            and self.seq * self.rows_half == LANES
        )

    def pieces(self):
        return ((self.group_size + 1) * self.rows + self.slots_here * self.rank) // self.rows_half

    def start_in_half(self, i):
        return jnp.minimum((i * self.features) // LANES, self.half // LANES - self.tiles) * LANES

    def start(self, chip):
        return (chip // self.side) * self.half + self.start_in_half(chip % self.side)


def request_column(sz, table, position):
    found = jnp.zeros_like(position)
    for r in range(sz.requests):
        found = found + (position >= table[0, r]).astype(jnp.int32)
    return found


def token_at(sz, place):
    count = sz.seq * sz.rows_half
    owner = (place >= count).astype(jnp.int32)
    place = place - owner * count
    return place // sz.rows_half * sz.rows + owner * sz.rows_half + place % sz.rows_half


def table_kernel(sz, lengths, adapters, ranks, slots, piece, out, held, sem):
    here, core, group = (lax.axis_index(a) for a in ("seq", "owner", "groups"))
    copy = pltpu.make_async_copy(piece, held, sem)
    copy.start()
    end = jnp.int32(0)
    for r in range(sz.requests):
        end = end + lengths[r]
        adapter = adapters[r]
        slot = slots[adapter]
        chip, local = slot >> sz.slot_bits, slot & (sz.slots_here - 1)
        other = (chip >> sz.side_bits) ^ core
        m = (here ^ chip) & (sz.side - 1)
        out[0, r] = end
        out[1, r] = ranks[adapter]
        out[2, r] = (((other << sz.slot_bits) | (local ^ group)) << sz.side_bits) | m
        out[3, r] = ((here ^ chip) * sz.slots_here + local) * sz.rank
    copy.wait()


def panels_kernel(sz, down, *outs_and_sem):
    outs, sem = outs_and_sem[:-1], outs_and_sem[-1]
    here = lax.axis_index("seq")
    copies = []
    for m, out in enumerate(outs):
        first = pl.multiple_of(sz.start_in_half((here % sz.side) ^ m), LANES)
        copies.append(
            pltpu.make_async_copy(down.at[0, :, pl.ds(first, sz.span)], out, sem.at[m])
        )
    for copy in copies:
        copy.start()
    for copy in copies:
        copy.wait()


def norm_kernel(sz, x, gain, queries, keys, up, *outs_and_scratch):
    outs, scratch = outs_and_scratch[: sz.seq], outs_and_scratch[sz.seq :]
    taken, gains, query, key, raised, whole, sem = scratch
    here, core = lax.axis_index("seq"), lax.axis_index("owner")
    place = pl.ds(pl.multiple_of(core * sz.rows_half, sz.rows_half), sz.rows_half)
    pairs = ((x.at[place], taken), (gain, gains), (queries, query), (keys, key), (up, raised))
    copies = [pltpu.make_async_copy(a, b, sem.at[i]) for i, (a, b) in enumerate(pairs)]
    for copy in copies:
        copy.start()
    for copy in copies[:2]:
        copy.wait()
    rows = taken[...].astype(f32)
    rows = rows * lax.rsqrt(jnp.mean(rows * rows, axis=1, keepdims=True) + norm_eps)
    whole[...] = (rows * gains[...]).astype(bf16)
    lane = lax.broadcasted_iota(jnp.int32, (sz.rows_half, sz.span), 1)
    for copy in copies[2:]:
        copy.wait()
    for k, out in enumerate(outs):
        head = here ^ k
        first = pl.multiple_of(sz.start(head), LANES)
        skip = head * sz.features - first
        piece = whole[:, pl.ds(first, sz.span)]
        live = (lane >= skip) & (lane < skip + sz.features)
        out[: sz.rows_half] = jnp.where(live, piece.astype(f32), 0.0).astype(bf16)
        parts = []
        for c in range(sz.group_size):
            first = pl.multiple_of((head * sz.group_size + c) * HEAD_SIZE, HEAD_SIZE)
            parts.append(query[:, pl.ds(first, HEAD_SIZE)])
        first = pl.multiple_of(head * HEAD_SIZE, HEAD_SIZE)
        parts.append(key[:, pl.ds(first, HEAD_SIZE)])
        for j in range(sz.slots_here):
            parts.append(raised[j, :, pl.ds(first, HEAD_SIZE)])
        at = 0
        for part in parts:
            for top in range(0, part.shape[0], sz.rows_half):
                out[sz.rows_half :, at : at + HEAD_SIZE] = part[top : top + sz.rows_half]
                at += HEAD_SIZE
        if at < sz.span:
            out[sz.rows_half :, at:] = jnp.zeros((sz.rows_half, sz.span - at), bf16)


def unpack(sz, piece, out, part, first, size):
    for top in range(0, size, sz.rows_half):
        lanes = slice((part + top // sz.rows_half) * HEAD_SIZE, (part + top // sz.rows_half + 1) * HEAD_SIZE)
        place = pl.ds(pl.multiple_of(first + top, sz.rows_half), sz.rows_half)
        out[place, :] = piece[sz.rows_half :, lanes]


def softmax_kernel(sz, table, *refs):
    pieces, (out, raise_picked, scale, query, key, raise_all) = refs[: sz.seq], refs[sz.seq :]
    here = lax.axis_index("seq")
    parts = sz.rows // sz.rows_half
    for k, piece in zip(sz.order, pieces):
        first = (here ^ k) * sz.rows
        for c in range(sz.group_size):
            unpack(sz, piece, query.at[c], c * parts, first, sz.rows)
        for owner in range(parts):
            place = sz.seq * owner * sz.rows_half + (here ^ k) * sz.rows_half
            unpack(sz, piece, key, sz.group_size * parts + owner, place, sz.rows_half)
        size = sz.slots_here * sz.rank
        unpack(sz, piece, raise_all, (sz.group_size + 1) * parts, k * size, size)
    shape = scale.shape
    request = request_column(sz, table, token_at(sz, lax.broadcasted_iota(jnp.int32, shape, 0)))
    rank_here = jnp.ones(shape, jnp.int32)
    for r in range(sz.requests):
        rank_here = jnp.where(request == r, table[1, r], rank_here)
        first = pl.multiple_of(table[3, r], sz.rank)
        raise_picked[r * sz.rank : (r + 1) * sz.rank] = raise_all[pl.ds(first, sz.rank), :]
    scale[...] = adapter_strength / rank_here.astype(f32)
    shape = (sz.tokens, sz.tokens)
    mine = lax.broadcasted_iota(jnp.int32, shape, 0)
    theirs = token_at(sz, lax.broadcasted_iota(jnp.int32, shape, 1))
    live = (theirs <= mine) & (theirs > mine - WINDOW)
    live = live & (request_column(sz, table, mine) == request_column(sz, table, theirs))
    for c in range(sz.group_size):
        scores = lax.dot_general(
            query[c], key[...], (((1,), (1,)), ((), ())), preferred_element_type=f32
        )
        scores = jnp.where(live, scores * query_scale, -1e30)
        weights = jnp.exp(scores - jnp.max(scores, axis=1, keepdims=True))
        out[c * sz.tokens : (c + 1) * sz.tokens] = (
            weights / jnp.sum(weights, axis=1, keepdims=True)
        ).astype(bf16)


def matrix_kernel(sz, base, base_other, out, sem):
    here, core = lax.axis_index("seq"), lax.axis_index("owner")
    depth, wide = base.shape[0], out.shape[1]
    skip = here * sz.features - sz.start(here)
    spare = sz.span - sz.features
    out[0:spare] = jnp.zeros((spare, wide), bf16)
    out[sz.span - spare :] = jnp.zeros((spare, wide), bf16)
    columns = pl.ds(pl.multiple_of(core * wide, wide), wide)
    copies = []
    for j, (ref, owner) in enumerate(((base, core), (base_other, 1 - core))):
        place = pl.ds(pl.multiple_of(skip + owner * depth, 16), depth)
        copies.append(pltpu.make_async_copy(ref.at[:, columns], out.at[place], sem.at[j]))
        copies[-1].start()
    for copy in copies:
        copy.wait()


def gather_kernel(sz, *refs):
    pieces, out = refs[: sz.seq], refs[sz.seq]
    here = lax.axis_index("seq")
    for k, piece in zip(sz.order, pieces):
        first = pl.multiple_of((here ^ k) * sz.rows_half, sz.rows_half)
        out[pl.ds(first, sz.rows_half), :] = piece[: sz.rows_half]


def project_half(sz, table, matrix, rows, picked, owner):
    values = jnp.dot(rows[...], matrix[...], preferred_element_type=f32)
    low = lax.dot_general(
        picked[...], rows[...], (((1,), (1,)), ((), ())), preferred_element_type=f32
    )
    shape = (sz.rank, sz.seq * sz.rows_half)
    place = lax.broadcasted_iota(jnp.int32, shape, 1) + owner * shape[1]
    request = request_column(sz, table, token_at(sz, place))
    rank = lax.broadcasted_iota(jnp.int32, shape, 0)
    reduced = jnp.zeros(shape, f32)
    for r in range(sz.requests):
        live = (request == r) & (rank < table[1, r])
        reduced = jnp.where(live, low[r * sz.rank : (r + 1) * sz.rank], reduced)
    return values.astype(bf16), reduced.astype(bf16)


def project_own_kernel(sz, table, matrix, own, *refs):
    panels, (picked, values, low, stacked) = refs[:-4], refs[-4:]
    for p, panel in enumerate(panels):
        stacked[p * sz.rank : (p + 1) * sz.rank] = panel[...]
    for r in range(sz.requests):
        first = pl.multiple_of(table[2, r] * sz.rank, sz.rank)
        picked[r * sz.rank : (r + 1) * sz.rank] = stacked[pl.ds(first, sz.rank), :]
    values[...], low[...] = project_half(
        sz, table, matrix, own, picked, lax.axis_index("owner")
    )


def project_other_kernel(sz, table, matrix, other, picked, values_own, low_own, *refs):
    outs, values_other = refs[: sz.seq], refs[sz.seq]
    here, core = lax.axis_index("seq"), lax.axis_index("owner")
    values_other[...], low_other = project_half(sz, table, matrix, other, picked, 1 - core)
    count = sz.seq * sz.rows_half
    for k, out in enumerate(outs):
        columns = pl.ds(pl.multiple_of((here ^ k) * HEAD_SIZE, HEAD_SIZE), HEAD_SIZE)
        for values, low, owner in (
            (values_own, low_own[...], core),
            (values_other, low_other, 1 - core),
        ):
            first = pl.multiple_of(owner * count, count)
            out[pl.ds(first, count), :] = values[:, columns]
            first = pl.multiple_of(sz.tokens + owner * sz.rank, sz.rank)
            out[pl.ds(first, sz.rank), :] = low


def mix_kernel(sz, table, softmax, raise_picked, scale, *refs):
    partials, refs = refs[: sz.seq], refs[sz.seq :]
    outs, (wide, mixed) = refs[: sz.seq], refs[sz.seq :]
    here = lax.axis_index("seq")
    count = sz.seq * sz.rows_half
    low = sum(partial[sz.tokens :].astype(f32) for partial in partials)
    shape = (sz.rank, count)
    for owner in range(2):
        place = lax.broadcasted_iota(jnp.int32, shape, 1) + owner * count
        request = request_column(sz, table, token_at(sz, place))
        own = low[owner * sz.rank : (owner + 1) * sz.rank]
        for r in range(sz.requests):
            wide[r * sz.rank : (r + 1) * sz.rank, owner * count : (owner + 1) * count] = jnp.where(
                request == r, own, 0.0
            ).astype(bf16)
    raised = lax.dot_general(
        wide[...], raise_picked[...], (((0,), (0,)), ((), ())), preferred_element_type=f32
    )
    base = sum(partial[: sz.tokens].astype(f32) for partial in partials)
    values = (base + scale[...] * raised).astype(bf16)
    mixed[...] = jnp.dot(softmax[...], values, preferred_element_type=f32).astype(bf16)
    for k, out in enumerate(outs):
        for c in range(sz.group_size):
            first = pl.multiple_of(c * sz.tokens + (here ^ k) * sz.rows, sz.rows)
            out[:, c * HEAD_SIZE : (c + 1) * HEAD_SIZE] = mixed[pl.ds(first, sz.rows), :]


def place_kernel(sz, *refs):
    pieces, out = refs[: sz.seq], refs[sz.seq]
    here = lax.axis_index("seq")
    wide = sz.group_size * HEAD_SIZE
    for k, piece in zip(sz.order, pieces):
        head = here ^ k
        out[:, pl.ds(pl.multiple_of(head * wide, wide), wide)] = piece[...]


def by_heads(sz, x, queries, keys, gain, base, down, up, lengths, adapters, ranks, slots):
    around = range(1, sz.seq)
    half_columns = base.shape[1] // 2

    def ordered(values):
        return [values[k] for k in sz.order]

    spread = (2 * sz.rows_half, sz.span)

    def call(kernel, name, ins, outs, args, scratch=(), params=PARAMS, cost=None):
        return pl.pallas_call(
            functools.partial(kernel, sz),
            out_shape=[jax.ShapeDtypeStruct(shape, dtype) for shape, dtype, _ in outs],
            in_specs=ins,
            out_specs=[spec for _, _, spec in outs],
            scratch_shapes=list(scratch),
            compiler_params=params,
            cost_estimate=cost,
            name=name,
        )(*args)

    panels_out = call(
        panels_kernel,
        "panels_out",
        [HBM],
        [((sz.rank, sz.span), bf16, VMEM)] * sz.side,
        (lax.dynamic_index_in_dim(jnp.swapaxes(down, 1, 2), lax.axis_index("groups"), 0, True),),
        (pltpu.SemaphoreType.DMA((sz.side,)),),
    )
    panels = []
    for m in range(sz.side):
        pairs = [
            (h * 2 + c, (c * sz.side + ((h % sz.side) ^ m)) * 2 + h // sz.side)
            for h in range(sz.seq)
            for c in range(2)
        ]
        panels.append(lax.ppermute(panels_out[m], ("seq", "owner"), pairs))
    x, _ = lax.optimization_barrier((x, panels_out[0]))
    rows_out = call(
        norm_kernel,
        "norm_rows",
        [HBM] * 5,
        [(spread, bf16, VMEM)] * sz.seq,
        (x, gain, queries, keys, up),
        (
            pltpu.VMEM((sz.rows_half, sz.width), bf16),
            pltpu.VMEM((1, sz.width), f32),
            pltpu.VMEM(queries.shape, bf16),
            pltpu.VMEM(keys.shape, bf16),
            pltpu.VMEM(up.shape, bf16),
            pltpu.VMEM((sz.rows_half, sz.width), bf16),
            pltpu.SemaphoreType.DMA((5,)),
        ),
        FIRST,
    )
    table, held = call(
        table_kernel,
        "table",
        [SMEM] * 4 + [ANY],
        [((4, sz.requests), jnp.int32, SMEM), (spread, bf16, VMEM)],
        (lengths, adapters, ranks, slots, rows_out[0]),
        (pltpu.SemaphoreType.DMA,),
        cost=pl.CostEstimate(flops=0, bytes_accessed=64 * 1024 * 1024, transcendentals=0),
    )
    (matrix,) = call(
        matrix_kernel,
        "matrix_rows",
        [HBM, ANY],
        [((sz.span, half_columns), bf16, VMEM)],
        (base, swap(base, "owner", 1)),
        (pltpu.SemaphoreType.DMA((2,)),),
    )
    rows_in = [held] + [swap(rows_out[k], "seq", k) for k in around]

    panels[0], table, matrix = lax.optimization_barrier((panels[0], table, matrix))
    panels[1], held = lax.optimization_barrier((panels[1], held))
    rows_in[0] = held
    panels = panels + [swap(p, "groups", k) for k in range(1, sz.groups) for p in panels]
    panels = panels + [swap(p, "owner", 1) for p in panels]
    rows_ordered, panels = lax.optimization_barrier(([rows_in[k] for k in sz.order_rows], panels))
    rows_in = [rows_ordered[sz.order_rows.index(k)] for k in range(sz.seq)]
    (own,) = call(
        gather_kernel,
        "gather_rows",
        [VMEM] * sz.seq,
        [((sz.seq * sz.rows_half, sz.span), bf16, VMEM)],
        ordered(rows_in),
    )
    other = swap(own, "owner", 1)
    softmax, raise_picked, scale = call(
        softmax_kernel,
        "softmax_rows",
        [SMEM] + [VMEM] * sz.seq,
        [
            ((sz.group_size * sz.tokens, sz.tokens), bf16, VMEM),
            ((sz.requests * sz.rank, HEAD_SIZE), bf16, VMEM),
            ((sz.tokens, HEAD_SIZE), f32, VMEM),
        ],
        (table, *ordered(rows_in)),
        (
            pltpu.VMEM((sz.group_size, sz.tokens, HEAD_SIZE), bf16),
            pltpu.VMEM((sz.tokens, HEAD_SIZE), bf16),
            pltpu.VMEM((sz.seq * sz.slots_here * sz.rank, HEAD_SIZE), bf16),
        ),
    )

    count = sz.seq * sz.rows_half
    partial_shape = (sz.tokens + 2 * sz.rank, HEAD_SIZE)
    picked, values_own, low_own = call(
        project_own_kernel,
        "project_own",
        [SMEM] + [VMEM] * (2 + len(panels)),
        [
            ((sz.requests * sz.rank, sz.span), bf16, VMEM),
            ((count, half_columns), bf16, VMEM),
            ((sz.rank, count), bf16, VMEM),
        ],
        (table, matrix, own, *panels),
        (pltpu.VMEM((len(panels) * sz.rank, sz.span), bf16),),
    )
    partial_out = call(
        project_other_kernel,
        "project_other",
        [SMEM] + [VMEM] * 5,
        [(partial_shape, bf16, VMEM)] * sz.seq,
        (table, matrix, other, picked, values_own, low_own),
        (pltpu.VMEM((count, half_columns), bf16),),
    )
    partial_in = [partial_out[0]] + [swap(partial_out[k], "seq", k) for k in around]
    wide = sz.group_size * HEAD_SIZE
    mixed = call(
        mix_kernel,
        "mix_values",
        [SMEM] + [VMEM] * (3 + sz.seq),
        [((sz.rows, wide), bf16, VMEM)] * sz.seq,
        (table, softmax, raise_picked, scale, *[partial_in[k] for k in sz.order_sum]),
        (
            pltpu.VMEM((sz.requests * sz.rank, sz.tokens), bf16),
            pltpu.VMEM((sz.group_size * sz.tokens, HEAD_SIZE), bf16),
        ),
    )
    mixed_in = [mixed[0]] + [swap(mixed[k], "seq", k) for k in around]
    (result,) = call(
        place_kernel,
        "place_heads",
        [VMEM] * sz.seq,
        [((sz.rows, sz.seq * wide), bf16, VMEM)],
        ordered(mixed_in),
    )
    return result


def broadcast(x, axis, root):
    mine = lax.axis_index(axis) == root
    return lax.psum(jnp.where(mine, x, jnp.zeros_like(x)), axis)


def from_behind(value, axis, steps):
    count = lax.axis_size(axis)
    first, last = (max(0, -steps), min(count, count - steps))
    return lax.ppermute(value, axis, [(source, source + steps) for source in range(first, last)])


def by_tokens(
    layer_input_rows,
    encoded_query_rows,
    encoded_key_rows,
    layer_norm_gain,
    base_value_matrix,
    adapter_down_panels,
    adapter_up_panels,
    request_token_lengths,
    adapter_per_request,
    rank_per_adapter,
    slot_per_adapter,
):
    hidden = layer_input_rows[0]
    row_count = hidden.shape[0]
    seq_now = lax.axis_index("seq")
    owner_now = lax.axis_index("owner")
    reach_count = min(WINDOW // row_count, lax.axis_size("seq") - 1)
    requests = request_token_lengths.shape[0]
    library = slot_per_adapter.shape[0]
    slots_here = adapter_down_panels.shape[1]
    rows_halved = adapter_down_panels.shape[2]
    rank_span_width = adapter_down_panels.shape[3]
    key_value_halved = adapter_up_panels.shape[3]
    group_size = HEADS // KEY_VALUE_HEADS
    request_ends = jnp.cumsum(request_token_lengths)
    position = seq_now * row_count + jnp.arange(row_count, dtype=jnp.int32)
    context = seq_now * row_count + jnp.arange(-reach_count * row_count, row_count, dtype=jnp.int32)
    request_lookup = jnp.sum((position[:, None] >= request_ends[None, :]).astype(jnp.int32), axis=1)
    request_ctx = jnp.sum((context[:, None] >= request_ends[None, :]).astype(jnp.int32), axis=1)
    live_mask = (context[None, :] <= position[:, None]) & (
        context[None, :] > position[:, None] - WINDOW
    )
    live_mask = (
        live_mask & (context[None, :] >= 0) & (request_ctx[None, :] == request_lookup[:, None])
    )
    choose = adapter_per_request[:, None] == jnp.arange(library, dtype=jnp.int32)[None, :]
    slot_of = jnp.sum(jnp.where(choose, slot_per_adapter[None, :], 0), axis=1)
    rank_lookup = jnp.sum(jnp.where(choose, rank_per_adapter[None, :], 0), axis=1)
    scale_lookup = adapter_strength / rank_lookup.astype(jnp.float32)
    in_request = request_lookup[:, None] == jnp.arange(requests, dtype=jnp.int32)[None, :]
    column_live = jnp.arange(rank_span_width, dtype=jnp.int32)[None, :] < rank_lookup[:, None]
    row_gain_weight = jnp.where(in_request, scale_lookup[None, :], jnp.float32(0.0))
    down_panel_here = adapter_down_panels[0]
    up_panel_here = adapter_up_panels[0]
    queries = encoded_query_rows[0]
    keys_own = encoded_key_rows[0]
    key_heads = keys_own.shape[1] // HEAD_SIZE
    wide_rows = hidden.astype(jnp.float32)
    normalized_rows = wide_rows * lax.rsqrt(
        jnp.mean(wide_rows * wide_rows, axis=1, keepdims=True) + norm_eps
    )
    normalized_rows = (normalized_rows * layer_norm_gain[0][None, :]).astype(jnp.bfloat16)
    normed_half = lax.dynamic_slice_in_dim(normalized_rows, owner_now * rows_halved, rows_halved, 1)
    full_value = jnp.dot(
        normalized_rows,
        lax.all_gather(base_value_matrix[0], ("seq", "owner"), axis=0, tiled=True),
        preferred_element_type=jnp.float32,
    )
    value_base_rows = lax.dynamic_slice_in_dim(
        full_value, owner_now * key_value_halved, key_value_halved, 1
    )

    def fetch_one(reduced_rows, request_index):
        owner_slot = slot_of[request_index]
        holder = owner_slot // slots_here
        local_slot = owner_slot % slots_here
        down_local = lax.dynamic_slice_in_dim(down_panel_here, local_slot, 1, 0)
        up_local = lax.dynamic_slice_in_dim(up_panel_here, local_slot, 1, 0)
        down_piece, up_piece = (
            broadcast(down_local, "seq", holder),
            broadcast(up_local, "seq", holder),
        )
        keep_mask = in_request[:, request_index][:, None] & column_live[request_index][None, :]
        matrix_product = jnp.dot(normed_half, down_piece[0], preferred_element_type=jnp.float32)
        return (reduced_rows + jnp.where(keep_mask, matrix_product, jnp.float32(0.0)), up_piece[0])

    start_low = jnp.zeros((row_count, rank_span_width), jnp.float32)
    reduced_rows, panels_up = lax.scan(fetch_one, start_low, jnp.arange(requests, dtype=jnp.int32))
    reduced_rows = lax.psum(reduced_rows, "owner").astype(jnp.bfloat16)
    raised_rows = jnp.einsum(
        "tr,qrk->qtk", reduced_rows, panels_up, preferred_element_type=jnp.float32
    )
    adapter_value = jnp.sum(row_gain_weight.T[:, :, None] * raised_rows, axis=0)
    value_output_rows = (value_base_rows + adapter_value).astype(jnp.bfloat16)
    key_parts = []
    value_parts = []
    for shift_by in range(reach_count, 0, -1):
        key_piece, value_piece = from_behind((keys_own, value_output_rows), "seq", shift_by)
        key_parts.append(key_piece)
        value_parts.append(value_piece)
    keys_all = jnp.concatenate(key_parts + [keys_own], axis=0)
    values_all = jnp.concatenate(value_parts + [value_output_rows], axis=0)
    query_view = queries.reshape(row_count, key_heads, group_size, HEAD_SIZE)
    key_view = keys_all.reshape(-1, key_heads, HEAD_SIZE)
    value_view = values_all.reshape(-1, key_heads, HEAD_SIZE)
    head_outputs = []
    for head_index in range(key_heads):
        query_head = query_view[:, head_index]
        scores = (
            jnp.einsum(
                "tcd,jd->ctj",
                query_head,
                key_view[:, head_index],
                preferred_element_type=jnp.float32,
            )
            * query_scale
        )
        scores = jnp.where(live_mask[None], scores, jnp.float32(-1e30))
        row_max = jnp.max(scores, axis=-1, keepdims=True)
        weights = jnp.exp(scores - row_max)
        row_total = jnp.sum(weights, axis=-1, keepdims=True)
        softmax_rows = (weights / row_total).astype(jnp.bfloat16)
        mixed = jnp.einsum(
            "ctj,jd->tcd",
            softmax_rows,
            value_view[:, head_index],
            preferred_element_type=jnp.float32,
        )
        head_outputs.append(mixed.astype(jnp.bfloat16).reshape(row_count, group_size * HEAD_SIZE))
    result = jnp.concatenate(head_outputs, axis=1)
    return result[None]


def per_device(
    layer_input_rows,
    encoded_query_rows,
    encoded_key_rows,
    layer_norm_gain,
    base_value_matrix,
    adapter_down_panels,
    adapter_up_panels,
    request_token_lengths,
    adapter_per_request,
    rank_per_adapter,
    slot_per_adapter,
):
    sz = Sizes(
        layer_input_rows[0],
        encoded_query_rows[0],
        adapter_down_panels[0],
        adapter_up_panels[0],
        request_token_lengths.shape[0],
    )
    scalars = (request_token_lengths, adapter_per_request, rank_per_adapter, slot_per_adapter)
    if not sz.fits():
        return by_tokens(
            layer_input_rows,
            encoded_query_rows,
            encoded_key_rows,
            layer_norm_gain,
            base_value_matrix,
            adapter_down_panels,
            adapter_up_panels,
            *scalars,
        )
    return by_heads(
        sz,
        layer_input_rows[0],
        encoded_query_rows[0],
        encoded_key_rows[0],
        layer_norm_gain,
        base_value_matrix[0],
        adapter_down_panels[0],
        adapter_up_panels[0],
        *scalars,
    )[None]


def solution(mesh):
    in_specs = (
        P("segment", ("groups", "seq"), None),
        P("segment", ("groups", "seq"), "owner"),
        P("segment", ("groups", "seq"), "owner"),
        P("segment", None),
        P("segment", ("seq", "owner"), None),
        P("segment", "seq", "owner", None),
        P("segment", "seq", None, "owner"),
        P("groups"),
        P("groups"),
        P(),
        P(),
    )
    out_specs = P("segment", ("groups", "seq"), "owner")
    return jax.shard_map(
        per_device, mesh=mesh, in_specs=in_specs, out_specs=out_specs, check_vma=False
    )
```

```python
import functools

import jax
import jax.numpy as jnp
from jax import lax
from jax.experimental import pallas as pl
from jax.experimental.pallas import tpu as pltpu
from jax.sharding import PartitionSpec as P

WINDOW = 1024
HEADS = 16
KEY_VALUE_HEADS = 8
HEAD_SIZE = 128
LANES = 128

query_scale = 168.0 ** (-0.5)
adapter_strength = 32.0
norm_eps = 1e-06

VMEM = pl.BlockSpec(memory_space=pltpu.VMEM)
SMEM = pl.BlockSpec(memory_space=pltpu.SMEM)
ANY = pl.BlockSpec(memory_space=pl.ANY)
HBM = pl.BlockSpec(memory_space=pltpu.HBM)
PARAMS = pltpu.CompilerParams(vmem_limit_bytes=16 * 1024 * 1024)
FIRST = pltpu.CompilerParams(vmem_limit_bytes=60 * 1024 * 1024)
bf16 = jnp.bfloat16
f32 = jnp.float32


def swap(value, axis, mask):
    return lax.ppermute(value, axis, [(i, i ^ mask) for i in range(lax.axis_size(axis))])


class Sizes:
    def __init__(self, x, queries, down, up, requests):
        self.seq = lax.axis_size("seq")
        self.groups = lax.axis_size("groups")
        self.rows = x.shape[0]
        self.rows_half = self.rows // 2
        self.width = x.shape[1]
        self.half = down.shape[1]
        self.side = self.seq // 2
        self.features = self.width // self.seq
        self.slots_here, self.rank = down.shape[0], down.shape[2]
        self.requests = requests
        self.slot_bits = self.slots_here.bit_length() - 1
        self.side_bits = self.side.bit_length() - 1
        self.heads_here = up.shape[2] // HEAD_SIZE
        self.group_size = HEADS // KEY_VALUE_HEADS
        self.tokens = self.rows * self.seq
        rest = list(range(1, self.seq))
        self.order = [0] + rest[::-1]
        self.order_rows = [0] + rest[:1] + rest[:0:-1]
        self.order_sum = [0] + rest[1:2] + rest[:1] + rest[2:]
        tiles = [
            -(-((i * self.features) % LANES + self.features) // LANES) for i in range(self.side)
        ]
        self.tiles = max(tiles)
        self.span = self.tiles * LANES

    def fits(self):
        return (
            lax.axis_size("owner") == 2
            and self.seq & (self.seq - 1) == 0
            and self.groups & (self.groups - 1) == 0
            and self.half % LANES == 0
            and self.half * 2 == self.width
            and self.heads_here == self.seq
            and self.slots_here == self.groups
            and self.features % 32 == 0
            and self.rows % 64 == 0
            and self.rank % self.rows_half == 0
            and self.pieces() * LANES <= self.span
            and 2 * self.rank == LANES
            and self.seq * self.rows_half == LANES
        )

    def pieces(self):
        return ((self.group_size + 1) * self.rows + self.slots_here * self.rank) // self.rows_half

    def start_in_half(self, i):
        return jnp.minimum((i * self.features) // LANES, self.half // LANES - self.tiles) * LANES

    def start(self, chip):
        return (chip // self.side) * self.half + self.start_in_half(chip % self.side)


def request_column(sz, table, position):
    found = jnp.zeros_like(position)
    for r in range(sz.requests):
        found = found + (position >= table[0, r]).astype(jnp.int32)
    return found


def token_at(sz, place):
    count = sz.seq * sz.rows_half
    owner = (place >= count).astype(jnp.int32)
    place = place - owner * count
    return place // sz.rows_half * sz.rows + owner * sz.rows_half + place % sz.rows_half


def table_kernel(sz, lengths, adapters, ranks, slots, piece, out, held, sem):
    here, core, group = (lax.axis_index(a) for a in ("seq", "owner", "groups"))
    copy = pltpu.make_async_copy(piece, held, sem)
    copy.start()
    end = jnp.int32(0)
    for r in range(sz.requests):
        end = end + lengths[r]
        adapter = adapters[r]
        slot = slots[adapter]
        chip, local = slot >> sz.slot_bits, slot & (sz.slots_here - 1)
        other = (chip >> sz.side_bits) ^ core
        m = (here ^ chip) & (sz.side - 1)
        out[0, r] = end
        out[1, r] = ranks[adapter]
        out[2, r] = (((other << sz.slot_bits) | (local ^ group)) << sz.side_bits) | m
        out[3, r] = ((here ^ chip) * sz.slots_here + local) * sz.rank
    copy.wait()


def panels_kernel(sz, down, *outs_and_sem):
    outs, sem = outs_and_sem[:-1], outs_and_sem[-1]
    here, group = lax.axis_index("seq"), lax.axis_index("groups")
    copies = []
    for m, out in enumerate(outs):
        first = pl.multiple_of(sz.start_in_half((here % sz.side) ^ m), LANES)
        copies.append(
            pltpu.make_async_copy(down.at[group, :, pl.ds(first, sz.span)], out, sem.at[m])
        )
    for copy in copies:
        copy.start()
    for copy in copies:
        copy.wait()


def norm_kernel(sz, x, gain, queries, keys, up, *outs_and_scratch):
    outs, scratch = outs_and_scratch[: sz.seq], outs_and_scratch[sz.seq :]
    taken, gains, query, key, raised, whole, sem = scratch
    here, core = lax.axis_index("seq"), lax.axis_index("owner")
    place = pl.ds(pl.multiple_of(core * sz.rows_half, sz.rows_half), sz.rows_half)
    pairs = ((x.at[place], taken), (gain, gains), (queries, query), (keys, key), (up, raised))
    copies = [pltpu.make_async_copy(a, b, sem.at[i]) for i, (a, b) in enumerate(pairs)]
    for copy in copies:
        copy.start()
    for copy in copies[:2]:
        copy.wait()
    rows = taken[...].astype(f32)
    rows = rows * lax.rsqrt(jnp.mean(rows * rows, axis=1, keepdims=True) + norm_eps)
    whole[...] = (rows * gains[...]).astype(bf16)
    lane = lax.broadcasted_iota(jnp.int32, (sz.rows_half, sz.span), 1)
    for copy in copies[2:]:
        copy.wait()
    for k, out in enumerate(outs):
        head = here ^ k
        first = pl.multiple_of(sz.start(head), LANES)
        skip = head * sz.features - first
        piece = whole[:, pl.ds(first, sz.span)]
        live = (lane >= skip) & (lane < skip + sz.features)
        out[: sz.rows_half] = jnp.where(live, piece.astype(f32), 0.0).astype(bf16)
        parts = []
        for c in range(sz.group_size):
            first = pl.multiple_of((head * sz.group_size + c) * HEAD_SIZE, HEAD_SIZE)
            parts.append(query[:, pl.ds(first, HEAD_SIZE)])
        first = pl.multiple_of(head * HEAD_SIZE, HEAD_SIZE)
        parts.append(key[:, pl.ds(first, HEAD_SIZE)])
        for j in range(sz.slots_here):
            parts.append(raised[j, :, pl.ds(first, HEAD_SIZE)])
        at = 0
        for part in parts:
            for top in range(0, part.shape[0], sz.rows_half):
                out[sz.rows_half :, at : at + HEAD_SIZE] = part[top : top + sz.rows_half]
                at += HEAD_SIZE
        if at < sz.span:
            out[sz.rows_half :, at:] = jnp.zeros((sz.rows_half, sz.span - at), bf16)


def unpack(sz, piece, out, part, first, size):
    for top in range(0, size, sz.rows_half):
        lanes = slice((part + top // sz.rows_half) * HEAD_SIZE, (part + top // sz.rows_half + 1) * HEAD_SIZE)
        place = pl.ds(pl.multiple_of(first + top, sz.rows_half), sz.rows_half)
        out[place, :] = piece[sz.rows_half :, lanes]


def softmax_kernel(sz, table, *refs):
    pieces, (out, raise_picked, scale, query, key, raise_all) = refs[: sz.seq], refs[sz.seq :]
    here = lax.axis_index("seq")
    parts = sz.rows // sz.rows_half
    for k, piece in zip(sz.order, pieces):
        first = (here ^ k) * sz.rows
        for c in range(sz.group_size):
            unpack(sz, piece, query.at[c], c * parts, first, sz.rows)
        for owner in range(parts):
            place = sz.seq * owner * sz.rows_half + (here ^ k) * sz.rows_half
            unpack(sz, piece, key, sz.group_size * parts + owner, place, sz.rows_half)
        size = sz.slots_here * sz.rank
        unpack(sz, piece, raise_all, (sz.group_size + 1) * parts, k * size, size)
    shape = scale.shape
    request = request_column(sz, table, token_at(sz, lax.broadcasted_iota(jnp.int32, shape, 0)))
    rank_here = jnp.ones(shape, jnp.int32)
    for r in range(sz.requests):
        rank_here = jnp.where(request == r, table[1, r], rank_here)
        first = pl.multiple_of(table[3, r], sz.rank)
        raise_picked[r * sz.rank : (r + 1) * sz.rank] = raise_all[pl.ds(first, sz.rank), :]
    scale[...] = adapter_strength / rank_here.astype(f32)
    shape = (sz.tokens, sz.tokens)
    mine = lax.broadcasted_iota(jnp.int32, shape, 0)
    theirs = token_at(sz, lax.broadcasted_iota(jnp.int32, shape, 1))
    live = (theirs <= mine) & (theirs > mine - WINDOW)
    live = live & (request_column(sz, table, mine) == request_column(sz, table, theirs))
    for c in range(sz.group_size):
        scores = lax.dot_general(
            query[c], key[...], (((1,), (1,)), ((), ())), preferred_element_type=f32
        )
        scores = jnp.where(live, scores * query_scale, -1e30)
        weights = jnp.exp(scores - jnp.max(scores, axis=1, keepdims=True))
        out[c * sz.tokens : (c + 1) * sz.tokens] = (
            weights / jnp.sum(weights, axis=1, keepdims=True)
        ).astype(bf16)


def matrix_kernel(sz, base, base_other, out, sem):
    here, core = lax.axis_index("seq"), lax.axis_index("owner")
    depth, wide = base.shape[0], out.shape[1]
    skip = here * sz.features - sz.start(here)
    spare = sz.span - sz.features
    out[0:spare] = jnp.zeros((spare, wide), bf16)
    out[sz.span - spare :] = jnp.zeros((spare, wide), bf16)
    columns = pl.ds(pl.multiple_of(core * wide, wide), wide)
    copies = []
    for j, (ref, owner) in enumerate(((base, core), (base_other, 1 - core))):
        place = pl.ds(pl.multiple_of(skip + owner * depth, 16), depth)
        copies.append(pltpu.make_async_copy(ref.at[:, columns], out.at[place], sem.at[j]))
        copies[-1].start()
    for copy in copies:
        copy.wait()


def gather_kernel(sz, *refs):
    pieces, out = refs[: sz.seq], refs[sz.seq]
    here = lax.axis_index("seq")
    for k, piece in zip(sz.order, pieces):
        first = pl.multiple_of((here ^ k) * sz.rows_half, sz.rows_half)
        out[pl.ds(first, sz.rows_half), :] = piece[: sz.rows_half]


def project_half(sz, table, matrix, rows, picked, owner):
    values = jnp.dot(rows[...], matrix[...], preferred_element_type=f32)
    low = lax.dot_general(
        picked[...], rows[...], (((1,), (1,)), ((), ())), preferred_element_type=f32
    )
    shape = (sz.rank, sz.seq * sz.rows_half)
    place = lax.broadcasted_iota(jnp.int32, shape, 1) + owner * shape[1]
    request = request_column(sz, table, token_at(sz, place))
    rank = lax.broadcasted_iota(jnp.int32, shape, 0)
    reduced = jnp.zeros(shape, f32)
    for r in range(sz.requests):
        live = (request == r) & (rank < table[1, r])
        reduced = jnp.where(live, low[r * sz.rank : (r + 1) * sz.rank], reduced)
    return values.astype(bf16), reduced.astype(bf16)


def project_own_kernel(sz, table, matrix, own, *refs):
    panels, (picked, values, low, stacked) = refs[:-4], refs[-4:]
    for p, panel in enumerate(panels):
        stacked[p * sz.rank : (p + 1) * sz.rank] = panel[...]
    for r in range(sz.requests):
        first = pl.multiple_of(table[2, r] * sz.rank, sz.rank)
        picked[r * sz.rank : (r + 1) * sz.rank] = stacked[pl.ds(first, sz.rank), :]
    values[...], low[...] = project_half(
        sz, table, matrix, own, picked, lax.axis_index("owner")
    )


def project_other_kernel(sz, table, matrix, other, picked, values_own, low_own, *refs):
    outs, values_other = refs[: sz.seq], refs[sz.seq]
    here, core = lax.axis_index("seq"), lax.axis_index("owner")
    values_other[...], low_other = project_half(sz, table, matrix, other, picked, 1 - core)
    count = sz.seq * sz.rows_half
    for k, out in enumerate(outs):
        columns = pl.ds(pl.multiple_of((here ^ k) * HEAD_SIZE, HEAD_SIZE), HEAD_SIZE)
        for values, low, owner in (
            (values_own, low_own[...], core),
            (values_other, low_other, 1 - core),
        ):
            first = pl.multiple_of(owner * count, count)
            out[pl.ds(first, count), :] = values[:, columns]
            first = pl.multiple_of(sz.tokens + owner * sz.rank, sz.rank)
            out[pl.ds(first, sz.rank), :] = low


def mix_kernel(sz, table, softmax, raise_picked, scale, *refs):
    partials, refs = refs[: sz.seq], refs[sz.seq :]
    outs, (wide, mixed) = refs[: sz.seq], refs[sz.seq :]
    here = lax.axis_index("seq")
    count = sz.seq * sz.rows_half
    low = sum(partial[sz.tokens :].astype(f32) for partial in partials)
    shape = (sz.rank, count)
    for owner in range(2):
        place = lax.broadcasted_iota(jnp.int32, shape, 1) + owner * count
        request = request_column(sz, table, token_at(sz, place))
        own = low[owner * sz.rank : (owner + 1) * sz.rank]
        for r in range(sz.requests):
            wide[r * sz.rank : (r + 1) * sz.rank, owner * count : (owner + 1) * count] = jnp.where(
                request == r, own, 0.0
            ).astype(bf16)
    raised = lax.dot_general(
        wide[...], raise_picked[...], (((0,), (0,)), ((), ())), preferred_element_type=f32
    )
    base = sum(partial[: sz.tokens].astype(f32) for partial in partials)
    values = (base + scale[...] * raised).astype(bf16)
    mixed[...] = jnp.dot(softmax[...], values, preferred_element_type=f32).astype(bf16)
    for k, out in enumerate(outs):
        for c in range(sz.group_size):
            first = pl.multiple_of(c * sz.tokens + (here ^ k) * sz.rows, sz.rows)
            out[:, c * HEAD_SIZE : (c + 1) * HEAD_SIZE] = mixed[pl.ds(first, sz.rows), :]


def place_kernel(sz, *refs):
    pieces, out = refs[: sz.seq], refs[sz.seq]
    here = lax.axis_index("seq")
    wide = sz.group_size * HEAD_SIZE
    for k, piece in zip(sz.order, pieces):
        head = here ^ k
        out[:, pl.ds(pl.multiple_of(head * wide, wide), wide)] = piece[...]


def by_heads(sz, x, queries, keys, gain, base, down, up, lengths, adapters, ranks, slots):
    around = range(1, sz.seq)
    half_columns = base.shape[1] // 2

    def ordered(values):
        return [values[k] for k in sz.order]

    spread = (2 * sz.rows_half, sz.span)

    def call(kernel, name, ins, outs, args, scratch=(), params=PARAMS, cost=None):
        return pl.pallas_call(
            functools.partial(kernel, sz),
            out_shape=[jax.ShapeDtypeStruct(shape, dtype) for shape, dtype, _ in outs],
            in_specs=ins,
            out_specs=[spec for _, _, spec in outs],
            scratch_shapes=list(scratch),
            compiler_params=params,
            cost_estimate=cost,
            name=name,
        )(*args)

    panels_out = call(
        panels_kernel,
        "panels_out",
        [HBM],
        [((sz.rank, sz.span), bf16, VMEM)] * sz.side,
        (jnp.swapaxes(down, 1, 2),),
        (pltpu.SemaphoreType.DMA((sz.side,)),),
    )
    panels = []
    for m in range(sz.side):
        pairs = [
            (h * 2 + c, (c * sz.side + ((h % sz.side) ^ m)) * 2 + h // sz.side)
            for h in range(sz.seq)
            for c in range(2)
        ]
        panels.append(lax.ppermute(panels_out[m], ("seq", "owner"), pairs))
    x, _ = lax.optimization_barrier((x, panels_out[0]))
    rows_out = call(
        norm_kernel,
        "norm_rows",
        [HBM] * 5,
        [(spread, bf16, VMEM)] * sz.seq,
        (x, gain, queries, keys, up),
        (
            pltpu.VMEM((sz.rows_half, sz.width), bf16),
            pltpu.VMEM((1, sz.width), f32),
            pltpu.VMEM(queries.shape, bf16),
            pltpu.VMEM(keys.shape, bf16),
            pltpu.VMEM(up.shape, bf16),
            pltpu.VMEM((sz.rows_half, sz.width), bf16),
            pltpu.SemaphoreType.DMA((5,)),
        ),
        FIRST,
    )
    table, held = call(
        table_kernel,
        "table",
        [SMEM] * 4 + [ANY],
        [((4, sz.requests), jnp.int32, SMEM), (spread, bf16, VMEM)],
        (lengths, adapters, ranks, slots, rows_out[0]),
        (pltpu.SemaphoreType.DMA,),
        cost=pl.CostEstimate(flops=0, bytes_accessed=64 * 1024 * 1024, transcendentals=0),
    )
    (matrix,) = call(
        matrix_kernel,
        "matrix_rows",
        [HBM, ANY],
        [((sz.span, half_columns), bf16, VMEM)],
        (base, swap(base, "owner", 1)),
        (pltpu.SemaphoreType.DMA((2,)),),
    )
    rows_in = [held] + [swap(rows_out[k], "seq", k) for k in around]

    panels[0], table, matrix = lax.optimization_barrier((panels[0], table, matrix))
    panels[1], held = lax.optimization_barrier((panels[1], held))
    rows_in[0] = held
    panels = panels + [swap(p, "groups", k) for k in range(1, sz.groups) for p in panels]
    panels = panels + [swap(p, "owner", 1) for p in panels]
    rows_ordered, panels = lax.optimization_barrier(([rows_in[k] for k in sz.order_rows], panels))
    rows_in = [rows_ordered[sz.order_rows.index(k)] for k in range(sz.seq)]
    (own,) = call(
        gather_kernel,
        "gather_rows",
        [VMEM] * sz.seq,
        [((sz.seq * sz.rows_half, sz.span), bf16, VMEM)],
        ordered(rows_in),
    )
    other = swap(own, "owner", 1)
    softmax, raise_picked, scale = call(
        softmax_kernel,
        "softmax_rows",
        [SMEM] + [VMEM] * sz.seq,
        [
            ((sz.group_size * sz.tokens, sz.tokens), bf16, VMEM),
            ((sz.requests * sz.rank, HEAD_SIZE), bf16, VMEM),
            ((sz.tokens, HEAD_SIZE), f32, VMEM),
        ],
        (table, *ordered(rows_in)),
        (
            pltpu.VMEM((sz.group_size, sz.tokens, HEAD_SIZE), bf16),
            pltpu.VMEM((sz.tokens, HEAD_SIZE), bf16),
            pltpu.VMEM((sz.seq * sz.slots_here * sz.rank, HEAD_SIZE), bf16),
        ),
    )

    count = sz.seq * sz.rows_half
    partial_shape = (sz.tokens + 2 * sz.rank, HEAD_SIZE)
    picked, values_own, low_own = call(
        project_own_kernel,
        "project_own",
        [SMEM] + [VMEM] * (2 + len(panels)),
        [
            ((sz.requests * sz.rank, sz.span), bf16, VMEM),
            ((count, half_columns), bf16, VMEM),
            ((sz.rank, count), bf16, VMEM),
        ],
        (table, matrix, own, *panels),
        (pltpu.VMEM((len(panels) * sz.rank, sz.span), bf16),),
    )
    partial_out = call(
        project_other_kernel,
        "project_other",
        [SMEM] + [VMEM] * 5,
        [(partial_shape, bf16, VMEM)] * sz.seq,
        (table, matrix, other, picked, values_own, low_own),
        (pltpu.VMEM((count, half_columns), bf16),),
    )
    partial_in = [partial_out[0]] + [swap(partial_out[k], "seq", k) for k in around]
    wide = sz.group_size * HEAD_SIZE
    mixed = call(
        mix_kernel,
        "mix_values",
        [SMEM] + [VMEM] * (3 + sz.seq),
        [((sz.rows, wide), bf16, VMEM)] * sz.seq,
        (table, softmax, raise_picked, scale, *[partial_in[k] for k in sz.order_sum]),
        (
            pltpu.VMEM((sz.requests * sz.rank, sz.tokens), bf16),
            pltpu.VMEM((sz.group_size * sz.tokens, HEAD_SIZE), bf16),
        ),
    )
    mixed_in = [mixed[0]] + [swap(mixed[k], "seq", k) for k in around]
    (result,) = call(
        place_kernel,
        "place_heads",
        [VMEM] * sz.seq,
        [((sz.rows, sz.seq * wide), bf16, VMEM)],
        ordered(mixed_in),
    )
    return result


def broadcast(x, axis, root):
    mine = lax.axis_index(axis) == root
    return lax.psum(jnp.where(mine, x, jnp.zeros_like(x)), axis)


def from_behind(value, axis, steps):
    count = lax.axis_size(axis)
    first, last = (max(0, -steps), min(count, count - steps))
    return lax.ppermute(value, axis, [(source, source + steps) for source in range(first, last)])


def by_tokens(
    layer_input_rows,
    encoded_query_rows,
    encoded_key_rows,
    layer_norm_gain,
    base_value_matrix,
    adapter_down_panels,
    adapter_up_panels,
    request_token_lengths,
    adapter_per_request,
    rank_per_adapter,
    slot_per_adapter,
):
    hidden = layer_input_rows[0]
    row_count = hidden.shape[0]
    seq_now = lax.axis_index("seq")
    owner_now = lax.axis_index("owner")
    reach_count = min(WINDOW // row_count, lax.axis_size("seq") - 1)
    requests = request_token_lengths.shape[0]
    library = slot_per_adapter.shape[0]
    slots_here = adapter_down_panels.shape[1]
    rows_halved = adapter_down_panels.shape[2]
    rank_span_width = adapter_down_panels.shape[3]
    key_value_halved = adapter_up_panels.shape[3]
    group_size = HEADS // KEY_VALUE_HEADS
    request_ends = jnp.cumsum(request_token_lengths)
    position = seq_now * row_count + jnp.arange(row_count, dtype=jnp.int32)
    context = seq_now * row_count + jnp.arange(-reach_count * row_count, row_count, dtype=jnp.int32)
    request_lookup = jnp.sum((position[:, None] >= request_ends[None, :]).astype(jnp.int32), axis=1)
    request_ctx = jnp.sum((context[:, None] >= request_ends[None, :]).astype(jnp.int32), axis=1)
    live_mask = (context[None, :] <= position[:, None]) & (
        context[None, :] > position[:, None] - WINDOW
    )
    live_mask = (
        live_mask & (context[None, :] >= 0) & (request_ctx[None, :] == request_lookup[:, None])
    )
    choose = adapter_per_request[:, None] == jnp.arange(library, dtype=jnp.int32)[None, :]
    slot_of = jnp.sum(jnp.where(choose, slot_per_adapter[None, :], 0), axis=1)
    rank_lookup = jnp.sum(jnp.where(choose, rank_per_adapter[None, :], 0), axis=1)
    scale_lookup = adapter_strength / rank_lookup.astype(jnp.float32)
    in_request = request_lookup[:, None] == jnp.arange(requests, dtype=jnp.int32)[None, :]
    column_live = jnp.arange(rank_span_width, dtype=jnp.int32)[None, :] < rank_lookup[:, None]
    row_gain_weight = jnp.where(in_request, scale_lookup[None, :], jnp.float32(0.0))
    down_panel_here = adapter_down_panels[0]
    up_panel_here = adapter_up_panels[0]
    queries = encoded_query_rows[0]
    keys_own = encoded_key_rows[0]
    key_heads = keys_own.shape[1] // HEAD_SIZE
    wide_rows = hidden.astype(jnp.float32)
    normalized_rows = wide_rows * lax.rsqrt(
        jnp.mean(wide_rows * wide_rows, axis=1, keepdims=True) + norm_eps
    )
    normalized_rows = (normalized_rows * layer_norm_gain[0][None, :]).astype(jnp.bfloat16)
    normed_half = lax.dynamic_slice_in_dim(normalized_rows, owner_now * rows_halved, rows_halved, 1)
    full_value = jnp.dot(
        normalized_rows,
        lax.all_gather(base_value_matrix[0], ("seq", "owner"), axis=0, tiled=True),
        preferred_element_type=jnp.float32,
    )
    value_base_rows = lax.dynamic_slice_in_dim(
        full_value, owner_now * key_value_halved, key_value_halved, 1
    )

    def fetch_one(reduced_rows, request_index):
        owner_slot = slot_of[request_index]
        holder = owner_slot // slots_here
        local_slot = owner_slot % slots_here
        down_local = lax.dynamic_slice_in_dim(down_panel_here, local_slot, 1, 0)
        up_local = lax.dynamic_slice_in_dim(up_panel_here, local_slot, 1, 0)
        down_piece, up_piece = (
            broadcast(down_local, "seq", holder),
            broadcast(up_local, "seq", holder),
        )
        keep_mask = in_request[:, request_index][:, None] & column_live[request_index][None, :]
        matrix_product = jnp.dot(normed_half, down_piece[0], preferred_element_type=jnp.float32)
        return (reduced_rows + jnp.where(keep_mask, matrix_product, jnp.float32(0.0)), up_piece[0])

    start_low = jnp.zeros((row_count, rank_span_width), jnp.float32)
    reduced_rows, panels_up = lax.scan(fetch_one, start_low, jnp.arange(requests, dtype=jnp.int32))
    reduced_rows = lax.psum(reduced_rows, "owner").astype(jnp.bfloat16)
    raised_rows = jnp.einsum(
        "tr,qrk->qtk", reduced_rows, panels_up, preferred_element_type=jnp.float32
    )
    adapter_value = jnp.sum(row_gain_weight.T[:, :, None] * raised_rows, axis=0)
    value_output_rows = (value_base_rows + adapter_value).astype(jnp.bfloat16)
    key_parts = []
    value_parts = []
    for shift_by in range(reach_count, 0, -1):
        key_piece, value_piece = from_behind((keys_own, value_output_rows), "seq", shift_by)
        key_parts.append(key_piece)
        value_parts.append(value_piece)
    keys_all = jnp.concatenate(key_parts + [keys_own], axis=0)
    values_all = jnp.concatenate(value_parts + [value_output_rows], axis=0)
    query_view = queries.reshape(row_count, key_heads, group_size, HEAD_SIZE)
    key_view = keys_all.reshape(-1, key_heads, HEAD_SIZE)
    value_view = values_all.reshape(-1, key_heads, HEAD_SIZE)
    head_outputs = []
    for head_index in range(key_heads):
        query_head = query_view[:, head_index]
        scores = (
            jnp.einsum(
                "tcd,jd->ctj",
                query_head,
                key_view[:, head_index],
                preferred_element_type=jnp.float32,
            )
            * query_scale
        )
        scores = jnp.where(live_mask[None], scores, jnp.float32(-1e30))
        row_max = jnp.max(scores, axis=-1, keepdims=True)
        weights = jnp.exp(scores - row_max)
        row_total = jnp.sum(weights, axis=-1, keepdims=True)
        softmax_rows = (weights / row_total).astype(jnp.bfloat16)
        mixed = jnp.einsum(
            "ctj,jd->tcd",
            softmax_rows,
            value_view[:, head_index],
            preferred_element_type=jnp.float32,
        )
        head_outputs.append(mixed.astype(jnp.bfloat16).reshape(row_count, group_size * HEAD_SIZE))
    result = jnp.concatenate(head_outputs, axis=1)
    return result[None]


def per_device(
    layer_input_rows,
    encoded_query_rows,
    encoded_key_rows,
    layer_norm_gain,
    base_value_matrix,
    adapter_down_panels,
    adapter_up_panels,
    request_token_lengths,
    adapter_per_request,
    rank_per_adapter,
    slot_per_adapter,
):
    sz = Sizes(
        layer_input_rows[0],
        encoded_query_rows[0],
        adapter_down_panels[0],
        adapter_up_panels[0],
        request_token_lengths.shape[0],
    )
    scalars = (request_token_lengths, adapter_per_request, rank_per_adapter, slot_per_adapter)
    if not sz.fits():
        return by_tokens(
            layer_input_rows,
            encoded_query_rows,
            encoded_key_rows,
            layer_norm_gain,
            base_value_matrix,
            adapter_down_panels,
            adapter_up_panels,
            *scalars,
        )
    return by_heads(
        sz,
        layer_input_rows[0],
        encoded_query_rows[0],
        encoded_key_rows[0],
        layer_norm_gain,
        base_value_matrix[0],
        adapter_down_panels[0],
        adapter_up_panels[0],
        *scalars,
    )[None]


def solution(mesh):
    in_specs = (
        P("segment", ("groups", "seq"), None),
        P("segment", ("groups", "seq"), "owner"),
        P("segment", ("groups", "seq"), "owner"),
        P("segment", None),
        P("segment", ("seq", "owner"), None),
        P("segment", "seq", "owner", None),
        P("segment", "seq", None, "owner"),
        P("groups"),
        P("groups"),
        P(),
        P(),
    )
    out_specs = P("segment", ("groups", "seq"), "owner")
    return jax.shard_map(
        per_device, mesh=mesh, in_specs=in_specs, out_specs=out_specs, check_vma=False
    )
```

```python
import functools

import jax
import jax.numpy as jnp
from jax import lax
from jax.experimental import pallas as pl
from jax.experimental.pallas import tpu as pltpu
from jax.sharding import PartitionSpec as P

WINDOW = 1024
HEADS = 16
KEY_VALUE_HEADS = 8
HEAD_SIZE = 128
LANES = 128

query_scale = 168.0 ** (-0.5)
adapter_strength = 32.0
norm_eps = 1e-06

VMEM = pl.BlockSpec(memory_space=pltpu.VMEM)
SMEM = pl.BlockSpec(memory_space=pltpu.SMEM)
ANY = pl.BlockSpec(memory_space=pl.ANY)
HBM = pl.BlockSpec(memory_space=pltpu.HBM)
PARAMS = pltpu.CompilerParams(vmem_limit_bytes=16 * 1024 * 1024)
FIRST = pltpu.CompilerParams(vmem_limit_bytes=60 * 1024 * 1024)
bf16 = jnp.bfloat16
f32 = jnp.float32


def swap(value, axis, mask):
    return lax.ppermute(value, axis, [(i, i ^ mask) for i in range(lax.axis_size(axis))])


class Sizes:
    def __init__(self, x, queries, down, up, requests):
        self.seq = lax.axis_size("seq")
        self.groups = lax.axis_size("groups")
        self.rows = x.shape[0]
        self.rows_half = self.rows // 2
        self.width = x.shape[1]
        self.half = down.shape[1]
        self.side = self.seq // 2
        self.features = self.width // self.seq
        self.slots_here, self.rank = down.shape[0], down.shape[2]
        self.requests = requests
        self.slot_bits = self.slots_here.bit_length() - 1
        self.side_bits = self.side.bit_length() - 1
        self.heads_here = up.shape[2] // HEAD_SIZE
        self.group_size = HEADS // KEY_VALUE_HEADS
        self.tokens = self.rows * self.seq
        rest = list(range(1, self.seq))
        self.order = [0] + rest[::-1]
        self.order_rows = [0] + rest[:1] + rest[:0:-1]
        self.order_sum = [0] + rest[1:2] + rest[:1] + rest[2:]
        tiles = [
            -(-((i * self.features) % LANES + self.features) // LANES) for i in range(self.side)
        ]
        self.tiles = max(tiles)
        self.span = self.tiles * LANES

    def fits(self):
        return (
            lax.axis_size("owner") == 2
            and self.seq & (self.seq - 1) == 0
            and self.groups & (self.groups - 1) == 0
            and self.half % LANES == 0
            and self.half * 2 == self.width
            and self.heads_here == self.seq
            and self.slots_here == self.groups
            and self.features % 32 == 0
            and self.rows % 64 == 0
            and self.rank % self.rows_half == 0
            and self.pieces() * LANES <= self.span
            and 2 * self.rank == LANES
            and self.seq * self.rows_half == LANES
        )

    def pieces(self):
        return ((self.group_size + 1) * self.rows + self.slots_here * self.rank) // self.rows_half

    def start_in_half(self, i):
        return jnp.minimum((i * self.features) // LANES, self.half // LANES - self.tiles) * LANES

    def start(self, chip):
        return (chip // self.side) * self.half + self.start_in_half(chip % self.side)


def request_column(sz, table, position):
    found = jnp.zeros_like(position)
    for r in range(sz.requests):
        found = found + (position >= table[0, r]).astype(jnp.int32)
    return found


def token_at(sz, place):
    count = sz.seq * sz.rows_half
    owner = (place >= count).astype(jnp.int32)
    place = place - owner * count
    return place // sz.rows_half * sz.rows + owner * sz.rows_half + place % sz.rows_half


def table_kernel(sz, lengths, adapters, ranks, slots, piece, out, held, sem):
    here, core, group = (lax.axis_index(a) for a in ("seq", "owner", "groups"))
    copy = pltpu.make_async_copy(piece, held, sem)
    copy.start()
    end = jnp.int32(0)
    for r in range(sz.requests):
        end = end + lengths[r]
        adapter = adapters[r]
        slot = slots[adapter]
        chip, local = slot >> sz.slot_bits, slot & (sz.slots_here - 1)
        other = (chip >> sz.side_bits) ^ core
        m = (here ^ chip) & (sz.side - 1)
        out[0, r] = end
        out[1, r] = ranks[adapter]
        out[2, r] = (((other << sz.slot_bits) | (local ^ group)) << sz.side_bits) | m
        out[3, r] = ((here ^ chip) * sz.slots_here + local) * sz.rank
    copy.wait()


def panels_kernel(sz, down, *outs_and_sem):
    outs, sem = outs_and_sem[:-1], outs_and_sem[-1]
    here, group = lax.axis_index("seq"), lax.axis_index("groups")
    copies = []
    for m, out in enumerate(outs):
        first = pl.multiple_of(sz.start_in_half((here % sz.side) ^ m), LANES)
        copies.append(
            pltpu.make_async_copy(down.at[group, :, pl.ds(first, sz.span)], out, sem.at[m])
        )
    for copy in copies:
        copy.start()
    for copy in copies:
        copy.wait()


def norm_kernel(sz, x, gain, queries, keys, up, *outs_and_scratch):
    outs, scratch = outs_and_scratch[: sz.seq], outs_and_scratch[sz.seq :]
    taken, gains, query, key, raised, whole, sem = scratch
    here, core = lax.axis_index("seq"), lax.axis_index("owner")
    place = pl.ds(pl.multiple_of(core * sz.rows_half, sz.rows_half), sz.rows_half)
    pairs = ((x.at[place], taken), (gain, gains), (queries, query), (keys, key), (up, raised))
    copies = [pltpu.make_async_copy(a, b, sem.at[i]) for i, (a, b) in enumerate(pairs)]
    for copy in copies:
        copy.start()
    for copy in copies[:2]:
        copy.wait()
    rows = taken[...].astype(f32)
    rows = rows * lax.rsqrt(jnp.mean(rows * rows, axis=1, keepdims=True) + norm_eps)
    whole[...] = (rows * gains[...]).astype(bf16)
    lane = lax.broadcasted_iota(jnp.int32, (sz.rows_half, sz.span), 1)
    for copy in copies[2:]:
        copy.wait()
    for k, out in enumerate(outs):
        head = here ^ k
        first = pl.multiple_of(sz.start(head), LANES)
        skip = head * sz.features - first
        piece = whole[:, pl.ds(first, sz.span)]
        live = (lane >= skip) & (lane < skip + sz.features)
        out[: sz.rows_half] = jnp.where(live, piece.astype(f32), 0.0).astype(bf16)
        parts = []
        for c in range(sz.group_size):
            first = pl.multiple_of((head * sz.group_size + c) * HEAD_SIZE, HEAD_SIZE)
            parts.append(query[:, pl.ds(first, HEAD_SIZE)])
        first = pl.multiple_of(head * HEAD_SIZE, HEAD_SIZE)
        parts.append(key[:, pl.ds(first, HEAD_SIZE)])
        for j in range(sz.slots_here):
            parts.append(raised[j, :, pl.ds(first, HEAD_SIZE)])
        at = 0
        for part in parts:
            for top in range(0, part.shape[0], sz.rows_half):
                out[sz.rows_half :, at : at + HEAD_SIZE] = part[top : top + sz.rows_half]
                at += HEAD_SIZE
        if at < sz.span:
            out[sz.rows_half :, at:] = jnp.zeros((sz.rows_half, sz.span - at), bf16)


def unpack(sz, piece, out, part, first, size):
    for top in range(0, size, sz.rows_half):
        lanes = slice((part + top // sz.rows_half) * HEAD_SIZE, (part + top // sz.rows_half + 1) * HEAD_SIZE)
        place = pl.ds(pl.multiple_of(first + top, sz.rows_half), sz.rows_half)
        out[place, :] = piece[sz.rows_half :, lanes]


def softmax_kernel(sz, table, *refs):
    pieces, (out, raise_picked, scale, query, key, raise_all) = refs[: sz.seq], refs[sz.seq :]
    here = lax.axis_index("seq")
    parts = sz.rows // sz.rows_half
    for k, piece in zip(sz.order, pieces):
        first = (here ^ k) * sz.rows
        for c in range(sz.group_size):
            unpack(sz, piece, query.at[c], c * parts, first, sz.rows)
        for owner in range(parts):
            place = sz.seq * owner * sz.rows_half + (here ^ k) * sz.rows_half
            unpack(sz, piece, key, sz.group_size * parts + owner, place, sz.rows_half)
        size = sz.slots_here * sz.rank
        unpack(sz, piece, raise_all, (sz.group_size + 1) * parts, k * size, size)
    shape = scale.shape
    request = request_column(sz, table, token_at(sz, lax.broadcasted_iota(jnp.int32, shape, 0)))
    rank_here = jnp.ones(shape, jnp.int32)
    for r in range(sz.requests):
        rank_here = jnp.where(request == r, table[1, r], rank_here)
        first = pl.multiple_of(table[3, r], sz.rank)
        raise_picked[r * sz.rank : (r + 1) * sz.rank] = raise_all[pl.ds(first, sz.rank), :]
    scale[...] = adapter_strength / rank_here.astype(f32)
    shape = (sz.tokens, sz.tokens)
    mine = lax.broadcasted_iota(jnp.int32, shape, 0)
    theirs = token_at(sz, lax.broadcasted_iota(jnp.int32, shape, 1))
    live = (theirs <= mine) & (theirs > mine - WINDOW)
    live = live & (request_column(sz, table, mine) == request_column(sz, table, theirs))
    for c in range(sz.group_size):
        scores = lax.dot_general(
            query[c], key[...], (((1,), (1,)), ((), ())), preferred_element_type=f32
        )
        scores = jnp.where(live, scores * query_scale, -1e30)
        weights = jnp.exp(scores - jnp.max(scores, axis=1, keepdims=True))
        out[c * sz.tokens : (c + 1) * sz.tokens] = (
            weights / jnp.sum(weights, axis=1, keepdims=True)
        ).astype(bf16)


def matrix_kernel(sz, base, base_other, out, sem):
    here, core = lax.axis_index("seq"), lax.axis_index("owner")
    depth, wide = base.shape[0], out.shape[1]
    skip = here * sz.features - sz.start(here)
    spare = sz.span - sz.features
    out[0:spare] = jnp.zeros((spare, wide), bf16)
    out[sz.span - spare :] = jnp.zeros((spare, wide), bf16)
    copies = []
    for j, (ref, owner) in enumerate(((base, core), (base_other, 1 - core))):
        place = pl.ds(pl.multiple_of(skip + owner * depth, 16), depth)
        copies.append(pltpu.make_async_copy(ref, out.at[place], sem.at[j]))
        copies[-1].start()
    for copy in copies:
        copy.wait()


def gather_kernel(sz, *refs):
    pieces, out = refs[: sz.seq], refs[sz.seq]
    here = lax.axis_index("seq")
    for k, piece in zip(sz.order, pieces):
        first = pl.multiple_of((here ^ k) * sz.rows_half, sz.rows_half)
        out[pl.ds(first, sz.rows_half), :] = piece[: sz.rows_half]


def project_kernel(sz, table, matrix, own, *refs):
    panels, refs = refs[: 2 * sz.groups * sz.side], refs[2 * sz.groups * sz.side :]
    outs, (picked, stacked, values) = refs[: sz.seq], refs[sz.seq :]
    here, core = lax.axis_index("seq"), lax.axis_index("owner")
    for p, panel in enumerate(panels):
        stacked[p * sz.rank : (p + 1) * sz.rank] = panel[...]
    for r in range(sz.requests):
        first = pl.multiple_of(table[2, r] * sz.rank, sz.rank)
        picked[r * sz.rank : (r + 1) * sz.rank] = stacked[pl.ds(first, sz.rank), :]
    values[...] = jnp.dot(own[...], matrix[...], preferred_element_type=f32).astype(bf16)
    low = lax.dot_general(
        picked[...], own[...], (((1,), (1,)), ((), ())), preferred_element_type=f32
    )
    count = sz.seq * sz.rows_half
    shape = (sz.rank, count)
    place = lax.broadcasted_iota(jnp.int32, shape, 1) + core * count
    request = request_column(sz, table, token_at(sz, place))
    rank = lax.broadcasted_iota(jnp.int32, shape, 0)
    reduced = jnp.zeros(shape, f32)
    for r in range(sz.requests):
        live = (request == r) & (rank < table[1, r])
        reduced = jnp.where(live, low[r * sz.rank : (r + 1) * sz.rank], reduced)
    reduced = reduced.astype(bf16)
    for k, out in enumerate(outs):
        for half in range(2):
            first = pl.multiple_of((half * sz.heads_here + (here ^ k)) * HEAD_SIZE, HEAD_SIZE)
            out[half * count : (half + 1) * count] = values[:, pl.ds(first, HEAD_SIZE)]
        out[2 * count :] = reduced


def add_kernel(sz, *refs):
    pieces, (kept, sent) = refs[: sz.seq], refs[sz.seq :]
    core = lax.axis_index("owner")
    count = sz.seq * sz.rows_half
    for out, head in ((kept, core), (sent, 1 - core)):
        place = pl.ds(pl.multiple_of(head * count, count), count)
        out[:count] = sum(piece[place, :].astype(f32) for piece in pieces)
    low = sum(piece[2 * count :].astype(f32) for piece in pieces)
    kept[count:] = low
    sent[count:] = low


def mix_kernel(sz, table, softmax, raise_picked, scale, kept, received, *refs):
    outs, (wide, base, mixed) = refs[: sz.seq], refs[sz.seq :]
    here, core = lax.axis_index("seq"), lax.axis_index("owner")
    count = sz.seq * sz.rows_half
    shape = (sz.rank, count)
    for ref, owner in ((kept, core), (received, 1 - core)):
        first = pl.multiple_of(owner * count, count)
        base[pl.ds(first, count), :] = ref[:count]
        place = lax.broadcasted_iota(jnp.int32, shape, 1) + first
        request = request_column(sz, table, token_at(sz, place))
        for r in range(sz.requests):
            wide[r * sz.rank : (r + 1) * sz.rank, pl.ds(first, count)] = jnp.where(
                request == r, ref[count:], 0.0
            ).astype(bf16)
    raised = lax.dot_general(
        wide[...], raise_picked[...], (((0,), (0,)), ((), ())), preferred_element_type=f32
    )
    values = (base[...] + scale[...] * raised).astype(bf16)
    mixed[...] = jnp.dot(softmax[...], values, preferred_element_type=f32).astype(bf16)
    for k, out in enumerate(outs):
        for c in range(sz.group_size):
            first = pl.multiple_of(c * sz.tokens + (here ^ k) * sz.rows, sz.rows)
            out[:, c * HEAD_SIZE : (c + 1) * HEAD_SIZE] = mixed[pl.ds(first, sz.rows), :]


def place_kernel(sz, *refs):
    pieces, out = refs[: sz.seq], refs[sz.seq]
    here = lax.axis_index("seq")
    wide = sz.group_size * HEAD_SIZE
    for k, piece in zip(sz.order, pieces):
        head = here ^ k
        out[:, pl.ds(pl.multiple_of(head * wide, wide), wide)] = piece[...]


def by_heads(sz, x, queries, keys, gain, base, down, up, lengths, adapters, ranks, slots):
    around = range(1, sz.seq)

    def ordered(values):
        return [values[k] for k in sz.order]

    spread = (2 * sz.rows_half, sz.span)

    def call(kernel, name, ins, outs, args, scratch=(), params=PARAMS, cost=None):
        return pl.pallas_call(
            functools.partial(kernel, sz),
            out_shape=[jax.ShapeDtypeStruct(shape, dtype) for shape, dtype, _ in outs],
            in_specs=ins,
            out_specs=[spec for _, _, spec in outs],
            scratch_shapes=list(scratch),
            compiler_params=params,
            cost_estimate=cost,
            name=name,
        )(*args)

    panels_out = call(
        panels_kernel,
        "panels_out",
        [HBM],
        [((sz.rank, sz.span), bf16, VMEM)] * sz.side,
        (jnp.swapaxes(down, 1, 2),),
        (pltpu.SemaphoreType.DMA((sz.side,)),),
    )
    panels = []
    for m in range(sz.side):
        pairs = [
            (h * 2 + c, (c * sz.side + ((h % sz.side) ^ m)) * 2 + h // sz.side)
            for h in range(sz.seq)
            for c in range(2)
        ]
        panels.append(lax.ppermute(panels_out[m], ("seq", "owner"), pairs))
    x, _ = lax.optimization_barrier((x, panels_out[0]))
    rows_out = call(
        norm_kernel,
        "norm_rows",
        [HBM] * 5,
        [(spread, bf16, VMEM)] * sz.seq,
        (x, gain, queries, keys, up),
        (
            pltpu.VMEM((sz.rows_half, sz.width), bf16),
            pltpu.VMEM((1, sz.width), f32),
            pltpu.VMEM(queries.shape, bf16),
            pltpu.VMEM(keys.shape, bf16),
            pltpu.VMEM(up.shape, bf16),
            pltpu.VMEM((sz.rows_half, sz.width), bf16),
            pltpu.SemaphoreType.DMA((5,)),
        ),
        FIRST,
    )
    table, held = call(
        table_kernel,
        "table",
        [SMEM] * 4 + [ANY],
        [((4, sz.requests), jnp.int32, SMEM), (spread, bf16, VMEM)],
        (lengths, adapters, ranks, slots, rows_out[0]),
        (pltpu.SemaphoreType.DMA,),
        cost=pl.CostEstimate(flops=0, bytes_accessed=64 * 1024 * 1024, transcendentals=0),
    )
    (matrix,) = call(
        matrix_kernel,
        "matrix_rows",
        [HBM, ANY],
        [((sz.span, base.shape[1]), bf16, VMEM)],
        (base, swap(base, "owner", 1)),
        (pltpu.SemaphoreType.DMA((2,)),),
    )
    rows_in = [held] + [swap(rows_out[k], "seq", k) for k in around]

    panels[0], table, matrix = lax.optimization_barrier((panels[0], table, matrix))
    panels[1], held = lax.optimization_barrier((panels[1], held))
    rows_in[0] = held
    panels = panels + [swap(p, "groups", k) for k in range(1, sz.groups) for p in panels]
    panels = panels + [swap(p, "owner", 1) for p in panels]
    rows_ordered, panels = lax.optimization_barrier(([rows_in[k] for k in sz.order_rows], panels))
    rows_in = [rows_ordered[sz.order_rows.index(k)] for k in range(sz.seq)]
    (own,) = call(
        gather_kernel,
        "gather_rows",
        [VMEM] * sz.seq,
        [((sz.seq * sz.rows_half, sz.span), bf16, VMEM)],
        ordered(rows_in),
    )
    softmax, raise_picked, scale = call(
        softmax_kernel,
        "softmax_rows",
        [SMEM] + [VMEM] * sz.seq,
        [
            ((sz.group_size * sz.tokens, sz.tokens), bf16, VMEM),
            ((sz.requests * sz.rank, HEAD_SIZE), bf16, VMEM),
            ((sz.tokens, HEAD_SIZE), f32, VMEM),
        ],
        (table, *ordered(rows_in)),
        (
            pltpu.VMEM((sz.group_size, sz.tokens, HEAD_SIZE), bf16),
            pltpu.VMEM((sz.tokens, HEAD_SIZE), bf16),
            pltpu.VMEM((sz.seq * sz.slots_here * sz.rank, HEAD_SIZE), bf16),
        ),
    )

    count = sz.seq * sz.rows_half
    partial_out = call(
        project_kernel,
        "project",
        [SMEM] + [VMEM] * (2 + len(panels)),
        [((2 * count + sz.rank, HEAD_SIZE), bf16, VMEM)] * sz.seq,
        (table, matrix, own, *panels),
        (
            pltpu.VMEM((sz.requests * sz.rank, sz.span), bf16),
            pltpu.VMEM((len(panels) * sz.rank, sz.span), bf16),
            pltpu.VMEM((count, base.shape[1]), bf16),
        ),
    )
    partial_in = [partial_out[0]] + [swap(partial_out[k], "seq", k) for k in around]
    kept, sent = call(
        add_kernel,
        "add_partials",
        [VMEM] * sz.seq,
        [((count + sz.rank, HEAD_SIZE), f32, VMEM)] * 2,
        [partial_in[k] for k in sz.order_sum],
    )
    wide = sz.group_size * HEAD_SIZE
    mixed = call(
        mix_kernel,
        "mix_values",
        [SMEM] + [VMEM] * 5,
        [((sz.rows, wide), bf16, VMEM)] * sz.seq,
        (table, softmax, raise_picked, scale, kept, swap(sent, "owner", 1)),
        (
            pltpu.VMEM((sz.requests * sz.rank, sz.tokens), bf16),
            pltpu.VMEM((sz.tokens, HEAD_SIZE), f32),
            pltpu.VMEM((sz.group_size * sz.tokens, HEAD_SIZE), bf16),
        ),
    )
    mixed_in = [mixed[0]] + [swap(mixed[k], "seq", k) for k in around]
    (result,) = call(
        place_kernel,
        "place_heads",
        [VMEM] * sz.seq,
        [((sz.rows, sz.seq * wide), bf16, VMEM)],
        ordered(mixed_in),
    )
    return result


def broadcast(x, axis, root):
    mine = lax.axis_index(axis) == root
    return lax.psum(jnp.where(mine, x, jnp.zeros_like(x)), axis)


def from_behind(value, axis, steps):
    count = lax.axis_size(axis)
    first, last = (max(0, -steps), min(count, count - steps))
    return lax.ppermute(value, axis, [(source, source + steps) for source in range(first, last)])


def by_tokens(
    layer_input_rows,
    encoded_query_rows,
    encoded_key_rows,
    layer_norm_gain,
    base_value_matrix,
    adapter_down_panels,
    adapter_up_panels,
    request_token_lengths,
    adapter_per_request,
    rank_per_adapter,
    slot_per_adapter,
):
    hidden = layer_input_rows[0]
    row_count = hidden.shape[0]
    seq_now = lax.axis_index("seq")
    owner_now = lax.axis_index("owner")
    reach_count = min(WINDOW // row_count, lax.axis_size("seq") - 1)
    requests = request_token_lengths.shape[0]
    library = slot_per_adapter.shape[0]
    slots_here = adapter_down_panels.shape[1]
    rows_halved = adapter_down_panels.shape[2]
    rank_span_width = adapter_down_panels.shape[3]
    key_value_halved = adapter_up_panels.shape[3]
    group_size = HEADS // KEY_VALUE_HEADS
    request_ends = jnp.cumsum(request_token_lengths)
    position = seq_now * row_count + jnp.arange(row_count, dtype=jnp.int32)
    context = seq_now * row_count + jnp.arange(-reach_count * row_count, row_count, dtype=jnp.int32)
    request_lookup = jnp.sum((position[:, None] >= request_ends[None, :]).astype(jnp.int32), axis=1)
    request_ctx = jnp.sum((context[:, None] >= request_ends[None, :]).astype(jnp.int32), axis=1)
    live_mask = (context[None, :] <= position[:, None]) & (
        context[None, :] > position[:, None] - WINDOW
    )
    live_mask = (
        live_mask & (context[None, :] >= 0) & (request_ctx[None, :] == request_lookup[:, None])
    )
    choose = adapter_per_request[:, None] == jnp.arange(library, dtype=jnp.int32)[None, :]
    slot_of = jnp.sum(jnp.where(choose, slot_per_adapter[None, :], 0), axis=1)
    rank_lookup = jnp.sum(jnp.where(choose, rank_per_adapter[None, :], 0), axis=1)
    scale_lookup = adapter_strength / rank_lookup.astype(jnp.float32)
    in_request = request_lookup[:, None] == jnp.arange(requests, dtype=jnp.int32)[None, :]
    column_live = jnp.arange(rank_span_width, dtype=jnp.int32)[None, :] < rank_lookup[:, None]
    row_gain_weight = jnp.where(in_request, scale_lookup[None, :], jnp.float32(0.0))
    down_panel_here = adapter_down_panels[0]
    up_panel_here = adapter_up_panels[0]
    queries = encoded_query_rows[0]
    keys_own = encoded_key_rows[0]
    key_heads = keys_own.shape[1] // HEAD_SIZE
    wide_rows = hidden.astype(jnp.float32)
    normalized_rows = wide_rows * lax.rsqrt(
        jnp.mean(wide_rows * wide_rows, axis=1, keepdims=True) + norm_eps
    )
    normalized_rows = (normalized_rows * layer_norm_gain[0][None, :]).astype(jnp.bfloat16)
    normed_half = lax.dynamic_slice_in_dim(normalized_rows, owner_now * rows_halved, rows_halved, 1)
    full_value = jnp.dot(
        normalized_rows,
        lax.all_gather(base_value_matrix[0], ("seq", "owner"), axis=0, tiled=True),
        preferred_element_type=jnp.float32,
    )
    value_base_rows = lax.dynamic_slice_in_dim(
        full_value, owner_now * key_value_halved, key_value_halved, 1
    )

    def fetch_one(reduced_rows, request_index):
        owner_slot = slot_of[request_index]
        holder = owner_slot // slots_here
        local_slot = owner_slot % slots_here
        down_local = lax.dynamic_slice_in_dim(down_panel_here, local_slot, 1, 0)
        up_local = lax.dynamic_slice_in_dim(up_panel_here, local_slot, 1, 0)
        down_piece, up_piece = (
            broadcast(down_local, "seq", holder),
            broadcast(up_local, "seq", holder),
        )
        keep_mask = in_request[:, request_index][:, None] & column_live[request_index][None, :]
        matrix_product = jnp.dot(normed_half, down_piece[0], preferred_element_type=jnp.float32)
        return (reduced_rows + jnp.where(keep_mask, matrix_product, jnp.float32(0.0)), up_piece[0])

    start_low = jnp.zeros((row_count, rank_span_width), jnp.float32)
    reduced_rows, panels_up = lax.scan(fetch_one, start_low, jnp.arange(requests, dtype=jnp.int32))
    reduced_rows = lax.psum(reduced_rows, "owner").astype(jnp.bfloat16)
    raised_rows = jnp.einsum(
        "tr,qrk->qtk", reduced_rows, panels_up, preferred_element_type=jnp.float32
    )
    adapter_value = jnp.sum(row_gain_weight.T[:, :, None] * raised_rows, axis=0)
    value_output_rows = (value_base_rows + adapter_value).astype(jnp.bfloat16)
    key_parts = []
    value_parts = []
    for shift_by in range(reach_count, 0, -1):
        key_piece, value_piece = from_behind((keys_own, value_output_rows), "seq", shift_by)
        key_parts.append(key_piece)
        value_parts.append(value_piece)
    keys_all = jnp.concatenate(key_parts + [keys_own], axis=0)
    values_all = jnp.concatenate(value_parts + [value_output_rows], axis=0)
    query_view = queries.reshape(row_count, key_heads, group_size, HEAD_SIZE)
    key_view = keys_all.reshape(-1, key_heads, HEAD_SIZE)
    value_view = values_all.reshape(-1, key_heads, HEAD_SIZE)
    head_outputs = []
    for head_index in range(key_heads):
        query_head = query_view[:, head_index]
        scores = (
            jnp.einsum(
                "tcd,jd->ctj",
                query_head,
                key_view[:, head_index],
                preferred_element_type=jnp.float32,
            )
            * query_scale
        )
        scores = jnp.where(live_mask[None], scores, jnp.float32(-1e30))
        row_max = jnp.max(scores, axis=-1, keepdims=True)
        weights = jnp.exp(scores - row_max)
        row_total = jnp.sum(weights, axis=-1, keepdims=True)
        softmax_rows = (weights / row_total).astype(jnp.bfloat16)
        mixed = jnp.einsum(
            "ctj,jd->tcd",
            softmax_rows,
            value_view[:, head_index],
            preferred_element_type=jnp.float32,
        )
        head_outputs.append(mixed.astype(jnp.bfloat16).reshape(row_count, group_size * HEAD_SIZE))
    result = jnp.concatenate(head_outputs, axis=1)
    return result[None]


def per_device(
    layer_input_rows,
    encoded_query_rows,
    encoded_key_rows,
    layer_norm_gain,
    base_value_matrix,
    adapter_down_panels,
    adapter_up_panels,
    request_token_lengths,
    adapter_per_request,
    rank_per_adapter,
    slot_per_adapter,
):
    sz = Sizes(
        layer_input_rows[0],
        encoded_query_rows[0],
        adapter_down_panels[0],
        adapter_up_panels[0],
        request_token_lengths.shape[0],
    )
    scalars = (request_token_lengths, adapter_per_request, rank_per_adapter, slot_per_adapter)
    if not sz.fits():
        return by_tokens(
            layer_input_rows,
            encoded_query_rows,
            encoded_key_rows,
            layer_norm_gain,
            base_value_matrix,
            adapter_down_panels,
            adapter_up_panels,
            *scalars,
        )
    return by_heads(
        sz,
        layer_input_rows[0],
        encoded_query_rows[0],
        encoded_key_rows[0],
        layer_norm_gain,
        base_value_matrix[0],
        adapter_down_panels[0],
        adapter_up_panels[0],
        *scalars,
    )[None]


def solution(mesh):
    in_specs = (
        P("segment", ("groups", "seq"), None),
        P("segment", ("groups", "seq"), "owner"),
        P("segment", ("groups", "seq"), "owner"),
        P("segment", None),
        P("segment", ("seq", "owner"), None),
        P("segment", "seq", "owner", None),
        P("segment", "seq", None, "owner"),
        P("groups"),
        P("groups"),
        P(),
        P(),
    )
    out_specs = P("segment", ("groups", "seq"), "owner")
    return jax.shard_map(
        per_device, mesh=mesh, in_specs=in_specs, out_specs=out_specs, check_vma=False
    )
```

```python
import functools

import jax
import jax.numpy as jnp
from jax import lax
from jax.experimental import pallas as pl
from jax.experimental.pallas import tpu as pltpu
from jax.sharding import PartitionSpec as P

WINDOW = 1024
HEADS = 16
KEY_VALUE_HEADS = 8
HEAD_SIZE = 128
LANES = 128

query_scale = 168.0 ** (-0.5)
adapter_strength = 32.0
norm_eps = 1e-06

VMEM = pl.BlockSpec(memory_space=pltpu.VMEM)
SMEM = pl.BlockSpec(memory_space=pltpu.SMEM)
ANY = pl.BlockSpec(memory_space=pl.ANY)
HBM = pl.BlockSpec(memory_space=pltpu.HBM)
PARAMS = pltpu.CompilerParams(vmem_limit_bytes=16 * 1024 * 1024)
FIRST = pltpu.CompilerParams(vmem_limit_bytes=60 * 1024 * 1024)
bf16 = jnp.bfloat16
f32 = jnp.float32


def swap(value, axis, mask):
    return lax.ppermute(value, axis, [(i, i ^ mask) for i in range(lax.axis_size(axis))])


class Sizes:
    def __init__(self, x, queries, down, up, requests):
        self.seq = lax.axis_size("seq")
        self.groups = lax.axis_size("groups")
        self.rows = x.shape[0]
        self.rows_half = self.rows // 2
        self.width = x.shape[1]
        self.half = down.shape[1]
        self.side = self.seq // 2
        self.features = self.width // self.seq
        self.slots_here, self.rank = down.shape[0], down.shape[2]
        self.requests = requests
        self.slot_bits = self.slots_here.bit_length() - 1
        self.side_bits = self.side.bit_length() - 1
        self.heads_here = up.shape[2] // HEAD_SIZE
        self.group_size = HEADS // KEY_VALUE_HEADS
        self.tokens = self.rows * self.seq
        rest = list(range(1, self.seq))
        self.order = [0] + rest[::-1]
        self.order_rows = [0] + rest[:1] + rest[:0:-1]
        self.order_sum = [0] + rest[1:2] + rest[:1] + rest[2:]
        tiles = [
            -(-((i * self.features) % LANES + self.features) // LANES) for i in range(self.side)
        ]
        self.tiles = max(tiles)
        self.span = self.tiles * LANES

    def fits(self):
        return (
            lax.axis_size("owner") == 2
            and self.seq >= 4
            and self.seq & (self.seq - 1) == 0
            and self.groups & (self.groups - 1) == 0
            and self.half % LANES == 0
            and self.half * 2 == self.width
            and self.heads_here == self.seq
            and self.slots_here == self.groups
            and self.features % 32 == 0
            and self.rows % 64 == 0
            and self.rank % self.rows_half == 0
            and self.pieces() * LANES <= self.span
            and 2 * self.rank == LANES
            and self.seq * self.rows_half == LANES
        )

    def pieces(self):
        return ((self.group_size + 1) * self.rows + self.slots_here * self.rank) // self.rows_half

    def start_in_half(self, i):
        return jnp.minimum((i * self.features) // LANES, self.half // LANES - self.tiles) * LANES

    def start(self, chip):
        return (chip // self.side) * self.half + self.start_in_half(chip % self.side)


def request_column(sz, table, position):
    found = jnp.zeros_like(position)
    for r in range(sz.requests):
        found = found + (position >= table[0, r]).astype(jnp.int32)
    return found


def token_at(sz, place):
    count = sz.seq * sz.rows_half
    owner = (place >= count).astype(jnp.int32)
    place = place - owner * count
    return place // sz.rows_half * sz.rows + owner * sz.rows_half + place % sz.rows_half


def table_kernel(sz, lengths, adapters, ranks, slots, piece, out, held, sem):
    here, core, group = (lax.axis_index(a) for a in ("seq", "owner", "groups"))
    copy = pltpu.make_async_copy(piece, held, sem)
    copy.start()
    end = jnp.int32(0)
    for r in range(sz.requests):
        end = end + lengths[r]
        adapter = adapters[r]
        slot = slots[adapter]
        chip, local = slot >> sz.slot_bits, slot & (sz.slots_here - 1)
        other = (chip >> sz.side_bits) ^ core
        m = (here ^ chip) & (sz.side - 1)
        out[0, r] = end
        out[1, r] = ranks[adapter]
        out[2, r] = (((other << sz.slot_bits) | (local ^ group)) << sz.side_bits) | m
        out[3, r] = ((here ^ chip) * sz.slots_here + local) * sz.rank
    copy.wait()


def panels_kernel(sz, down, *outs_and_sem):
    outs, sem = outs_and_sem[:-1], outs_and_sem[-1]
    here, group = lax.axis_index("seq"), lax.axis_index("groups")
    copies = []
    for m, out in enumerate(outs):
        first = pl.multiple_of(sz.start_in_half((here % sz.side) ^ m), LANES)
        copies.append(
            pltpu.make_async_copy(down.at[group, :, pl.ds(first, sz.span)], out, sem.at[m])
        )
    for copy in copies:
        copy.start()
    for copy in copies:
        copy.wait()


def norm_kernel(sz, x, gain, queries, keys, up, *outs_and_scratch):
    outs, scratch = outs_and_scratch[: sz.seq], outs_and_scratch[sz.seq :]
    taken, gains, query, key, raised, whole, sem = scratch
    here, core = lax.axis_index("seq"), lax.axis_index("owner")
    place = pl.ds(pl.multiple_of(core * sz.rows_half, sz.rows_half), sz.rows_half)
    pairs = ((x.at[place], taken), (gain, gains), (queries, query), (keys, key), (up, raised))
    copies = [pltpu.make_async_copy(a, b, sem.at[i]) for i, (a, b) in enumerate(pairs)]
    for copy in copies:
        copy.start()
    for copy in copies[:2]:
        copy.wait()
    rows = taken[...].astype(f32)
    rows = rows * lax.rsqrt(jnp.mean(rows * rows, axis=1, keepdims=True) + norm_eps)
    whole[...] = (rows * gains[...]).astype(bf16)
    lane = lax.broadcasted_iota(jnp.int32, (sz.rows_half, sz.span), 1)
    for copy in copies[2:]:
        copy.wait()
    for k, out in enumerate(outs):
        head = here ^ k
        first = pl.multiple_of(sz.start(head), LANES)
        skip = head * sz.features - first
        piece = whole[:, pl.ds(first, sz.span)]
        live = (lane >= skip) & (lane < skip + sz.features)
        out[: sz.rows_half] = jnp.where(live, piece.astype(f32), 0.0).astype(bf16)
        parts = []
        for c in range(sz.group_size):
            first = pl.multiple_of((head * sz.group_size + c) * HEAD_SIZE, HEAD_SIZE)
            parts.append(query[:, pl.ds(first, HEAD_SIZE)])
        first = pl.multiple_of(head * HEAD_SIZE, HEAD_SIZE)
        parts.append(key[:, pl.ds(first, HEAD_SIZE)])
        for j in range(sz.slots_here):
            parts.append(raised[j, :, pl.ds(first, HEAD_SIZE)])
        at = 0
        for part in parts:
            for top in range(0, part.shape[0], sz.rows_half):
                out[sz.rows_half :, at : at + HEAD_SIZE] = part[top : top + sz.rows_half]
                at += HEAD_SIZE
        if at < sz.span:
            out[sz.rows_half :, at:] = jnp.zeros((sz.rows_half, sz.span - at), bf16)


def unpack(sz, piece, out, part, first, size):
    for top in range(0, size, sz.rows_half):
        lanes = slice((part + top // sz.rows_half) * HEAD_SIZE, (part + top // sz.rows_half + 1) * HEAD_SIZE)
        place = pl.ds(pl.multiple_of(first + top, sz.rows_half), sz.rows_half)
        out[place, :] = piece[sz.rows_half :, lanes]


def softmax_kernel(sz, table, *refs):
    pieces, (out, raise_picked, scale, query, key, raise_all) = refs[: sz.seq], refs[sz.seq :]
    here = lax.axis_index("seq")
    parts = sz.rows // sz.rows_half
    for k, piece in zip(sz.order, pieces):
        first = (here ^ k) * sz.rows
        for c in range(sz.group_size):
            unpack(sz, piece, query.at[c], c * parts, first, sz.rows)
        for owner in range(parts):
            place = sz.seq * owner * sz.rows_half + (here ^ k) * sz.rows_half
            unpack(sz, piece, key, sz.group_size * parts + owner, place, sz.rows_half)
        size = sz.slots_here * sz.rank
        unpack(sz, piece, raise_all, (sz.group_size + 1) * parts, k * size, size)
    shape = scale.shape
    request = request_column(sz, table, token_at(sz, lax.broadcasted_iota(jnp.int32, shape, 0)))
    rank_here = jnp.ones(shape, jnp.int32)
    for r in range(sz.requests):
        rank_here = jnp.where(request == r, table[1, r], rank_here)
        first = pl.multiple_of(table[3, r], sz.rank)
        raise_picked[r * sz.rank : (r + 1) * sz.rank] = raise_all[pl.ds(first, sz.rank), :]
    scale[...] = adapter_strength / rank_here.astype(f32)
    shape = (sz.tokens, sz.tokens)
    mine = lax.broadcasted_iota(jnp.int32, shape, 0)
    theirs = token_at(sz, lax.broadcasted_iota(jnp.int32, shape, 1))
    live = (theirs <= mine) & (theirs > mine - WINDOW)
    live = live & (request_column(sz, table, mine) == request_column(sz, table, theirs))
    for c in range(sz.group_size):
        scores = lax.dot_general(
            query[c], key[...], (((1,), (1,)), ((), ())), preferred_element_type=f32
        )
        scores = jnp.where(live, scores * query_scale, -1e30)
        weights = jnp.exp(scores - jnp.max(scores, axis=1, keepdims=True))
        out[c * sz.tokens : (c + 1) * sz.tokens] = (
            weights / jnp.sum(weights, axis=1, keepdims=True)
        ).astype(bf16)


def matrix_kernel(sz, base, base_other, out, sem):
    here, core = lax.axis_index("seq"), lax.axis_index("owner")
    depth, wide = base.shape[0], out.shape[1]
    skip = here * sz.features - sz.start(here)
    spare = sz.span - sz.features
    out[0:spare] = jnp.zeros((spare, wide), bf16)
    out[sz.span - spare :] = jnp.zeros((spare, wide), bf16)
    copies = []
    for j, (ref, owner) in enumerate(((base, core), (base_other, 1 - core))):
        place = pl.ds(pl.multiple_of(skip + owner * depth, 16), depth)
        copies.append(pltpu.make_async_copy(ref, out.at[place], sem.at[j]))
        copies[-1].start()
    for copy in copies:
        copy.wait()


def project_kernel(sz, table, matrix, *refs):
    pieces, refs = refs[: sz.seq], refs[sz.seq :]
    panels, refs = refs[: 2 * sz.groups * sz.side], refs[2 * sz.groups * sz.side :]
    outs, (own, picked, stacked, values) = refs[: sz.seq], refs[sz.seq :]
    here, core = lax.axis_index("seq"), lax.axis_index("owner")
    for k, piece in zip(sz.order, pieces):
        first = pl.multiple_of((here ^ k) * sz.rows_half, sz.rows_half)
        own[pl.ds(first, sz.rows_half), :] = piece[: sz.rows_half]
    for p, panel in enumerate(panels):
        stacked[p * sz.rank : (p + 1) * sz.rank] = panel[...]
    for r in range(sz.requests):
        first = pl.multiple_of(table[2, r] * sz.rank, sz.rank)
        picked[r * sz.rank : (r + 1) * sz.rank] = stacked[pl.ds(first, sz.rank), :]
    values[...] = jnp.dot(own[...], matrix[...], preferred_element_type=f32).astype(bf16)
    low = lax.dot_general(
        picked[...], own[...], (((1,), (1,)), ((), ())), preferred_element_type=f32
    )
    count = sz.seq * sz.rows_half
    shape = (sz.rank, count)
    place = lax.broadcasted_iota(jnp.int32, shape, 1) + core * count
    request = request_column(sz, table, token_at(sz, place))
    rank = lax.broadcasted_iota(jnp.int32, shape, 0)
    reduced = jnp.zeros(shape, f32)
    for r in range(sz.requests):
        live = (request == r) & (rank < table[1, r])
        reduced = jnp.where(live, low[r * sz.rank : (r + 1) * sz.rank], reduced)
    reduced = reduced.astype(bf16)
    for k, out in enumerate(outs):
        for half in range(2):
            first = pl.multiple_of((half * sz.heads_here + (here ^ k)) * HEAD_SIZE, HEAD_SIZE)
            out[half * count : (half + 1) * count] = values[:, pl.ds(first, HEAD_SIZE)]
        out[2 * count :] = reduced


def add_kernel(sz, *refs):
    pieces, (kept, sent) = refs[: sz.seq], refs[sz.seq :]
    core = lax.axis_index("owner")
    count = sz.seq * sz.rows_half
    for out, head in ((kept, core), (sent, 1 - core)):
        place = pl.ds(pl.multiple_of(head * count, count), count)
        out[:count] = sum(piece[place, :].astype(f32) for piece in pieces)
    low = sum(piece[2 * count :].astype(f32) for piece in pieces)
    kept[count:] = low
    sent[count:] = low


def mix_kernel(sz, table, softmax, raise_picked, scale, kept, received, *refs):
    outs, (wide, base, mixed) = refs[: sz.seq], refs[sz.seq :]
    here, core = lax.axis_index("seq"), lax.axis_index("owner")
    count = sz.seq * sz.rows_half
    shape = (sz.rank, count)
    for ref, owner in ((kept, core), (received, 1 - core)):
        first = pl.multiple_of(owner * count, count)
        base[pl.ds(first, count), :] = ref[:count]
        place = lax.broadcasted_iota(jnp.int32, shape, 1) + first
        request = request_column(sz, table, token_at(sz, place))
        for r in range(sz.requests):
            wide[r * sz.rank : (r + 1) * sz.rank, pl.ds(first, count)] = jnp.where(
                request == r, ref[count:], 0.0
            ).astype(bf16)
    raised = lax.dot_general(
        wide[...], raise_picked[...], (((0,), (0,)), ((), ())), preferred_element_type=f32
    )
    values = (base[...] + scale[...] * raised).astype(bf16)
    mixed[...] = jnp.dot(softmax[...], values, preferred_element_type=f32).astype(bf16)
    for k, out in enumerate(outs):
        for c in range(sz.group_size):
            first = pl.multiple_of(c * sz.tokens + (here ^ k) * sz.rows, sz.rows)
            out[:, c * HEAD_SIZE : (c + 1) * HEAD_SIZE] = mixed[pl.ds(first, sz.rows), :]


def place_kernel(sz, *refs):
    pieces, out = refs[: sz.seq], refs[sz.seq]
    here = lax.axis_index("seq")
    wide = sz.group_size * HEAD_SIZE
    for k, piece in zip(sz.order, pieces):
        head = here ^ k
        out[:, pl.ds(pl.multiple_of(head * wide, wide), wide)] = piece[...]


def by_heads(sz, x, queries, keys, gain, base, down, up, lengths, adapters, ranks, slots):
    around = range(1, sz.seq)

    def ordered(values):
        return [values[k] for k in sz.order]

    spread = (2 * sz.rows_half, sz.span)

    def call(kernel, name, ins, outs, args, scratch=(), params=PARAMS):
        return pl.pallas_call(
            functools.partial(kernel, sz),
            out_shape=[jax.ShapeDtypeStruct(shape, dtype) for shape, dtype, _ in outs],
            in_specs=ins,
            out_specs=[spec for _, _, spec in outs],
            scratch_shapes=list(scratch),
            compiler_params=params,
            name=name,
        )(*args)

    panels_out = call(
        panels_kernel,
        "panels_out",
        [HBM],
        [((sz.rank, sz.span), bf16, VMEM)] * sz.side,
        (jnp.swapaxes(down, 1, 2),),
        (pltpu.SemaphoreType.DMA((sz.side,)),),
    )
    panels = []
    for m in range(sz.side):
        pairs = [
            (h * 2 + c, (c * sz.side + ((h % sz.side) ^ m)) * 2 + h // sz.side)
            for h in range(sz.seq)
            for c in range(2)
        ]
        panels.append(lax.ppermute(panels_out[m], ("seq", "owner"), pairs))
    x, _ = lax.optimization_barrier((x, panels_out[0]))
    rows_out = call(
        norm_kernel,
        "norm_rows",
        [HBM] * 5,
        [(spread, bf16, VMEM)] * sz.seq,
        (x, gain, queries, keys, up),
        (
            pltpu.VMEM((sz.rows_half, sz.width), bf16),
            pltpu.VMEM((1, sz.width), f32),
            pltpu.VMEM(queries.shape, bf16),
            pltpu.VMEM(keys.shape, bf16),
            pltpu.VMEM(up.shape, bf16),
            pltpu.VMEM((sz.rows_half, sz.width), bf16),
            pltpu.SemaphoreType.DMA((5,)),
        ),
        FIRST,
    )
    table, held = call(
        table_kernel,
        "table",
        [SMEM] * 4 + [ANY],
        [((4, sz.requests), jnp.int32, SMEM), (spread, bf16, VMEM)],
        (lengths, adapters, ranks, slots, rows_out[0]),
        (pltpu.SemaphoreType.DMA,),
    )
    (matrix,) = call(
        matrix_kernel,
        "matrix_rows",
        [HBM, ANY],
        [((sz.span, base.shape[1]), bf16, VMEM)],
        (base, swap(base, "owner", 1)),
        (pltpu.SemaphoreType.DMA((2,)),),
    )
    rows_in = [held] + [swap(rows_out[k], "seq", k) for k in around]

    panels[0], table, matrix = lax.optimization_barrier((panels[0], table, matrix))
    panels[1], held = lax.optimization_barrier((panels[1], held))
    rows_in[0] = held
    panels = panels + [swap(p, "groups", k) for k in range(1, sz.groups) for p in panels]
    panels = panels + [swap(p, "owner", 1) for p in panels]
    rows_ordered, panels = lax.optimization_barrier(([rows_in[k] for k in sz.order_rows], panels))
    rows_in = [rows_ordered[sz.order_rows.index(k)] for k in range(sz.seq)]
    softmax, raise_picked, scale = call(
        softmax_kernel,
        "softmax_rows",
        [SMEM] + [VMEM] * sz.seq,
        [
            ((sz.group_size * sz.tokens, sz.tokens), bf16, VMEM),
            ((sz.requests * sz.rank, HEAD_SIZE), bf16, VMEM),
            ((sz.tokens, HEAD_SIZE), f32, VMEM),
        ],
        (table, *ordered(rows_in)),
        (
            pltpu.VMEM((sz.group_size, sz.tokens, HEAD_SIZE), bf16),
            pltpu.VMEM((sz.tokens, HEAD_SIZE), bf16),
            pltpu.VMEM((sz.seq * sz.slots_here * sz.rank, HEAD_SIZE), bf16),
        ),
    )

    count = sz.seq * sz.rows_half
    partial_out = call(
        project_kernel,
        "project",
        [SMEM] + [VMEM] * (1 + sz.seq + len(panels)),
        [((2 * count + sz.rank, HEAD_SIZE), bf16, VMEM)] * sz.seq,
        (table, matrix, *ordered(rows_in), *panels),
        (
            pltpu.VMEM((count, sz.span), bf16),
            pltpu.VMEM((sz.requests * sz.rank, sz.span), bf16),
            pltpu.VMEM((len(panels) * sz.rank, sz.span), bf16),
            pltpu.VMEM((count, base.shape[1]), bf16),
        ),
    )
    partial_in = [partial_out[0]] + [swap(partial_out[k], "seq", k) for k in around]
    kept, sent = call(
        add_kernel,
        "add_partials",
        [VMEM] * sz.seq,
        [((count + sz.rank, HEAD_SIZE), f32, VMEM)] * 2,
        [partial_in[k] for k in sz.order_sum],
    )
    wide = sz.group_size * HEAD_SIZE
    mixed = call(
        mix_kernel,
        "mix_values",
        [SMEM] + [VMEM] * 5,
        [((sz.rows, wide), bf16, VMEM)] * sz.seq,
        (table, softmax, raise_picked, scale, kept, swap(sent, "owner", 1)),
        (
            pltpu.VMEM((sz.requests * sz.rank, sz.tokens), bf16),
            pltpu.VMEM((sz.tokens, HEAD_SIZE), f32),
            pltpu.VMEM((sz.group_size * sz.tokens, HEAD_SIZE), bf16),
        ),
    )
    mixed_in = [mixed[0]] + [swap(mixed[k], "seq", k) for k in around]
    (result,) = call(
        place_kernel,
        "place_heads",
        [VMEM] * sz.seq,
        [((sz.rows, sz.seq * wide), bf16, VMEM)],
        ordered(mixed_in),
    )
    return result


def broadcast(x, axis, root):
    mine = lax.axis_index(axis) == root
    return lax.psum(jnp.where(mine, x, jnp.zeros_like(x)), axis)


def from_behind(value, axis, steps):
    count = lax.axis_size(axis)
    first, last = (max(0, -steps), min(count, count - steps))
    return lax.ppermute(value, axis, [(source, source + steps) for source in range(first, last)])


def by_tokens(
    layer_input_rows,
    encoded_query_rows,
    encoded_key_rows,
    layer_norm_gain,
    base_value_matrix,
    adapter_down_panels,
    adapter_up_panels,
    request_token_lengths,
    adapter_per_request,
    rank_per_adapter,
    slot_per_adapter,
):
    hidden = layer_input_rows[0]
    row_count = hidden.shape[0]
    seq_now = lax.axis_index("seq")
    owner_now = lax.axis_index("owner")
    reach_count = min(WINDOW // row_count, lax.axis_size("seq") - 1)
    requests = request_token_lengths.shape[0]
    library = slot_per_adapter.shape[0]
    slots_here = adapter_down_panels.shape[1]
    rows_halved = adapter_down_panels.shape[2]
    rank_span_width = adapter_down_panels.shape[3]
    key_value_halved = adapter_up_panels.shape[3]
    group_size = HEADS // KEY_VALUE_HEADS
    request_ends = jnp.cumsum(request_token_lengths)
    position = seq_now * row_count + jnp.arange(row_count, dtype=jnp.int32)
    context = seq_now * row_count + jnp.arange(-reach_count * row_count, row_count, dtype=jnp.int32)
    request_lookup = jnp.sum((position[:, None] >= request_ends[None, :]).astype(jnp.int32), axis=1)
    request_ctx = jnp.sum((context[:, None] >= request_ends[None, :]).astype(jnp.int32), axis=1)
    live_mask = (context[None, :] <= position[:, None]) & (
        context[None, :] > position[:, None] - WINDOW
    )
    live_mask = (
        live_mask & (context[None, :] >= 0) & (request_ctx[None, :] == request_lookup[:, None])
    )
    choose = adapter_per_request[:, None] == jnp.arange(library, dtype=jnp.int32)[None, :]
    slot_of = jnp.sum(jnp.where(choose, slot_per_adapter[None, :], 0), axis=1)
    rank_lookup = jnp.sum(jnp.where(choose, rank_per_adapter[None, :], 0), axis=1)
    scale_lookup = adapter_strength / rank_lookup.astype(jnp.float32)
    in_request = request_lookup[:, None] == jnp.arange(requests, dtype=jnp.int32)[None, :]
    column_live = jnp.arange(rank_span_width, dtype=jnp.int32)[None, :] < rank_lookup[:, None]
    row_gain_weight = jnp.where(in_request, scale_lookup[None, :], jnp.float32(0.0))
    down_panel_here = adapter_down_panels[0]
    up_panel_here = adapter_up_panels[0]
    queries = encoded_query_rows[0]
    keys_own = encoded_key_rows[0]
    key_heads = keys_own.shape[1] // HEAD_SIZE
    wide_rows = hidden.astype(jnp.float32)
    normalized_rows = wide_rows * lax.rsqrt(
        jnp.mean(wide_rows * wide_rows, axis=1, keepdims=True) + norm_eps
    )
    normalized_rows = (normalized_rows * layer_norm_gain[0][None, :]).astype(jnp.bfloat16)
    normed_half = lax.dynamic_slice_in_dim(normalized_rows, owner_now * rows_halved, rows_halved, 1)
    full_value = jnp.dot(
        normalized_rows,
        lax.all_gather(base_value_matrix[0], ("seq", "owner"), axis=0, tiled=True),
        preferred_element_type=jnp.float32,
    )
    value_base_rows = lax.dynamic_slice_in_dim(
        full_value, owner_now * key_value_halved, key_value_halved, 1
    )

    def fetch_one(reduced_rows, request_index):
        owner_slot = slot_of[request_index]
        holder = owner_slot // slots_here
        local_slot = owner_slot % slots_here
        down_local = lax.dynamic_slice_in_dim(down_panel_here, local_slot, 1, 0)
        up_local = lax.dynamic_slice_in_dim(up_panel_here, local_slot, 1, 0)
        down_piece, up_piece = (
            broadcast(down_local, "seq", holder),
            broadcast(up_local, "seq", holder),
        )
        keep_mask = in_request[:, request_index][:, None] & column_live[request_index][None, :]
        matrix_product = jnp.dot(normed_half, down_piece[0], preferred_element_type=jnp.float32)
        return (reduced_rows + jnp.where(keep_mask, matrix_product, jnp.float32(0.0)), up_piece[0])

    start_low = jnp.zeros((row_count, rank_span_width), jnp.float32)
    reduced_rows, panels_up = lax.scan(fetch_one, start_low, jnp.arange(requests, dtype=jnp.int32))
    reduced_rows = lax.psum(reduced_rows, "owner").astype(jnp.bfloat16)
    raised_rows = jnp.einsum(
        "tr,qrk->qtk", reduced_rows, panels_up, preferred_element_type=jnp.float32
    )
    adapter_value = jnp.sum(row_gain_weight.T[:, :, None] * raised_rows, axis=0)
    value_output_rows = (value_base_rows + adapter_value).astype(jnp.bfloat16)
    key_parts = []
    value_parts = []
    for shift_by in range(reach_count, 0, -1):
        key_piece, value_piece = from_behind((keys_own, value_output_rows), "seq", shift_by)
        key_parts.append(key_piece)
        value_parts.append(value_piece)
    keys_all = jnp.concatenate(key_parts + [keys_own], axis=0)
    values_all = jnp.concatenate(value_parts + [value_output_rows], axis=0)
    query_view = queries.reshape(row_count, key_heads, group_size, HEAD_SIZE)
    key_view = keys_all.reshape(-1, key_heads, HEAD_SIZE)
    value_view = values_all.reshape(-1, key_heads, HEAD_SIZE)
    head_outputs = []
    for head_index in range(key_heads):
        query_head = query_view[:, head_index]
        scores = (
            jnp.einsum(
                "tcd,jd->ctj",
                query_head,
                key_view[:, head_index],
                preferred_element_type=jnp.float32,
            )
            * query_scale
        )
        scores = jnp.where(live_mask[None], scores, jnp.float32(-1e30))
        row_max = jnp.max(scores, axis=-1, keepdims=True)
        weights = jnp.exp(scores - row_max)
        row_total = jnp.sum(weights, axis=-1, keepdims=True)
        softmax_rows = (weights / row_total).astype(jnp.bfloat16)
        mixed = jnp.einsum(
            "ctj,jd->tcd",
            softmax_rows,
            value_view[:, head_index],
            preferred_element_type=jnp.float32,
        )
        head_outputs.append(mixed.astype(jnp.bfloat16).reshape(row_count, group_size * HEAD_SIZE))
    result = jnp.concatenate(head_outputs, axis=1)
    return result[None]


def per_device(
    layer_input_rows,
    encoded_query_rows,
    encoded_key_rows,
    layer_norm_gain,
    base_value_matrix,
    adapter_down_panels,
    adapter_up_panels,
    request_token_lengths,
    adapter_per_request,
    rank_per_adapter,
    slot_per_adapter,
):
    sz = Sizes(
        layer_input_rows[0],
        encoded_query_rows[0],
        adapter_down_panels[0],
        adapter_up_panels[0],
        request_token_lengths.shape[0],
    )
    scalars = (request_token_lengths, adapter_per_request, rank_per_adapter, slot_per_adapter)
    if not sz.fits():
        return by_tokens(
            layer_input_rows,
            encoded_query_rows,
            encoded_key_rows,
            layer_norm_gain,
            base_value_matrix,
            adapter_down_panels,
            adapter_up_panels,
            *scalars,
        )
    return by_heads(
        sz,
        layer_input_rows[0],
        encoded_query_rows[0],
        encoded_key_rows[0],
        layer_norm_gain,
        base_value_matrix[0],
        adapter_down_panels[0],
        adapter_up_panels[0],
        *scalars,
    )[None]


def solution(mesh):
    in_specs = (
        P("segment", ("groups", "seq"), None),
        P("segment", ("groups", "seq"), "owner"),
        P("segment", ("groups", "seq"), "owner"),
        P("segment", None),
        P("segment", ("seq", "owner"), None),
        P("segment", "seq", "owner", None),
        P("segment", "seq", None, "owner"),
        P("groups"),
        P("groups"),
        P(),
        P(),
    )
    out_specs = P("segment", ("groups", "seq"), "owner")
    return jax.shard_map(
        per_device, mesh=mesh, in_specs=in_specs, out_specs=out_specs, check_vma=False
    )
```

```python
import functools

import jax
import jax.numpy as jnp
from jax import lax
from jax.experimental import pallas as pl
from jax.experimental.pallas import tpu as pltpu
from jax.sharding import PartitionSpec as P

WINDOW = 1024
HEADS = 16
KEY_VALUE_HEADS = 8
HEAD_SIZE = 128
LANES = 128

query_scale = 168.0 ** (-0.5)
adapter_strength = 32.0
norm_eps = 1e-06

VMEM = pl.BlockSpec(memory_space=pltpu.VMEM)
SMEM = pl.BlockSpec(memory_space=pltpu.SMEM)
ANY = pl.BlockSpec(memory_space=pl.ANY)
HBM = pl.BlockSpec(memory_space=pltpu.HBM)
PARAMS = pltpu.CompilerParams(vmem_limit_bytes=16 * 1024 * 1024)
FIRST = pltpu.CompilerParams(vmem_limit_bytes=60 * 1024 * 1024)
SLOT = pltpu.CompilerParams(vmem_limit_bytes=107 * 512 * 1024)
bf16 = jnp.bfloat16
f32 = jnp.float32


def swap(value, axis, mask):
    return lax.ppermute(value, axis, [(i, i ^ mask) for i in range(lax.axis_size(axis))])


class Sizes:
    def __init__(self, x, queries, down, up, requests):
        self.seq = lax.axis_size("seq")
        self.groups = lax.axis_size("groups")
        self.rows = x.shape[0]
        self.rows_half = self.rows // 2
        self.width = x.shape[1]
        self.half = down.shape[1]
        self.side = self.seq // 2
        self.features = self.width // self.seq
        self.slots_here, self.rank = down.shape[0], down.shape[2]
        self.requests = requests
        self.slot_bits = self.slots_here.bit_length() - 1
        self.side_bits = self.side.bit_length() - 1
        self.heads_here = up.shape[2] // HEAD_SIZE
        self.group_size = HEADS // KEY_VALUE_HEADS
        self.tokens = self.rows * self.seq
        rest = list(range(1, self.seq))
        self.order = [0] + rest[::-1]
        self.order_rows = [0] + rest[:1] + rest[:0:-1]
        self.order_sum = [0] + rest[1:2] + rest[:1] + rest[2:]
        tiles = [
            -(-((i * self.features) % LANES + self.features) // LANES) for i in range(self.side)
        ]
        self.tiles = max(tiles)
        self.span = self.tiles * LANES

    def fits(self):
        return (
            lax.axis_size("owner") == 2
            and self.seq >= 4
            and self.seq & (self.seq - 1) == 0
            and self.groups & (self.groups - 1) == 0
            and self.half % LANES == 0
            and self.half * 2 == self.width
            and self.heads_here == self.seq
            and self.slots_here == self.groups
            and self.features % 32 == 0
            and self.rows % 64 == 0
            and self.rank % self.rows_half == 0
            and self.pieces() * LANES <= self.span
            and 2 * self.rank == LANES
            and self.seq * self.rows_half == LANES
        )

    def pieces(self):
        return ((self.group_size + 1) * self.rows + self.slots_here * self.rank) // self.rows_half

    def start_in_half(self, i):
        return jnp.minimum((i * self.features) // LANES, self.half // LANES - self.tiles) * LANES

    def start(self, chip):
        return (chip // self.side) * self.half + self.start_in_half(chip % self.side)


def request_column(sz, table, position):
    found = jnp.zeros_like(position)
    for r in range(sz.requests):
        found = found + (position >= table[0, r]).astype(jnp.int32)
    return found


def token_at(sz, place):
    count = sz.seq * sz.rows_half
    owner = (place >= count).astype(jnp.int32)
    place = place - owner * count
    return place // sz.rows_half * sz.rows + owner * sz.rows_half + place % sz.rows_half


def table_kernel(sz, lengths, adapters, ranks, slots, piece, out, held, sem):
    here, core, group = (lax.axis_index(a) for a in ("seq", "owner", "groups"))
    copy = pltpu.make_async_copy(piece, held, sem)
    copy.start()
    end = jnp.int32(0)
    for r in range(sz.requests):
        end = end + lengths[r]
        adapter = adapters[r]
        slot = slots[adapter]
        chip, local = slot >> sz.slot_bits, slot & (sz.slots_here - 1)
        other = (chip >> sz.side_bits) ^ core
        m = (here ^ chip) & (sz.side - 1)
        out[0, r] = end
        out[1, r] = ranks[adapter]
        out[2, r] = (((other << sz.slot_bits) | (local ^ group)) << sz.side_bits) | m
        out[3, r] = ((here ^ chip) * sz.slots_here + local) * sz.rank
    copy.wait()


def panels_kernel(sz, down, *outs_and_sem):
    outs, sem = outs_and_sem[:-1], outs_and_sem[-1]
    here, group = lax.axis_index("seq"), lax.axis_index("groups")
    copies = []
    for m, out in enumerate(outs):
        first = pl.multiple_of(sz.start_in_half((here % sz.side) ^ m), LANES)
        copies.append(
            pltpu.make_async_copy(down.at[group, :, pl.ds(first, sz.span)], out, sem.at[m])
        )
    for copy in copies:
        copy.start()
    for copy in copies:
        copy.wait()


def norm_kernel(sz, x, gain, queries, keys, up, *outs_and_scratch):
    outs, scratch = outs_and_scratch[: sz.seq], outs_and_scratch[sz.seq :]
    taken, gains, query, key, raised, whole, sem = scratch
    here, core = lax.axis_index("seq"), lax.axis_index("owner")
    place = pl.ds(pl.multiple_of(core * sz.rows_half, sz.rows_half), sz.rows_half)
    pairs = ((x.at[place], taken), (gain, gains), (queries, query), (keys, key), (up, raised))
    copies = [pltpu.make_async_copy(a, b, sem.at[i]) for i, (a, b) in enumerate(pairs)]
    for copy in copies:
        copy.start()
    for copy in copies[:2]:
        copy.wait()
    rows = taken[...].astype(f32)
    rows = rows * lax.rsqrt(jnp.mean(rows * rows, axis=1, keepdims=True) + norm_eps)
    whole[...] = (rows * gains[...]).astype(bf16)
    lane = lax.broadcasted_iota(jnp.int32, (sz.rows_half, sz.span), 1)
    for copy in copies[2:]:
        copy.wait()
    for k, out in enumerate(outs):
        head = here ^ k
        first = pl.multiple_of(sz.start(head), LANES)
        skip = head * sz.features - first
        piece = whole[:, pl.ds(first, sz.span)]
        live = (lane >= skip) & (lane < skip + sz.features)
        out[: sz.rows_half] = jnp.where(live, piece.astype(f32), 0.0).astype(bf16)
        parts = []
        for c in range(sz.group_size):
            first = pl.multiple_of((head * sz.group_size + c) * HEAD_SIZE, HEAD_SIZE)
            parts.append(query[:, pl.ds(first, HEAD_SIZE)])
        first = pl.multiple_of(head * HEAD_SIZE, HEAD_SIZE)
        parts.append(key[:, pl.ds(first, HEAD_SIZE)])
        for j in range(sz.slots_here):
            parts.append(raised[j, :, pl.ds(first, HEAD_SIZE)])
        at = 0
        for part in parts:
            for top in range(0, part.shape[0], sz.rows_half):
                out[sz.rows_half :, at : at + HEAD_SIZE] = part[top : top + sz.rows_half]
                at += HEAD_SIZE
        if at < sz.span:
            out[sz.rows_half :, at:] = jnp.zeros((sz.rows_half, sz.span - at), bf16)


def unpack(sz, piece, out, part, first, size):
    for top in range(0, size, sz.rows_half):
        lanes = slice((part + top // sz.rows_half) * HEAD_SIZE, (part + top // sz.rows_half + 1) * HEAD_SIZE)
        place = pl.ds(pl.multiple_of(first + top, sz.rows_half), sz.rows_half)
        out[place, :] = piece[sz.rows_half :, lanes]


def softmax_kernel(sz, table, *refs):
    pieces, (out, raise_picked, scale, query, key, raise_all) = refs[: sz.seq], refs[sz.seq :]
    here = lax.axis_index("seq")
    parts = sz.rows // sz.rows_half
    for k, piece in zip(sz.order, pieces):
        first = (here ^ k) * sz.rows
        for c in range(sz.group_size):
            unpack(sz, piece, query.at[c], c * parts, first, sz.rows)
        for owner in range(parts):
            place = sz.seq * owner * sz.rows_half + (here ^ k) * sz.rows_half
            unpack(sz, piece, key, sz.group_size * parts + owner, place, sz.rows_half)
        size = sz.slots_here * sz.rank
        unpack(sz, piece, raise_all, (sz.group_size + 1) * parts, k * size, size)
    shape = scale.shape
    request = request_column(sz, table, token_at(sz, lax.broadcasted_iota(jnp.int32, shape, 0)))
    rank_here = jnp.ones(shape, jnp.int32)
    for r in range(sz.requests):
        rank_here = jnp.where(request == r, table[1, r], rank_here)
        first = pl.multiple_of(table[3, r], sz.rank)
        raise_picked[r * sz.rank : (r + 1) * sz.rank] = raise_all[pl.ds(first, sz.rank), :]
    scale[...] = adapter_strength / rank_here.astype(f32)
    shape = (sz.tokens, sz.tokens)
    mine = lax.broadcasted_iota(jnp.int32, shape, 0)
    theirs = token_at(sz, lax.broadcasted_iota(jnp.int32, shape, 1))
    live = (theirs <= mine) & (theirs > mine - WINDOW)
    live = live & (request_column(sz, table, mine) == request_column(sz, table, theirs))
    for c in range(sz.group_size):
        scores = lax.dot_general(
            query[c], key[...], (((1,), (1,)), ((), ())), preferred_element_type=f32
        )
        scores = jnp.where(live, scores * query_scale, -1e30)
        weights = jnp.exp(scores - jnp.max(scores, axis=1, keepdims=True))
        out[c * sz.tokens : (c + 1) * sz.tokens] = (
            weights / jnp.sum(weights, axis=1, keepdims=True)
        ).astype(bf16)


def matrix_kernel(sz, base, base_other, out, sem):
    here, core = lax.axis_index("seq"), lax.axis_index("owner")
    depth, wide = base.shape[0], out.shape[1]
    skip = here * sz.features - sz.start(here)
    spare = sz.span - sz.features
    out[0:spare] = jnp.zeros((spare, wide), bf16)
    out[sz.span - spare :] = jnp.zeros((spare, wide), bf16)
    copies = []
    for j, (ref, owner) in enumerate(((base, core), (base_other, 1 - core))):
        place = pl.ds(pl.multiple_of(skip + owner * depth, 16), depth)
        copies.append(pltpu.make_async_copy(ref, out.at[place], sem.at[j]))
        copies[-1].start()
    for copy in copies:
        copy.wait()


def project_kernel(sz, table, matrix, *refs):
    pieces, refs = refs[: sz.seq], refs[sz.seq :]
    panels, refs = refs[: 2 * sz.groups * sz.side], refs[2 * sz.groups * sz.side :]
    outs, (own, picked, stacked, values) = refs[: sz.seq], refs[sz.seq :]
    here, core = lax.axis_index("seq"), lax.axis_index("owner")
    for k, piece in zip(sz.order, pieces):
        first = pl.multiple_of((here ^ k) * sz.rows_half, sz.rows_half)
        own[pl.ds(first, sz.rows_half), :] = piece[: sz.rows_half]
    for p, panel in enumerate(panels):
        stacked[p * sz.rank : (p + 1) * sz.rank] = panel[...]
    for r in range(sz.requests):
        first = pl.multiple_of(table[2, r] * sz.rank, sz.rank)
        picked[r * sz.rank : (r + 1) * sz.rank] = stacked[pl.ds(first, sz.rank), :]
    values[...] = jnp.dot(own[...], matrix[...], preferred_element_type=f32).astype(bf16)
    low = lax.dot_general(
        picked[...], own[...], (((1,), (1,)), ((), ())), preferred_element_type=f32
    )
    count = sz.seq * sz.rows_half
    shape = (sz.rank, count)
    place = lax.broadcasted_iota(jnp.int32, shape, 1) + core * count
    request = request_column(sz, table, token_at(sz, place))
    rank = lax.broadcasted_iota(jnp.int32, shape, 0)
    reduced = jnp.zeros(shape, f32)
    for r in range(sz.requests):
        live = (request == r) & (rank < table[1, r])
        reduced = jnp.where(live, low[r * sz.rank : (r + 1) * sz.rank], reduced)
    reduced = reduced.astype(bf16)
    for k, out in enumerate(outs):
        for half in range(2):
            first = pl.multiple_of((half * sz.heads_here + (here ^ k)) * HEAD_SIZE, HEAD_SIZE)
            out[half * count : (half + 1) * count] = values[:, pl.ds(first, HEAD_SIZE)]
        out[2 * count :] = reduced


def add_kernel(sz, *refs):
    pieces, (kept, sent) = refs[: sz.seq], refs[sz.seq :]
    core = lax.axis_index("owner")
    count = sz.seq * sz.rows_half
    for out, head in ((kept, core), (sent, 1 - core)):
        place = pl.ds(pl.multiple_of(head * count, count), count)
        out[:count] = sum(piece[place, :].astype(f32) for piece in pieces)
    low = sum(piece[2 * count :].astype(f32) for piece in pieces)
    kept[count:] = low
    sent[count:] = low


def mix_kernel(sz, table, softmax, raise_picked, scale, kept, received, *refs):
    outs, (wide, base, mixed) = refs[: sz.seq], refs[sz.seq :]
    here, core = lax.axis_index("seq"), lax.axis_index("owner")
    count = sz.seq * sz.rows_half
    shape = (sz.rank, count)
    for ref, owner in ((kept, core), (received, 1 - core)):
        first = pl.multiple_of(owner * count, count)
        base[pl.ds(first, count), :] = ref[:count]
        place = lax.broadcasted_iota(jnp.int32, shape, 1) + first
        request = request_column(sz, table, token_at(sz, place))
        for r in range(sz.requests):
            wide[r * sz.rank : (r + 1) * sz.rank, pl.ds(first, count)] = jnp.where(
                request == r, ref[count:], 0.0
            ).astype(bf16)
    raised = lax.dot_general(
        wide[...], raise_picked[...], (((0,), (0,)), ((), ())), preferred_element_type=f32
    )
    values = (base[...] + scale[...] * raised).astype(bf16)
    mixed[...] = jnp.dot(softmax[...], values, preferred_element_type=f32).astype(bf16)
    for k, out in enumerate(outs):
        for c in range(sz.group_size):
            first = pl.multiple_of(c * sz.tokens + (here ^ k) * sz.rows, sz.rows)
            out[:, c * HEAD_SIZE : (c + 1) * HEAD_SIZE] = mixed[pl.ds(first, sz.rows), :]


def place_kernel(sz, *refs):
    pieces, out = refs[: sz.seq], refs[sz.seq]
    here = lax.axis_index("seq")
    wide = sz.group_size * HEAD_SIZE
    for k, piece in zip(sz.order, pieces):
        head = here ^ k
        out[:, pl.ds(pl.multiple_of(head * wide, wide), wide)] = piece[...]


def by_heads(sz, x, queries, keys, gain, base, down, up, lengths, adapters, ranks, slots):
    around = range(1, sz.seq)

    def ordered(values):
        return [values[k] for k in sz.order]

    spread = (2 * sz.rows_half, sz.span)

    def call(kernel, name, ins, outs, args, scratch=(), params=PARAMS):
        return pl.pallas_call(
            functools.partial(kernel, sz),
            out_shape=[jax.ShapeDtypeStruct(shape, dtype) for shape, dtype, _ in outs],
            in_specs=ins,
            out_specs=[spec for _, _, spec in outs],
            scratch_shapes=list(scratch),
            compiler_params=params,
            name=name,
        )(*args)

    panels_out = call(
        panels_kernel,
        "panels_out",
        [HBM],
        [((sz.rank, sz.span), bf16, VMEM)] * sz.side,
        (jnp.swapaxes(down, 1, 2),),
        (pltpu.SemaphoreType.DMA((sz.side,)),),
        SLOT,
    )
    panels = []
    for m in range(sz.side):
        pairs = [
            (h * 2 + c, (c * sz.side + ((h % sz.side) ^ m)) * 2 + h // sz.side)
            for h in range(sz.seq)
            for c in range(2)
        ]
        panels.append(lax.ppermute(panels_out[m], ("seq", "owner"), pairs))
    x, _ = lax.optimization_barrier((x, panels_out[0]))
    rows_out = call(
        norm_kernel,
        "norm_rows",
        [HBM] * 5,
        [(spread, bf16, VMEM)] * sz.seq,
        (x, gain, queries, keys, up),
        (
            pltpu.VMEM((sz.rows_half, sz.width), bf16),
            pltpu.VMEM((1, sz.width), f32),
            pltpu.VMEM(queries.shape, bf16),
            pltpu.VMEM(keys.shape, bf16),
            pltpu.VMEM(up.shape, bf16),
            pltpu.VMEM((sz.rows_half, sz.width), bf16),
            pltpu.SemaphoreType.DMA((5,)),
        ),
        FIRST,
    )
    table, held = call(
        table_kernel,
        "table",
        [SMEM] * 4 + [ANY],
        [((4, sz.requests), jnp.int32, SMEM), (spread, bf16, VMEM)],
        (lengths, adapters, ranks, slots, rows_out[0]),
        (pltpu.SemaphoreType.DMA,),
    )
    (matrix,) = call(
        matrix_kernel,
        "matrix_rows",
        [HBM, ANY],
        [((sz.span, base.shape[1]), bf16, VMEM)],
        (base, swap(base, "owner", 1)),
        (pltpu.SemaphoreType.DMA((2,)),),
    )
    rows_in = [held] + [swap(rows_out[k], "seq", k) for k in around]

    panels[0], table, matrix = lax.optimization_barrier((panels[0], table, matrix))
    panels[1], held = lax.optimization_barrier((panels[1], held))
    rows_in[0] = held
    panels = panels + [swap(p, "groups", k) for k in range(1, sz.groups) for p in panels]
    panels = panels + [swap(p, "owner", 1) for p in panels]
    rows_ordered, panels = lax.optimization_barrier(([rows_in[k] for k in sz.order_rows], panels))
    rows_in = [rows_ordered[sz.order_rows.index(k)] for k in range(sz.seq)]
    softmax, raise_picked, scale = call(
        softmax_kernel,
        "softmax_rows",
        [SMEM] + [VMEM] * sz.seq,
        [
            ((sz.group_size * sz.tokens, sz.tokens), bf16, VMEM),
            ((sz.requests * sz.rank, HEAD_SIZE), bf16, VMEM),
            ((sz.tokens, HEAD_SIZE), f32, VMEM),
        ],
        (table, *ordered(rows_in)),
        (
            pltpu.VMEM((sz.group_size, sz.tokens, HEAD_SIZE), bf16),
            pltpu.VMEM((sz.tokens, HEAD_SIZE), bf16),
            pltpu.VMEM((sz.seq * sz.slots_here * sz.rank, HEAD_SIZE), bf16),
        ),
    )

    count = sz.seq * sz.rows_half
    partial_out = call(
        project_kernel,
        "project",
        [SMEM] + [VMEM] * (1 + sz.seq + len(panels)),
        [((2 * count + sz.rank, HEAD_SIZE), bf16, VMEM)] * sz.seq,
        (table, matrix, *ordered(rows_in), *panels),
        (
            pltpu.VMEM((count, sz.span), bf16),
            pltpu.VMEM((sz.requests * sz.rank, sz.span), bf16),
            pltpu.VMEM((len(panels) * sz.rank, sz.span), bf16),
            pltpu.VMEM((count, base.shape[1]), bf16),
        ),
    )
    partial_in = [partial_out[0]] + [swap(partial_out[k], "seq", k) for k in around]
    kept, sent = call(
        add_kernel,
        "add_partials",
        [VMEM] * sz.seq,
        [((count + sz.rank, HEAD_SIZE), f32, VMEM)] * 2,
        [partial_in[k] for k in sz.order_sum],
    )
    wide = sz.group_size * HEAD_SIZE
    mixed = call(
        mix_kernel,
        "mix_values",
        [SMEM] + [VMEM] * 5,
        [((sz.rows, wide), bf16, VMEM)] * sz.seq,
        (table, softmax, raise_picked, scale, kept, swap(sent, "owner", 1)),
        (
            pltpu.VMEM((sz.requests * sz.rank, sz.tokens), bf16),
            pltpu.VMEM((sz.tokens, HEAD_SIZE), f32),
            pltpu.VMEM((sz.group_size * sz.tokens, HEAD_SIZE), bf16),
        ),
    )
    mixed_in = [mixed[0]] + [swap(mixed[k], "seq", k) for k in around]
    (result,) = call(
        place_kernel,
        "place_heads",
        [VMEM] * sz.seq,
        [((sz.rows, sz.seq * wide), bf16, VMEM)],
        ordered(mixed_in),
    )
    return result


def broadcast(x, axis, root):
    mine = lax.axis_index(axis) == root
    return lax.psum(jnp.where(mine, x, jnp.zeros_like(x)), axis)


def from_behind(value, axis, steps):
    count = lax.axis_size(axis)
    first, last = (max(0, -steps), min(count, count - steps))
    return lax.ppermute(value, axis, [(source, source + steps) for source in range(first, last)])


def by_tokens(
    layer_input_rows,
    encoded_query_rows,
    encoded_key_rows,
    layer_norm_gain,
    base_value_matrix,
    adapter_down_panels,
    adapter_up_panels,
    request_token_lengths,
    adapter_per_request,
    rank_per_adapter,
    slot_per_adapter,
):
    hidden = layer_input_rows[0]
    row_count = hidden.shape[0]
    seq_now = lax.axis_index("seq")
    owner_now = lax.axis_index("owner")
    reach_count = min(WINDOW // row_count, lax.axis_size("seq") - 1)
    requests = request_token_lengths.shape[0]
    library = slot_per_adapter.shape[0]
    slots_here = adapter_down_panels.shape[1]
    rows_halved = adapter_down_panels.shape[2]
    rank_span_width = adapter_down_panels.shape[3]
    key_value_halved = adapter_up_panels.shape[3]
    group_size = HEADS // KEY_VALUE_HEADS
    request_ends = jnp.cumsum(request_token_lengths)
    position = seq_now * row_count + jnp.arange(row_count, dtype=jnp.int32)
    context = seq_now * row_count + jnp.arange(-reach_count * row_count, row_count, dtype=jnp.int32)
    request_lookup = jnp.sum((position[:, None] >= request_ends[None, :]).astype(jnp.int32), axis=1)
    request_ctx = jnp.sum((context[:, None] >= request_ends[None, :]).astype(jnp.int32), axis=1)
    live_mask = (context[None, :] <= position[:, None]) & (
        context[None, :] > position[:, None] - WINDOW
    )
    live_mask = (
        live_mask & (context[None, :] >= 0) & (request_ctx[None, :] == request_lookup[:, None])
    )
    choose = adapter_per_request[:, None] == jnp.arange(library, dtype=jnp.int32)[None, :]
    slot_of = jnp.sum(jnp.where(choose, slot_per_adapter[None, :], 0), axis=1)
    rank_lookup = jnp.sum(jnp.where(choose, rank_per_adapter[None, :], 0), axis=1)
    scale_lookup = adapter_strength / rank_lookup.astype(jnp.float32)
    in_request = request_lookup[:, None] == jnp.arange(requests, dtype=jnp.int32)[None, :]
    column_live = jnp.arange(rank_span_width, dtype=jnp.int32)[None, :] < rank_lookup[:, None]
    row_gain_weight = jnp.where(in_request, scale_lookup[None, :], jnp.float32(0.0))
    down_panel_here = adapter_down_panels[0]
    up_panel_here = adapter_up_panels[0]
    queries = encoded_query_rows[0]
    keys_own = encoded_key_rows[0]
    key_heads = keys_own.shape[1] // HEAD_SIZE
    wide_rows = hidden.astype(jnp.float32)
    normalized_rows = wide_rows * lax.rsqrt(
        jnp.mean(wide_rows * wide_rows, axis=1, keepdims=True) + norm_eps
    )
    normalized_rows = (normalized_rows * layer_norm_gain[0][None, :]).astype(jnp.bfloat16)
    normed_half = lax.dynamic_slice_in_dim(normalized_rows, owner_now * rows_halved, rows_halved, 1)
    full_value = jnp.dot(
        normalized_rows,
        lax.all_gather(base_value_matrix[0], ("seq", "owner"), axis=0, tiled=True),
        preferred_element_type=jnp.float32,
    )
    value_base_rows = lax.dynamic_slice_in_dim(
        full_value, owner_now * key_value_halved, key_value_halved, 1
    )

    def fetch_one(reduced_rows, request_index):
        owner_slot = slot_of[request_index]
        holder = owner_slot // slots_here
        local_slot = owner_slot % slots_here
        down_local = lax.dynamic_slice_in_dim(down_panel_here, local_slot, 1, 0)
        up_local = lax.dynamic_slice_in_dim(up_panel_here, local_slot, 1, 0)
        down_piece, up_piece = (
            broadcast(down_local, "seq", holder),
            broadcast(up_local, "seq", holder),
        )
        keep_mask = in_request[:, request_index][:, None] & column_live[request_index][None, :]
        matrix_product = jnp.dot(normed_half, down_piece[0], preferred_element_type=jnp.float32)
        return (reduced_rows + jnp.where(keep_mask, matrix_product, jnp.float32(0.0)), up_piece[0])

    start_low = jnp.zeros((row_count, rank_span_width), jnp.float32)
    reduced_rows, panels_up = lax.scan(fetch_one, start_low, jnp.arange(requests, dtype=jnp.int32))
    reduced_rows = lax.psum(reduced_rows, "owner").astype(jnp.bfloat16)
    raised_rows = jnp.einsum(
        "tr,qrk->qtk", reduced_rows, panels_up, preferred_element_type=jnp.float32
    )
    adapter_value = jnp.sum(row_gain_weight.T[:, :, None] * raised_rows, axis=0)
    value_output_rows = (value_base_rows + adapter_value).astype(jnp.bfloat16)
    key_parts = []
    value_parts = []
    for shift_by in range(reach_count, 0, -1):
        key_piece, value_piece = from_behind((keys_own, value_output_rows), "seq", shift_by)
        key_parts.append(key_piece)
        value_parts.append(value_piece)
    keys_all = jnp.concatenate(key_parts + [keys_own], axis=0)
    values_all = jnp.concatenate(value_parts + [value_output_rows], axis=0)
    query_view = queries.reshape(row_count, key_heads, group_size, HEAD_SIZE)
    key_view = keys_all.reshape(-1, key_heads, HEAD_SIZE)
    value_view = values_all.reshape(-1, key_heads, HEAD_SIZE)
    head_outputs = []
    for head_index in range(key_heads):
        query_head = query_view[:, head_index]
        scores = (
            jnp.einsum(
                "tcd,jd->ctj",
                query_head,
                key_view[:, head_index],
                preferred_element_type=jnp.float32,
            )
            * query_scale
        )
        scores = jnp.where(live_mask[None], scores, jnp.float32(-1e30))
        row_max = jnp.max(scores, axis=-1, keepdims=True)
        weights = jnp.exp(scores - row_max)
        row_total = jnp.sum(weights, axis=-1, keepdims=True)
        softmax_rows = (weights / row_total).astype(jnp.bfloat16)
        mixed = jnp.einsum(
            "ctj,jd->tcd",
            softmax_rows,
            value_view[:, head_index],
            preferred_element_type=jnp.float32,
        )
        head_outputs.append(mixed.astype(jnp.bfloat16).reshape(row_count, group_size * HEAD_SIZE))
    result = jnp.concatenate(head_outputs, axis=1)
    return result[None]


def per_device(
    layer_input_rows,
    encoded_query_rows,
    encoded_key_rows,
    layer_norm_gain,
    base_value_matrix,
    adapter_down_panels,
    adapter_up_panels,
    request_token_lengths,
    adapter_per_request,
    rank_per_adapter,
    slot_per_adapter,
):
    sz = Sizes(
        layer_input_rows[0],
        encoded_query_rows[0],
        adapter_down_panels[0],
        adapter_up_panels[0],
        request_token_lengths.shape[0],
    )
    scalars = (request_token_lengths, adapter_per_request, rank_per_adapter, slot_per_adapter)
    if not sz.fits():
        return by_tokens(
            layer_input_rows,
            encoded_query_rows,
            encoded_key_rows,
            layer_norm_gain,
            base_value_matrix,
            adapter_down_panels,
            adapter_up_panels,
            *scalars,
        )
    return by_heads(
        sz,
        layer_input_rows[0],
        encoded_query_rows[0],
        encoded_key_rows[0],
        layer_norm_gain,
        base_value_matrix[0],
        adapter_down_panels[0],
        adapter_up_panels[0],
        *scalars,
    )[None]


def solution(mesh):
    in_specs = (
        P("segment", ("groups", "seq"), None),
        P("segment", ("groups", "seq"), "owner"),
        P("segment", ("groups", "seq"), "owner"),
        P("segment", None),
        P("segment", ("seq", "owner"), None),
        P("segment", "seq", "owner", None),
        P("segment", "seq", None, "owner"),
        P("groups"),
        P("groups"),
        P(),
        P(),
    )
    out_specs = P("segment", ("groups", "seq"), "owner")
    return jax.shard_map(
        per_device, mesh=mesh, in_specs=in_specs, out_specs=out_specs, check_vma=False
    )
```

```python
import functools

import jax
import jax.numpy as jnp
from jax import lax
from jax.experimental import pallas as pl
from jax.experimental.pallas import tpu as pltpu
from jax.sharding import PartitionSpec as P

WINDOW = 1024
HEADS = 16
KEY_VALUE_HEADS = 8
HEAD_SIZE = 128
LANES = 128

query_scale = 168.0 ** (-0.5)
adapter_strength = 32.0
norm_eps = 1e-06

VMEM = pl.BlockSpec(memory_space=pltpu.VMEM)
SMEM = pl.BlockSpec(memory_space=pltpu.SMEM)
ANY = pl.BlockSpec(memory_space=pl.ANY)
HBM = pl.BlockSpec(memory_space=pltpu.HBM)
PARAMS = pltpu.CompilerParams(vmem_limit_bytes=16 * 1024 * 1024)
FIRST = pltpu.CompilerParams(vmem_limit_bytes=60 * 1024 * 1024)
bf16 = jnp.bfloat16
f32 = jnp.float32


def swap(value, axis, mask):
    return lax.ppermute(value, axis, [(i, i ^ mask) for i in range(lax.axis_size(axis))])


class Sizes:
    def __init__(self, x, queries, down, up, requests):
        self.seq = lax.axis_size("seq")
        self.groups = lax.axis_size("groups")
        self.rows = x.shape[0]
        self.rows_half = self.rows // 2
        self.width = x.shape[1]
        self.half = down.shape[1]
        self.side = self.seq // 2
        self.features = self.width // self.seq
        self.slots_here, self.rank = down.shape[0], down.shape[2]
        self.requests = requests
        self.slot_bits = self.slots_here.bit_length() - 1
        self.side_bits = self.side.bit_length() - 1
        self.heads_here = up.shape[2] // HEAD_SIZE
        self.group_size = HEADS // KEY_VALUE_HEADS
        self.tokens = self.rows * self.seq
        rest = list(range(1, self.seq))
        self.order = [0] + rest[::-1]
        self.order_rows = [0] + rest[:1] + rest[:0:-1]
        self.order_sum = [0] + rest[-1:] + rest[:-1]
        tiles = [
            -(-((i * self.features) % LANES + self.features) // LANES) for i in range(self.side)
        ]
        self.tiles = max(tiles)
        self.span = self.tiles * LANES

    def fits(self):
        return (
            lax.axis_size("owner") == 2
            and self.seq >= 4
            and self.seq & (self.seq - 1) == 0
            and self.groups & (self.groups - 1) == 0
            and self.half % LANES == 0
            and self.half * 2 == self.width
            and self.heads_here == self.seq
            and self.slots_here == self.groups
            and self.features % 32 == 0
            and self.rows % 64 == 0
            and self.rank % self.rows_half == 0
            and self.pieces() * LANES <= self.span
            and 2 * self.rank == LANES
            and self.seq * self.rows_half == LANES
        )

    def pieces(self):
        return ((self.group_size + 1) * self.rows + self.slots_here * self.rank) // self.rows_half

    def start_in_half(self, i):
        return jnp.minimum((i * self.features) // LANES, self.half // LANES - self.tiles) * LANES

    def start(self, chip):
        return (chip // self.side) * self.half + self.start_in_half(chip % self.side)


def request_column(sz, table, position):
    found = jnp.zeros_like(position)
    for r in range(sz.requests):
        found = found + (position >= table[0, r]).astype(jnp.int32)
    return found


def token_at(sz, place):
    count = sz.seq * sz.rows_half
    owner = (place >= count).astype(jnp.int32)
    place = place - owner * count
    return place // sz.rows_half * sz.rows + owner * sz.rows_half + place % sz.rows_half


def table_kernel(sz, lengths, adapters, ranks, slots, piece, out, held, sem):
    here, core, group = (lax.axis_index(a) for a in ("seq", "owner", "groups"))
    copy = pltpu.make_async_copy(piece, held, sem)
    copy.start()
    end = jnp.int32(0)
    for r in range(sz.requests):
        end = end + lengths[r]
        adapter = adapters[r]
        slot = slots[adapter]
        chip, local = slot >> sz.slot_bits, slot & (sz.slots_here - 1)
        other = (chip >> sz.side_bits) ^ core
        m = (here ^ chip) & (sz.side - 1)
        out[0, r] = end
        out[1, r] = ranks[adapter]
        out[2, r] = (((other << sz.slot_bits) | (local ^ group)) << sz.side_bits) | m
        out[3, r] = ((here ^ chip) * sz.slots_here + local) * sz.rank
    copy.wait()


def panels_kernel(sz, down, *outs_and_sem):
    outs, sem = outs_and_sem[:-1], outs_and_sem[-1]
    here, group = lax.axis_index("seq"), lax.axis_index("groups")
    copies = []
    for m, out in enumerate(outs):
        first = pl.multiple_of(sz.start_in_half((here % sz.side) ^ m), LANES)
        copies.append(
            pltpu.make_async_copy(down.at[group, :, pl.ds(first, sz.span)], out, sem.at[m])
        )
    for copy in copies:
        copy.start()
    for copy in copies:
        copy.wait()


def norm_kernel(sz, x, gain, queries, keys, up, *outs_and_scratch):
    outs, scratch = outs_and_scratch[: sz.seq], outs_and_scratch[sz.seq :]
    taken, gains, query, key, raised, whole, sem = scratch
    here, core = lax.axis_index("seq"), lax.axis_index("owner")
    place = pl.ds(pl.multiple_of(core * sz.rows_half, sz.rows_half), sz.rows_half)
    pairs = ((x.at[place], taken), (gain, gains), (queries, query), (keys, key), (up, raised))
    copies = [pltpu.make_async_copy(a, b, sem.at[i]) for i, (a, b) in enumerate(pairs)]
    for copy in copies:
        copy.start()
    for copy in copies[:2]:
        copy.wait()
    rows = taken[...].astype(f32)
    rows = rows * lax.rsqrt(jnp.mean(rows * rows, axis=1, keepdims=True) + norm_eps)
    whole[...] = (rows * gains[...]).astype(bf16)
    lane = lax.broadcasted_iota(jnp.int32, (sz.rows_half, sz.span), 1)
    for copy in copies[2:]:
        copy.wait()
    for k, out in enumerate(outs):
        head = here ^ k
        first = pl.multiple_of(sz.start(head), LANES)
        skip = head * sz.features - first
        piece = whole[:, pl.ds(first, sz.span)]
        live = (lane >= skip) & (lane < skip + sz.features)
        out[: sz.rows_half] = jnp.where(live, piece.astype(f32), 0.0).astype(bf16)
        parts = []
        for c in range(sz.group_size):
            first = pl.multiple_of((head * sz.group_size + c) * HEAD_SIZE, HEAD_SIZE)
            parts.append(query[:, pl.ds(first, HEAD_SIZE)])
        first = pl.multiple_of(head * HEAD_SIZE, HEAD_SIZE)
        parts.append(key[:, pl.ds(first, HEAD_SIZE)])
        for j in range(sz.slots_here):
            parts.append(raised[j, :, pl.ds(first, HEAD_SIZE)])
        at = 0
        for part in parts:
            for top in range(0, part.shape[0], sz.rows_half):
                out[sz.rows_half :, at : at + HEAD_SIZE] = part[top : top + sz.rows_half]
                at += HEAD_SIZE
        if at < sz.span:
            out[sz.rows_half :, at:] = jnp.zeros((sz.rows_half, sz.span - at), bf16)


def unpack(sz, piece, out, part, first, size):
    for top in range(0, size, sz.rows_half):
        lanes = slice((part + top // sz.rows_half) * HEAD_SIZE, (part + top // sz.rows_half + 1) * HEAD_SIZE)
        place = pl.ds(pl.multiple_of(first + top, sz.rows_half), sz.rows_half)
        out[place, :] = piece[sz.rows_half :, lanes]


def softmax_kernel(sz, table, *refs):
    pieces, (out, raise_picked, scale, query, key, raise_all) = refs[: sz.seq], refs[sz.seq :]
    here = lax.axis_index("seq")
    parts = sz.rows // sz.rows_half
    for k, piece in zip(sz.order, pieces):
        first = (here ^ k) * sz.rows
        for c in range(sz.group_size):
            unpack(sz, piece, query.at[c], c * parts, first, sz.rows)
        for owner in range(parts):
            place = sz.seq * owner * sz.rows_half + (here ^ k) * sz.rows_half
            unpack(sz, piece, key, sz.group_size * parts + owner, place, sz.rows_half)
        size = sz.slots_here * sz.rank
        unpack(sz, piece, raise_all, (sz.group_size + 1) * parts, k * size, size)
    shape = scale.shape
    request = request_column(sz, table, token_at(sz, lax.broadcasted_iota(jnp.int32, shape, 0)))
    rank_here = jnp.ones(shape, jnp.int32)
    for r in range(sz.requests):
        rank_here = jnp.where(request == r, table[1, r], rank_here)
        first = pl.multiple_of(table[3, r], sz.rank)
        raise_picked[r * sz.rank : (r + 1) * sz.rank] = raise_all[pl.ds(first, sz.rank), :]
    scale[...] = adapter_strength / rank_here.astype(f32)
    shape = (sz.tokens, sz.tokens)
    mine = lax.broadcasted_iota(jnp.int32, shape, 0)
    theirs = token_at(sz, lax.broadcasted_iota(jnp.int32, shape, 1))
    live = (theirs <= mine) & (theirs > mine - WINDOW)
    live = live & (request_column(sz, table, mine) == request_column(sz, table, theirs))
    for c in range(sz.group_size):
        scores = lax.dot_general(
            query[c], key[...], (((1,), (1,)), ((), ())), preferred_element_type=f32
        )
        scores = jnp.where(live, scores * query_scale, -1e30)
        weights = jnp.exp(scores - jnp.max(scores, axis=1, keepdims=True))
        out[c * sz.tokens : (c + 1) * sz.tokens] = (
            weights / jnp.sum(weights, axis=1, keepdims=True)
        ).astype(bf16)


def matrix_kernel(sz, base, base_other, out, sem):
    here, core = lax.axis_index("seq"), lax.axis_index("owner")
    depth, wide = base.shape[0], out.shape[1]
    skip = here * sz.features - sz.start(here)
    spare = sz.span - sz.features
    out[0:spare] = jnp.zeros((spare, wide), bf16)
    out[sz.span - spare :] = jnp.zeros((spare, wide), bf16)
    copies = []
    for j, (ref, owner) in enumerate(((base, core), (base_other, 1 - core))):
        place = pl.ds(pl.multiple_of(skip + owner * depth, 16), depth)
        copies.append(pltpu.make_async_copy(ref, out.at[place], sem.at[j]))
        copies[-1].start()
    for copy in copies:
        copy.wait()


def project_kernel(sz, table, matrix, *refs):
    pieces, refs = refs[: sz.seq], refs[sz.seq :]
    panels, refs = refs[: 2 * sz.groups * sz.side], refs[2 * sz.groups * sz.side :]
    outs, (own, picked, stacked, values) = refs[: sz.seq], refs[sz.seq :]
    here, core = lax.axis_index("seq"), lax.axis_index("owner")
    for k, piece in zip(sz.order, pieces):
        first = pl.multiple_of((here ^ k) * sz.rows_half, sz.rows_half)
        own[pl.ds(first, sz.rows_half), :] = piece[: sz.rows_half]
    for p, panel in enumerate(panels):
        stacked[p * sz.rank : (p + 1) * sz.rank] = panel[...]
    for r in range(sz.requests):
        first = pl.multiple_of(table[2, r] * sz.rank, sz.rank)
        picked[r * sz.rank : (r + 1) * sz.rank] = stacked[pl.ds(first, sz.rank), :]
    values[...] = jnp.dot(own[...], matrix[...], preferred_element_type=f32).astype(bf16)
    low = lax.dot_general(
        picked[...], own[...], (((1,), (1,)), ((), ())), preferred_element_type=f32
    )
    count = sz.seq * sz.rows_half
    shape = (sz.rank, count)
    place = lax.broadcasted_iota(jnp.int32, shape, 1) + core * count
    request = request_column(sz, table, token_at(sz, place))
    rank = lax.broadcasted_iota(jnp.int32, shape, 0)
    reduced = jnp.zeros(shape, f32)
    for r in range(sz.requests):
        live = (request == r) & (rank < table[1, r])
        reduced = jnp.where(live, low[r * sz.rank : (r + 1) * sz.rank], reduced)
    reduced = reduced.astype(bf16)
    for k, out in enumerate(outs):
        for half in range(2):
            first = pl.multiple_of((half * sz.heads_here + (here ^ k)) * HEAD_SIZE, HEAD_SIZE)
            out[half * count : (half + 1) * count] = values[:, pl.ds(first, HEAD_SIZE)]
        out[2 * count :] = reduced


def add_kernel(sz, *refs):
    pieces, (kept, sent) = refs[: sz.seq], refs[sz.seq :]
    core = lax.axis_index("owner")
    count = sz.seq * sz.rows_half
    for out, head in ((kept, core), (sent, 1 - core)):
        place = pl.ds(pl.multiple_of(head * count, count), count)
        out[:count] = sum(piece[place, :].astype(f32) for piece in pieces)
    low = sum(piece[2 * count :].astype(f32) for piece in pieces)
    kept[count:] = low
    sent[count:] = low


def mix_kernel(sz, table, softmax, raise_picked, scale, kept, received, *refs):
    outs, (wide, base, mixed) = refs[: sz.seq], refs[sz.seq :]
    here, core = lax.axis_index("seq"), lax.axis_index("owner")
    count = sz.seq * sz.rows_half
    shape = (sz.rank, count)
    for ref, owner in ((kept, core), (received, 1 - core)):
        first = pl.multiple_of(owner * count, count)
        base[pl.ds(first, count), :] = ref[:count]
        place = lax.broadcasted_iota(jnp.int32, shape, 1) + first
        request = request_column(sz, table, token_at(sz, place))
        for r in range(sz.requests):
            wide[r * sz.rank : (r + 1) * sz.rank, pl.ds(first, count)] = jnp.where(
                request == r, ref[count:], 0.0
            ).astype(bf16)
    raised = lax.dot_general(
        wide[...], raise_picked[...], (((0,), (0,)), ((), ())), preferred_element_type=f32
    )
    values = (base[...] + scale[...] * raised).astype(bf16)
    mixed[...] = jnp.dot(softmax[...], values, preferred_element_type=f32).astype(bf16)
    for k, out in enumerate(outs):
        for c in range(sz.group_size):
            first = pl.multiple_of(c * sz.tokens + (here ^ k) * sz.rows, sz.rows)
            out[:, c * HEAD_SIZE : (c + 1) * HEAD_SIZE] = mixed[pl.ds(first, sz.rows), :]


def place_kernel(sz, *refs):
    pieces, out = refs[: sz.seq], refs[sz.seq]
    here = lax.axis_index("seq")
    wide = sz.group_size * HEAD_SIZE
    for k, piece in zip(sz.order, pieces):
        head = here ^ k
        out[:, pl.ds(pl.multiple_of(head * wide, wide), wide)] = piece[...]


def by_heads(sz, x, queries, keys, gain, base, down, up, lengths, adapters, ranks, slots):
    around = range(1, sz.seq)

    def ordered(values):
        return [values[k] for k in sz.order]

    spread = (2 * sz.rows_half, sz.span)

    def call(kernel, name, ins, outs, args, scratch=(), params=PARAMS):
        return pl.pallas_call(
            functools.partial(kernel, sz),
            out_shape=[jax.ShapeDtypeStruct(shape, dtype) for shape, dtype, _ in outs],
            in_specs=ins,
            out_specs=[spec for _, _, spec in outs],
            scratch_shapes=list(scratch),
            compiler_params=params,
            name=name,
        )(*args)

    panels_out = call(
        panels_kernel,
        "panels_out",
        [HBM],
        [((sz.rank, sz.span), bf16, VMEM)] * sz.side,
        (jnp.swapaxes(down, 1, 2),),
        (pltpu.SemaphoreType.DMA((sz.side,)),),
    )
    panels = []
    for m in range(sz.side):
        pairs = [
            (h * 2 + c, (c * sz.side + ((h % sz.side) ^ m)) * 2 + h // sz.side)
            for h in range(sz.seq)
            for c in range(2)
        ]
        panels.append(lax.ppermute(panels_out[m], ("seq", "owner"), pairs))
    x, _ = lax.optimization_barrier((x, panels_out[0]))
    rows_out = call(
        norm_kernel,
        "norm_rows",
        [HBM] * 5,
        [(spread, bf16, VMEM)] * sz.seq,
        (x, gain, queries, keys, up),
        (
            pltpu.VMEM((sz.rows_half, sz.width), bf16),
            pltpu.VMEM((1, sz.width), f32),
            pltpu.VMEM(queries.shape, bf16),
            pltpu.VMEM(keys.shape, bf16),
            pltpu.VMEM(up.shape, bf16),
            pltpu.VMEM((sz.rows_half, sz.width), bf16),
            pltpu.SemaphoreType.DMA((5,)),
        ),
        FIRST,
    )
    table, held = call(
        table_kernel,
        "table",
        [SMEM] * 4 + [ANY],
        [((4, sz.requests), jnp.int32, SMEM), (spread, bf16, VMEM)],
        (lengths, adapters, ranks, slots, rows_out[0]),
        (pltpu.SemaphoreType.DMA,),
    )
    (matrix,) = call(
        matrix_kernel,
        "matrix_rows",
        [HBM, ANY],
        [((sz.span, base.shape[1]), bf16, VMEM)],
        (base, swap(base, "owner", 1)),
        (pltpu.SemaphoreType.DMA((2,)),),
    )
    rows_in = [held] + [swap(rows_out[k], "seq", k) for k in around]

    panels[0], table, matrix = lax.optimization_barrier((panels[0], table, matrix))
    panels[1], held = lax.optimization_barrier((panels[1], held))
    rows_in[0] = held
    panels = panels + [swap(p, "groups", k) for k in range(1, sz.groups) for p in panels]
    panels = panels + [swap(p, "owner", 1) for p in panels]
    rows_ordered, panels = lax.optimization_barrier(([rows_in[k] for k in sz.order_rows], panels))
    rows_in = [rows_ordered[sz.order_rows.index(k)] for k in range(sz.seq)]
    softmax, raise_picked, scale = call(
        softmax_kernel,
        "softmax_rows",
        [SMEM] + [VMEM] * sz.seq,
        [
            ((sz.group_size * sz.tokens, sz.tokens), bf16, VMEM),
            ((sz.requests * sz.rank, HEAD_SIZE), bf16, VMEM),
            ((sz.tokens, HEAD_SIZE), f32, VMEM),
        ],
        (table, *ordered(rows_in)),
        (
            pltpu.VMEM((sz.group_size, sz.tokens, HEAD_SIZE), bf16),
            pltpu.VMEM((sz.tokens, HEAD_SIZE), bf16),
            pltpu.VMEM((sz.seq * sz.slots_here * sz.rank, HEAD_SIZE), bf16),
        ),
    )

    count = sz.seq * sz.rows_half
    partial_out = call(
        project_kernel,
        "project",
        [SMEM] + [VMEM] * (1 + sz.seq + len(panels)),
        [((2 * count + sz.rank, HEAD_SIZE), bf16, VMEM)] * sz.seq,
        (table, matrix, *ordered(rows_in), *panels),
        (
            pltpu.VMEM((count, sz.span), bf16),
            pltpu.VMEM((sz.requests * sz.rank, sz.span), bf16),
            pltpu.VMEM((len(panels) * sz.rank, sz.span), bf16),
            pltpu.VMEM((count, base.shape[1]), bf16),
        ),
    )
    partial_in = [partial_out[0]] + [swap(partial_out[k], "seq", k) for k in around]
    kept, sent = call(
        add_kernel,
        "add_partials",
        [VMEM] * sz.seq,
        [((count + sz.rank, HEAD_SIZE), f32, VMEM)] * 2,
        [partial_in[k] for k in sz.order_sum],
    )
    wide = sz.group_size * HEAD_SIZE
    mixed = call(
        mix_kernel,
        "mix_values",
        [SMEM] + [VMEM] * 5,
        [((sz.rows, wide), bf16, VMEM)] * sz.seq,
        (table, softmax, raise_picked, scale, kept, swap(sent, "owner", 1)),
        (
            pltpu.VMEM((sz.requests * sz.rank, sz.tokens), bf16),
            pltpu.VMEM((sz.tokens, HEAD_SIZE), f32),
            pltpu.VMEM((sz.group_size * sz.tokens, HEAD_SIZE), bf16),
        ),
    )
    mixed_in = [mixed[0]] + [swap(mixed[k], "seq", k) for k in around]
    (result,) = call(
        place_kernel,
        "place_heads",
        [VMEM] * sz.seq,
        [((sz.rows, sz.seq * wide), bf16, VMEM)],
        ordered(mixed_in),
    )
    return result


def broadcast(x, axis, root):
    mine = lax.axis_index(axis) == root
    return lax.psum(jnp.where(mine, x, jnp.zeros_like(x)), axis)


def from_behind(value, axis, steps):
    count = lax.axis_size(axis)
    first, last = (max(0, -steps), min(count, count - steps))
    return lax.ppermute(value, axis, [(source, source + steps) for source in range(first, last)])


def by_tokens(
    layer_input_rows,
    encoded_query_rows,
    encoded_key_rows,
    layer_norm_gain,
    base_value_matrix,
    adapter_down_panels,
    adapter_up_panels,
    request_token_lengths,
    adapter_per_request,
    rank_per_adapter,
    slot_per_adapter,
):
    hidden = layer_input_rows[0]
    row_count = hidden.shape[0]
    seq_now = lax.axis_index("seq")
    owner_now = lax.axis_index("owner")
    reach_count = min(WINDOW // row_count, lax.axis_size("seq") - 1)
    requests = request_token_lengths.shape[0]
    library = slot_per_adapter.shape[0]
    slots_here = adapter_down_panels.shape[1]
    rows_halved = adapter_down_panels.shape[2]
    rank_span_width = adapter_down_panels.shape[3]
    key_value_halved = adapter_up_panels.shape[3]
    group_size = HEADS // KEY_VALUE_HEADS
    request_ends = jnp.cumsum(request_token_lengths)
    position = seq_now * row_count + jnp.arange(row_count, dtype=jnp.int32)
    context = seq_now * row_count + jnp.arange(-reach_count * row_count, row_count, dtype=jnp.int32)
    request_lookup = jnp.sum((position[:, None] >= request_ends[None, :]).astype(jnp.int32), axis=1)
    request_ctx = jnp.sum((context[:, None] >= request_ends[None, :]).astype(jnp.int32), axis=1)
    live_mask = (context[None, :] <= position[:, None]) & (
        context[None, :] > position[:, None] - WINDOW
    )
    live_mask = (
        live_mask & (context[None, :] >= 0) & (request_ctx[None, :] == request_lookup[:, None])
    )
    choose = adapter_per_request[:, None] == jnp.arange(library, dtype=jnp.int32)[None, :]
    slot_of = jnp.sum(jnp.where(choose, slot_per_adapter[None, :], 0), axis=1)
    rank_lookup = jnp.sum(jnp.where(choose, rank_per_adapter[None, :], 0), axis=1)
    scale_lookup = adapter_strength / rank_lookup.astype(jnp.float32)
    in_request = request_lookup[:, None] == jnp.arange(requests, dtype=jnp.int32)[None, :]
    column_live = jnp.arange(rank_span_width, dtype=jnp.int32)[None, :] < rank_lookup[:, None]
    row_gain_weight = jnp.where(in_request, scale_lookup[None, :], jnp.float32(0.0))
    down_panel_here = adapter_down_panels[0]
    up_panel_here = adapter_up_panels[0]
    queries = encoded_query_rows[0]
    keys_own = encoded_key_rows[0]
    key_heads = keys_own.shape[1] // HEAD_SIZE
    wide_rows = hidden.astype(jnp.float32)
    normalized_rows = wide_rows * lax.rsqrt(
        jnp.mean(wide_rows * wide_rows, axis=1, keepdims=True) + norm_eps
    )
    normalized_rows = (normalized_rows * layer_norm_gain[0][None, :]).astype(jnp.bfloat16)
    normed_half = lax.dynamic_slice_in_dim(normalized_rows, owner_now * rows_halved, rows_halved, 1)
    full_value = jnp.dot(
        normalized_rows,
        lax.all_gather(base_value_matrix[0], ("seq", "owner"), axis=0, tiled=True),
        preferred_element_type=jnp.float32,
    )
    value_base_rows = lax.dynamic_slice_in_dim(
        full_value, owner_now * key_value_halved, key_value_halved, 1
    )

    def fetch_one(reduced_rows, request_index):
        owner_slot = slot_of[request_index]
        holder = owner_slot // slots_here
        local_slot = owner_slot % slots_here
        down_local = lax.dynamic_slice_in_dim(down_panel_here, local_slot, 1, 0)
        up_local = lax.dynamic_slice_in_dim(up_panel_here, local_slot, 1, 0)
        down_piece, up_piece = (
            broadcast(down_local, "seq", holder),
            broadcast(up_local, "seq", holder),
        )
        keep_mask = in_request[:, request_index][:, None] & column_live[request_index][None, :]
        matrix_product = jnp.dot(normed_half, down_piece[0], preferred_element_type=jnp.float32)
        return (reduced_rows + jnp.where(keep_mask, matrix_product, jnp.float32(0.0)), up_piece[0])

    start_low = jnp.zeros((row_count, rank_span_width), jnp.float32)
    reduced_rows, panels_up = lax.scan(fetch_one, start_low, jnp.arange(requests, dtype=jnp.int32))
    reduced_rows = lax.psum(reduced_rows, "owner").astype(jnp.bfloat16)
    raised_rows = jnp.einsum(
        "tr,qrk->qtk", reduced_rows, panels_up, preferred_element_type=jnp.float32
    )
    adapter_value = jnp.sum(row_gain_weight.T[:, :, None] * raised_rows, axis=0)
    value_output_rows = (value_base_rows + adapter_value).astype(jnp.bfloat16)
    key_parts = []
    value_parts = []
    for shift_by in range(reach_count, 0, -1):
        key_piece, value_piece = from_behind((keys_own, value_output_rows), "seq", shift_by)
        key_parts.append(key_piece)
        value_parts.append(value_piece)
    keys_all = jnp.concatenate(key_parts + [keys_own], axis=0)
    values_all = jnp.concatenate(value_parts + [value_output_rows], axis=0)
    query_view = queries.reshape(row_count, key_heads, group_size, HEAD_SIZE)
    key_view = keys_all.reshape(-1, key_heads, HEAD_SIZE)
    value_view = values_all.reshape(-1, key_heads, HEAD_SIZE)
    head_outputs = []
    for head_index in range(key_heads):
        query_head = query_view[:, head_index]
        scores = (
            jnp.einsum(
                "tcd,jd->ctj",
                query_head,
                key_view[:, head_index],
                preferred_element_type=jnp.float32,
            )
            * query_scale
        )
        scores = jnp.where(live_mask[None], scores, jnp.float32(-1e30))
        row_max = jnp.max(scores, axis=-1, keepdims=True)
        weights = jnp.exp(scores - row_max)
        row_total = jnp.sum(weights, axis=-1, keepdims=True)
        softmax_rows = (weights / row_total).astype(jnp.bfloat16)
        mixed = jnp.einsum(
            "ctj,jd->tcd",
            softmax_rows,
            value_view[:, head_index],
            preferred_element_type=jnp.float32,
        )
        head_outputs.append(mixed.astype(jnp.bfloat16).reshape(row_count, group_size * HEAD_SIZE))
    result = jnp.concatenate(head_outputs, axis=1)
    return result[None]


def per_device(
    layer_input_rows,
    encoded_query_rows,
    encoded_key_rows,
    layer_norm_gain,
    base_value_matrix,
    adapter_down_panels,
    adapter_up_panels,
    request_token_lengths,
    adapter_per_request,
    rank_per_adapter,
    slot_per_adapter,
):
    sz = Sizes(
        layer_input_rows[0],
        encoded_query_rows[0],
        adapter_down_panels[0],
        adapter_up_panels[0],
        request_token_lengths.shape[0],
    )
    scalars = (request_token_lengths, adapter_per_request, rank_per_adapter, slot_per_adapter)
    if not sz.fits():
        return by_tokens(
            layer_input_rows,
            encoded_query_rows,
            encoded_key_rows,
            layer_norm_gain,
            base_value_matrix,
            adapter_down_panels,
            adapter_up_panels,
            *scalars,
        )
    return by_heads(
        sz,
        layer_input_rows[0],
        encoded_query_rows[0],
        encoded_key_rows[0],
        layer_norm_gain,
        base_value_matrix[0],
        adapter_down_panels[0],
        adapter_up_panels[0],
        *scalars,
    )[None]


def solution(mesh):
    in_specs = (
        P("segment", ("groups", "seq"), None),
        P("segment", ("groups", "seq"), "owner"),
        P("segment", ("groups", "seq"), "owner"),
        P("segment", None),
        P("segment", ("seq", "owner"), None),
        P("segment", "seq", "owner", None),
        P("segment", "seq", None, "owner"),
        P("groups"),
        P("groups"),
        P(),
        P(),
    )
    out_specs = P("segment", ("groups", "seq"), "owner")
    return jax.shard_map(
        per_device, mesh=mesh, in_specs=in_specs, out_specs=out_specs, check_vma=False
    )
```
